128 devices in a mesh: dp: 16 (over z_hi, x, core), tensor: 8 (over y, z_lo).
Axes of the slice: x: 4, y: 4, z: 4 (z_hi: 2, z_lo: 2; z = z_hi * 2 + z_lo), core: 2. Of those that a mesh axis runs over, the one named last changes fastest.
Arguments:
- tokens: bfloat16 [16384, 2048], P(('dp', 'tensor')), may hold values from -6 to 6
- doc_ids: int32 [16384], P(('dp', 'tensor')), may hold values from -1 to 3, as said below
- qkv_weight: bfloat16 [3, 2048, 2048], P(None, 'dp', 'tensor'), may hold values from -0.125 to 0.125
- qkv_bias: float32 [3, 2048], P(None, 'tensor'), may hold values from -3 to 3
- out_weight: bfloat16 [2048, 2048], P('tensor', 'dp'), may hold values from -0.375 to 0.375
- norm1_gain: float32 [2048], replicated, may hold values from 0.5 to 1.5
- norm1_shift: float32 [2048], replicated, may hold values from -2 to 2
- norm2_gain: float32 [2048], replicated, may hold values from 0.5 to 1.5
- norm2_shift: float32 [2048], replicated, may hold values from -2 to 2
- gate_up_weight: bfloat16 [2, 2048, 5632], P(None, 'dp', 'tensor'), may hold values from -0.125 to 0.125
- down_weight: bfloat16 [5632, 2048], P('tensor', 'dp'), may hold values from -0.109375 to 0.109375
- cotangent: bfloat16 [16384, 2048], P(('dp', 'tensor')), may hold values from -6 to 6
Outputs:
- layer_out: bfloat16 [16384, 2048], P(('dp', 'tensor'))
- token_grad: bfloat16 [16384, 2048], P(('dp', 'tensor'))
- qkv_weight_grad: float32 [3, 2048, 2048], P(None, 'dp', 'tensor')
- qkv_bias_grad: float32 [3, 2048], P(None, 'tensor')
- out_weight_grad: float32 [2048, 2048], P('tensor', 'dp')
- norm1_gain_grad: float32 [2048], replicated
- norm1_shift_grad: float32 [2048], replicated
- norm2_gain_grad: float32 [2048], replicated
- norm2_shift_grad: float32 [2048], replicated
- gate_up_weight_grad: float32 [2, 2048, 5632], P(None, 'dp', 'tensor')
- down_weight_grad: float32 [5632, 2048], P('tensor', 'dp')
The draws below stay inside these ranges and needn't reach their ends.
Inputs may be any that keep to these rules, and one draw needn't show every extreme that they name: `doc_ids`: within each aligned block of 1024 tokens, documents 0 to 3 are consecutive runs in increasing order and the padding (-1) is one run at the block's end, at least one token long.
All inputs are finite; a program needn't handle non-finite values.
Results may differ from the reference program's by a relative error of at most 0.025.
Values may be sent and summed in bfloat16 or wider, within the bound.
A program may use at most 192 MiB of HBM per device.

```python
import jax
import jax.numpy as jnp
from jax import lax

D = 2048
HEADS = 32
HEAD_DIM = 64
ROT = 16
FF = 5632
TOK_DEV = 128
DOCS = 4
GROUP = 1024
TOKENS = 16384


def draw_doc_ids(key, part):
    key = jax.random.fold_in(key, 7)
    key_lens, key_pad, key_pick = jax.random.split(key, 3)
    groups = TOKENS // GROUP
    most = TOK_DEV // 8
    lens = jax.random.randint(key_lens, (groups, DOCS), 1, most + 1)
    padding = jax.random.randint(key_pad, (groups,), 1, most + 1)
    longest = jax.random.randint(key_pick, (groups,), 0, DOCS)
    pick = jnp.arange(DOCS)[None, :] == longest[:, None]
    others = jnp.sum(jnp.where(pick, 0, lens), axis=1)
    lens = jnp.where(pick, (GROUP - padding - others)[:, None], lens)
    ends = jnp.cumsum(lens, axis=1)
    index = jnp.arange(GROUP)
    numbers = jnp.sum((index[None, :, None] >= ends[:, None, :]).astype(jnp.int32), axis=-1)
    numbers = jnp.where(numbers >= DOCS, -1, numbers)
    return numbers.reshape(-1).astype(jnp.int32)


def steps_of(rng, dims, shards, smallest, high):
    def one(dim, parts):
        heights = jax.random.uniform(jax.random.fold_in(jax.random.fold_in(rng, 6), dim), (parts,), jnp.float32, smallest / len(shards), high / len(shards))
        return jnp.repeat(jnp.exp(heights), dims[dim] // parts).reshape((-1,) + (1,) * (len(dims) - dim - 1))

    factor_of = one(*shards[0])
    for cut in shards[1:]:
        factor_of = factor_of * one(*cut)
    return factor_of


def normal_values(stream_key, extent, width, limit, cuts=(), kind=jnp.bfloat16):
    level = steps_of(stream_key, extent, cuts, -0.22, 0.18) if cuts else 1.0
    values = jax.random.normal(stream_key, extent, jnp.float32) * width * level
    return jnp.minimum(jnp.maximum(values, -limit), limit).astype(kind)


def setup_inputs(seed: int = 0) -> dict:
    arg_keys = jax.random.split(jax.random.key(seed), 13)
    return {
        "tokens": normal_values(arg_keys[0], (TOKENS, D), 1.0, 6.0, ((0, 128),)),
        "doc_ids": draw_doc_ids(jax.random.fold_in(arg_keys[12], 71), 0),
        "qkv_weight": normal_values(arg_keys[2], (3, D, D), D ** -0.5, 0.125, ((1, 16), (2, 8))),
        "qkv_bias": normal_values(arg_keys[3], (3, D), 0.5, 3.0, ((1, 8),), jnp.float32),
        "out_weight": normal_values(arg_keys[4], (D, D), (D // 8) ** -0.5, 0.375, ((0, 8), (1, 16))),
        "norm1_gain": jnp.clip(1.0 + 0.1 * jax.random.normal(arg_keys[5], (D,), jnp.float32), 0.5, 1.5),
        "norm1_shift": normal_values(arg_keys[6], (D,), 0.3, 2.0, (), jnp.float32),
        "norm2_gain": jnp.clip(1.0 + 0.1 * jax.random.normal(arg_keys[7], (D,), jnp.float32), 0.5, 1.5),
        "norm2_shift": normal_values(arg_keys[8], (D,), 0.3, 2.0, (), jnp.float32),
        "gate_up_weight": normal_values(arg_keys[9], (2, D, FF), D ** -0.5, 0.125, ((1, 16), (2, 8))),
        "down_weight": normal_values(arg_keys[10], (FF, D), (FF // 2) ** -0.5, 0.109375, ((0, 8), (1, 16))),
        "cotangent": normal_values(arg_keys[11], (TOKENS, D), 1.0, 6.0, ((0, 128),)),
    }


EPS = 1e-05

@jax.custom_vjp
def low(v):
    return lax.optimization_barrier(v.astype(jnp.bfloat16)).astype(jnp.float32)

@jax.custom_vjp
def low_back(v):
    return v

def low_keep(v):
    return (low(v), None)

def low_pass(kept, grad):
    return (grad,)

def back_keep(v):
    return (v, None)

def back_low(kept, grad):
    return (low(grad),)
low.defvjp(low_keep, low_pass)
low_back.defvjp(back_keep, back_low)

def layer_norm(values, gain, shift):
    centred = values - lax.optimization_barrier(jnp.mean(values, axis=-1, keepdims=True))
    variance = lax.optimization_barrier(jnp.mean(centred * centred, axis=-1, keepdims=True))
    return centred * lax.rsqrt(variance + EPS) * gain + shift

def angles(group_ids):
    group = group_ids.shape[0]
    index = jnp.arange(group, dtype=jnp.int32)
    numbers = jnp.arange(DOCS, dtype=jnp.int32)
    before = (group_ids[None, :] >= 0) & (group_ids[None, :] < numbers[:, None])
    starts = lax.optimization_barrier(jnp.sum(before.astype(jnp.int32), axis=1))
    offset = lax.optimization_barrier(jnp.sum(jnp.where(group_ids[:, None] == numbers[None, :], starts[None, :], 0), axis=1))
    position = (index - offset).astype(jnp.float32)
    freq = jnp.power(10000.0, -2.0 * jnp.arange(ROT // 2, dtype=jnp.float32) / ROT)
    angle = position[:, None] * freq[None, :]
    return (jnp.cos(angle), jnp.sin(angle))

def rotate(values, cosine, sine):
    half = ROT // 2
    first_part = values[..., :half]
    second_part = values[..., half:ROT]
    cosine = cosine[:, None, :]
    sine = sine[:, None, :]
    return jnp.concatenate([first_part * cosine - second_part * sine, second_part * cosine + first_part * sine, values[..., ROT:]], axis=-1)

def allowed_keys(row_ids, row_first, col_ids):
    rows = row_first + jnp.arange(row_ids.shape[0], dtype=jnp.int32)
    cols = jnp.arange(col_ids.shape[0], dtype=jnp.int32)
    same = (row_ids[:, None] == col_ids[None, :]) & (col_ids[None, :] >= 0) & (cols[None, :] < rows[:, None])
    return same | (cols[None, :] == rows[:, None])

def layer(values, group_ids, qkv_weight, qkv_bias, out_weight, norm1_gain, norm1_shift, norm2_gain, norm2_shift, gate_up_weight, down_weight):
    high = lax.Precision.HIGHEST
    group = values.shape[0]
    cosine, sine = angles(group_ids)
    normed1 = low(layer_norm(values, norm1_gain, norm1_shift))
    projected = low_back(jnp.einsum('td,cde->cte', normed1, qkv_weight, precision=high) + qkv_bias[:, None, :])
    query = low(rotate(projected[0].reshape(group, HEADS, HEAD_DIM), cosine, sine))
    keys_all = low(rotate(projected[1].reshape(group, HEADS, HEAD_DIM), cosine, sine))
    values_all = low(projected[2].reshape(group, HEADS, HEAD_DIM))
    scores = low_back(jnp.einsum('qhd,khd->hqk', query, keys_all, precision=high) * HEAD_DIM ** (-0.5))
    allow = allowed_keys(group_ids, 0, group_ids)
    probs = jax.nn.softmax(jnp.where(allow[None], scores, -1e+30), axis=-1)
    attended = jnp.einsum('hqk,khd->qhd', low(probs), values_all, precision=high).reshape(group, D)
    attended = low(low_back(attended))
    mixed = values + low_back(jnp.dot(attended, out_weight, precision=high))
    normed2 = low(layer_norm(mixed, norm2_gain, norm2_shift))
    gate_up = low_back(jnp.einsum('td,cdf->ctf', normed2, gate_up_weight, precision=high))
    hidden = low(jax.nn.silu(gate_up[0]) * gate_up[1])
    return mixed + low_back(jnp.dot(hidden, down_weight, precision=high))

def reference(tokens, doc_ids, qkv_weight, qkv_bias, out_weight, norm1_gain, norm1_shift, norm2_gain, norm2_shift, gate_up_weight, down_weight, cotangent):
    count = TOKENS // GROUP
    params = tuple((item.astype(jnp.float32) for item in (qkv_weight, qkv_bias, out_weight, norm1_gain, norm1_shift, norm2_gain, norm2_shift, gate_up_weight, down_weight)))
    inputs = tokens.astype(jnp.float32).reshape(count, GROUP, D)
    grads_out = cotangent.astype(jnp.float32).reshape(count, GROUP, D)
    id_groups = doc_ids.reshape(count, GROUP)

    def one_group(totals, slices):
        values, group_ids, grad_out = slices

        def forward(values, *weights):
            return layer(values, group_ids, *weights)
        result, pullback = jax.vjp(forward, values, *params)
        grads = pullback(grad_out)
        totals = tuple((total + grad for total, grad in zip(totals, grads[1:])))
        return (totals, (result, grads[0]))
    start = tuple((jnp.zeros_like(item) for item in params))
    totals, (results, input_grads) = lax.scan(one_group, start, (inputs, id_groups, grads_out))
    return (results.reshape(TOKENS, D).astype(jnp.bfloat16), input_grads.reshape(TOKENS, D).astype(jnp.bfloat16), totals[0], totals[1], totals[2], totals[3], totals[4], totals[5], totals[6], totals[7], totals[8])
```

```python
import functools

import jax
import jax.numpy as jnp
from jax import lax
from jax.experimental import pallas as pl
from jax.experimental.pallas import tpu as pltpu
from jax.sharding import PartitionSpec as P

HEAD_DIM = 64
ROT = 16
DOCS = 4
EPS = 1e-05

ROWS = 128
WIDTH = 2048
TENSOR = 8
HALF = ROWS // 2
QUARTER = ROWS // 4
MESH = pl.DeviceIdType.MESH
BF16 = jnp.bfloat16
F32 = jnp.float32
VMEM_LIMIT = 56 * 2**20


def coordinates():
    tensor = lax.axis_index("tensor")
    return lax.axis_index("dp"), tensor // 2, lax.rem(tensor, 2)


class Around:
    def __init__(self):
        dp, y, z = coordinates()
        up, down, far = lax.rem(y + 1, 4), lax.rem(y + 3, 4), lax.rem(y + 2, 4)
        other = 1 - z
        self.me, self.across = y * 2 + z, y * 2 + other
        self.up, self.down, self.far = up * 2 + z, down * 2 + z, far * 2 + z
        self.up_o, self.down_o, self.far_o = up * 2 + other, down * 2 + other, far * 2 + other
        self.y, self.z = y, z
        self.y_up, self.y_down, self.y_far = up, down, far
        self.to_up, self.to_down, self.to_across = (dp, self.up), (dp, self.down), (dp, self.across)

    def peers(self):
        return [self.to_up, self.to_down, self.to_across]


class Ring:
    def __init__(self):
        dp = lax.axis_index("dp")
        tensor = lax.axis_index("tensor")
        zh, x, core = dp // 8, lax.rem(dp // 2, 4), lax.rem(dp, 2)
        self.zh, self.x, self.core, self.dp, self.tensor = zh, x, core, dp, tensor
        self.xs = [lax.rem(x + step, 4) for step in range(4)]
        self.to_x = [(self.index(zh, self.xs[step], core), tensor) for step in range(4)]
        self.to_zh = (self.index(1 - zh, x, core), tensor)
        self.to_core = (self.index(zh, x, 1 - core), tensor)

    def index(self, zh, x, core):
        return zh * 8 + x * 2 + core

    def peers(self):
        return self.to_x[1:] + [self.to_zh, self.to_core]


def greet(peers):
    barrier = pltpu.get_barrier_semaphore()
    for peer in peers:
        pl.semaphore_signal(barrier, inc=1, device_id=peer, device_id_type=MESH)
    pl.semaphore_wait(barrier, len(peers))


class Mail:
    def __init__(self, sends, receives):
        self.sends, self.receives = sends, receives
        self.out = []

    def send(self, number, source, target, device):
        copy = pltpu.make_async_remote_copy(
            src_ref=source,
            dst_ref=target,
            send_sem=self.sends.at[number],
            recv_sem=self.receives.at[number],
            device_id=device,
            device_id_type=MESH,
        )
        copy.start()
        self.out.append(copy)

    def landed(self, number, target, device):
        pltpu.make_async_remote_copy(
            src_ref=target,
            dst_ref=target,
            send_sem=self.sends.at[number],
            recv_sem=self.receives.at[number],
            device_id=device,
            device_id_type=MESH,
        ).wait_recv()

    def finish(self):
        for copy in self.out:
            copy.wait_send()


def gather_steps(around, mail, own, rows):
    a = around

    def part(slot, first, count):
        return rows.at[slot, pl.ds(first, count)]

    def begin():
        for number, first, device in (
            (0, 0, a.to_up),
            (1, HALF, a.to_down),
            (2, HALF, a.to_across),
            (3, HALF, a.to_up),
            (4, 0, a.to_down),
            (5, 0, a.to_across),
        ):
            mail.send(number, own.at[pl.ds(first, HALF)], part(a.me, first, HALF), device)

    def pass_on(number, slot, first, count, device):
        mail.send(number, part(slot, first, count), part(slot, first, count), device)

    def got(number, slot, first, count):
        mail.landed(number, part(slot, first, count), a.to_up)

    def one():
        got(0, a.down, 0, HALF)
        pass_on(6, a.down, 0, HALF, a.to_up)
        pass_on(7, a.down, 0, HALF, a.to_across)
        got(1, a.up, HALF, HALF)
        pass_on(8, a.up, HALF, HALF, a.to_down)
        got(2, a.across, HALF, HALF)
        pass_on(9, a.across, HALF, HALF, a.to_up)
        pass_on(10, a.across, HALF, HALF, a.to_down)

    def two():
        got(4, a.up, 0, HALF)
        pass_on(11, a.up, 0, HALF, a.to_across)
        got(3, a.down, HALF, HALF)
        got(5, a.across, 0, HALF)

    def three():
        got(6, a.far, 0, HALF)
        pass_on(12, a.far, 0, HALF, a.to_across)
        got(8, a.far, HALF, HALF)

    def four():
        got(9, a.down_o, HALF, HALF)
        pass_on(13, a.down_o, HALF, QUARTER, a.to_up)
        got(10, a.up_o, HALF, HALF)
        pass_on(14, a.up_o, HALF + QUARTER, QUARTER, a.to_down)

    def five():
        got(7, a.down_o, 0, HALF)
        got(11, a.up_o, 0, HALF)

    def six():
        got(13, a.far_o, HALF, QUARTER)
        got(14, a.far_o, HALF + QUARTER, QUARTER)
        got(12, a.far_o, 0, HALF)

    return begin, one, two, three, four, five, six


GATHER_MAILS = 15


def gather_kernel(own, rows, sends, receives, local):
    around = Around()
    mail = Mail(sends, receives)
    keep = pltpu.make_async_copy(own, rows.at[around.me], local.at[0])
    keep.start()
    greet(around.peers())
    for step in gather_steps(around, mail, own, rows):
        step()
    mail.finish()
    keep.wait()


def gather_rows(own, collective):
    return pl.pallas_call(
        gather_kernel,
        out_shape=jax.ShapeDtypeStruct((TENSOR,) + own.shape, own.dtype),
        in_specs=[pl.BlockSpec(memory_space=pltpu.VMEM)],
        out_specs=pl.BlockSpec(memory_space=pl.ANY),
        scratch_shapes=[
            pltpu.SemaphoreType.DMA((GATHER_MAILS,)),
            pltpu.SemaphoreType.DMA((GATHER_MAILS,)),
            pltpu.SemaphoreType.DMA((1,)),
        ],
        compiler_params=pltpu.CompilerParams(
            collective_id=collective, has_side_effects=True, vmem_limit_bytes=VMEM_LIMIT
        ),
        name="gather_rows",
    )(own)


IDS = 4


def gather_weights_kernel(
    own, ids, shard, rows, id_rows, full, sends, receives, w_sends, w_receives, i_sends, i_receives, local
):
    around = Around()
    ring = Ring()
    mail, wmail, imail = (
        Mail(sends, receives),
        Mail(w_sends, w_receives),
        Mail(i_sends, i_receives),
    )
    a, r = around, ring
    keeps = [
        pltpu.make_async_copy(own, rows.at[a.me], local.at[0]),
        pltpu.make_async_copy(ids, id_rows.at[a.z, a.y], local.at[1]),
    ]

    def block(zh, x, core):
        first = pl.multiple_of(r.index(zh, x, core) * ROWS, ROWS)
        return full.at[:, pl.ds(first, ROWS), :]

    mine = block(r.zh, r.x, r.core)
    keeps.append(pltpu.make_async_copy(shard, mine, local.at[2]))
    for keep in keeps:
        keep.start()
    greet(a.peers() + r.peers())

    def share(number, zh, x, device):
        wmail.send(number, block(zh, x, r.core), block(zh, x, r.core), device)

    def came(number, zh, x, core):
        wmail.landed(number, block(zh, x, core), r.to_core)

    begin, one, two, three, four, five, six = gather_steps(a, mail, own, rows)
    begin()
    imail.send(0, ids, id_rows.at[a.z, a.y], a.to_up)
    imail.send(1, ids, id_rows.at[a.z, a.y], a.to_down)
    wmail.send(0, shard, mine, r.to_zh)
    for step in (1, 2, 3):
        wmail.send(step, shard, mine, r.to_x[step])
    wmail.send(7, shard, mine, r.to_core)
    imail.landed(0, id_rows.at[a.z, a.y_down], a.to_up)
    imail.send(2, id_rows.at[a.z, a.y_down], id_rows.at[a.z, a.y_down], a.to_up)
    imail.landed(1, id_rows.at[a.z, a.y_up], a.to_up)
    imail.landed(2, id_rows.at[a.z, a.y_far], a.to_up)
    keeps[1].wait()
    imail.send(3, id_rows.at[a.z], id_rows.at[a.z], a.to_across)
    one()
    came(0, 1 - r.zh, r.x, r.core)
    for step in (1, 2, 3):
        share(3 + step, 1 - r.zh, r.x, r.to_x[step])
    share(8, 1 - r.zh, r.x, r.to_core)
    two()
    for step in (1, 2, 3):
        came(step, r.zh, r.xs[4 - step], r.core)
        share(8 + step, r.zh, r.xs[4 - step], r.to_core)
    three()
    four()
    for step in (1, 2, 3):
        came(3 + step, 1 - r.zh, r.xs[4 - step], r.core)
        share(11 + step, 1 - r.zh, r.xs[4 - step], r.to_core)
    five()
    six()
    sibling = 1 - r.core
    came(7, r.zh, r.x, sibling)
    came(8, 1 - r.zh, r.x, sibling)
    for step in (1, 2, 3):
        came(8 + step, r.zh, r.xs[4 - step], sibling)
        came(11 + step, 1 - r.zh, r.xs[4 - step], sibling)
    imail.landed(3, id_rows.at[1 - a.z], a.to_up)
    mail.finish()
    wmail.finish()
    imail.finish()
    keeps[0].wait()
    keeps[2].wait()


WEIGHT_MAILS = 15


def gather_weights(own, ids, shard, collective):
    parts, rows, columns = shard.shape
    return pl.pallas_call(
        gather_weights_kernel,
        out_shape=(
            jax.ShapeDtypeStruct((TENSOR,) + own.shape, own.dtype),
            jax.ShapeDtypeStruct((2, 4) + ids.shape, ids.dtype),
            jax.ShapeDtypeStruct((parts, rows * 16, columns), shard.dtype),
        ),
        in_specs=[pl.BlockSpec(memory_space=pltpu.VMEM)] * 3,
        out_specs=(pl.BlockSpec(memory_space=pl.ANY),) * 3,
        scratch_shapes=[
            pltpu.SemaphoreType.DMA((GATHER_MAILS,)),
            pltpu.SemaphoreType.DMA((GATHER_MAILS,)),
            pltpu.SemaphoreType.DMA((WEIGHT_MAILS,)),
            pltpu.SemaphoreType.DMA((WEIGHT_MAILS,)),
            pltpu.SemaphoreType.DMA((IDS,)),
            pltpu.SemaphoreType.DMA((IDS,)),
            pltpu.SemaphoreType.DMA((3,)),
        ],
        compiler_params=pltpu.CompilerParams(
            collective_id=collective, has_side_effects=True, vmem_limit_bytes=VMEM_LIMIT
        ),
        name="gather_weights",
    )(own, ids, shard)


def added(*terms):
    total = terms[0].astype(F32)
    for term in terms[1:]:
        total = total + term.astype(F32)
    return total


SCATTER_MAILS = 17
SCATTER_ROWS = (32, 32, 64, 64, 64, 64, 32, 32, 64, 64, 64, 32, 32, 64, 64, 64, 64)
SCATTER_FIRST = tuple(sum(SCATTER_ROWS[:k]) for k in range(SCATTER_MAILS))


def scatter_steps(around, mail, parts, total, land):
    a = around

    def part(slot, first, count):
        return parts.at[slot, pl.ds(first, count)]

    def box(number):
        return land.at[pl.ds(SCATTER_FIRST[number], SCATTER_ROWS[number])]

    def direct(number, slot, first, device):
        mail.send(number, part(slot, first, SCATTER_ROWS[number]), box(number), device)

    def got(number):
        mail.landed(number, box(number), a.to_up)

    def fold(stage, slot, first, others=()):
        count = SCATTER_ROWS[stage]
        terms = [part(slot, first, count)[...], box(stage)[...]]
        terms += [box(other)[...] for other in others]
        box(stage)[...] = added(*terms).astype(BF16)

    def begin():
        direct(0, a.far_o, 96, a.to_up)
        direct(1, a.far_o, 64, a.to_down)
        direct(2, a.far_o, 0, a.to_across)
        direct(3, a.far, 64, a.to_up)
        direct(4, a.up_o, 0, a.to_across)
        direct(5, a.down_o, 0, a.to_across)
        direct(6, a.down_o, 96, a.to_down)
        direct(7, a.up_o, 64, a.to_up)
        direct(8, a.down, 64, a.to_down)
        direct(9, a.across, 0, a.to_across)

    def one():
        got(1)
        fold(1, a.down_o, 64)
        mail.send(11, box(1), box(11), a.to_down)
        got(0)
        fold(0, a.up_o, 96)
        mail.send(12, box(0), box(12), a.to_up)
        got(2)
        fold(2, a.far, 0)
        mail.send(10, box(2), box(10), a.to_down)
        got(3)
        fold(3, a.up, 64)
        mail.send(13, box(3), box(13), a.to_up)

    def two():
        got(4)
        fold(4, a.up, 0)
        mail.send(14, box(4), box(14), a.to_up)
        got(5)
        got(10)
        fold(5, a.down, 0, (10,))
        mail.send(15, box(5), box(15), a.to_down)
        got(6)
        got(7)
        got(11)
        got(12)
        upper = added(part(a.across, 64, 32)[...], box(7)[...], box(11)[...]).astype(BF16)
        lower = added(part(a.across, 96, 32)[...], box(6)[...], box(12)[...]).astype(BF16)
        land.at[pl.ds(SCATTER_FIRST[6], 32)][...] = upper
        land.at[pl.ds(SCATTER_FIRST[7], 32)][...] = lower
        both = land.at[pl.ds(SCATTER_FIRST[6], 64)]
        mail.send(16, both, box(16), a.to_across)

    def three():
        got(9)
        got(14)
        got(15)
        total[pl.ds(0, HALF), :] = added(
            part(a.me, 0, HALF)[...], box(9)[...], box(14)[...], box(15)[...]
        )
        got(8)
        got(13)
        got(16)
        total[pl.ds(HALF, HALF), :] = added(
            part(a.me, HALF, HALF)[...], box(8)[...], box(13)[...], box(16)[...]
        )

    return begin, one, two, three


def scatter_kernel(parts, total, land, sends, receives):
    around = Around()
    mail = Mail(sends, receives)
    greet(around.peers())
    for step in scatter_steps(around, mail, parts, total, land):
        step()
    mail.finish()


def scatter_rows(parts, collective):
    return pl.pallas_call(
        scatter_kernel,
        out_shape=jax.ShapeDtypeStruct(parts.shape[1:], F32),
        in_specs=[pl.BlockSpec(memory_space=pltpu.VMEM)],
        out_specs=pl.BlockSpec(memory_space=pltpu.VMEM),
        scratch_shapes=[
            pltpu.VMEM((sum(SCATTER_ROWS), parts.shape[2]), parts.dtype),
            pltpu.SemaphoreType.DMA((SCATTER_MAILS,)),
            pltpu.SemaphoreType.DMA((SCATTER_MAILS,)),
        ],
        compiler_params=pltpu.CompilerParams(
            collective_id=collective, has_side_effects=True, vmem_limit_bytes=VMEM_LIMIT
        ),
        name="scatter_rows",
    )(parts)


def scatter_weights_kernel(
    parts, grads, total, shard, land, w_land, w_sum, sends, receives, w_sends, w_receives
):
    around, ring = Around(), Ring()
    mail, wmail = Mail(sends, receives), Mail(w_sends, w_receives)
    a, r = around, ring
    greet(a.peers() + r.peers())
    begin, one, two, three = scatter_steps(a, mail, parts, total, land)
    begin()
    blocks = [(side, step) for step in (1, 2, 3, 0) for side in (0, 1)]

    def place(side, step):
        zh = r.zh if side == 0 else 1 - r.zh
        return zh * 4 + r.xs[step]

    for number, (side, step) in enumerate(blocks):
        wmail.send(number, grads.at[place(side, step), 1 - r.core], w_land.at[number], r.to_core)
    for number, (side, step) in enumerate(blocks):
        wmail.landed(number, w_land.at[number], r.to_core)
        w_land[number] = added(grads[place(side, step), r.core], w_land[number]).astype(BF16)
        if step:
            wmail.send(8 + number, w_land.at[number], w_land.at[8 + number], r.to_x[step])
    one()
    two()
    for number in range(6):
        wmail.landed(8 + number, w_land.at[8 + number], r.to_core)
    w_land[7] = added(w_land[7], w_land[9], w_land[11], w_land[13]).astype(BF16)
    wmail.send(14, w_land.at[7], w_land.at[14], r.to_zh)
    w_sum[...] = added(w_land[6], w_land[8], w_land[10], w_land[12])
    three()
    wmail.landed(14, w_land.at[14], r.to_core)
    shard[...] = added(w_sum[...], w_land[14])
    mail.finish()
    wmail.finish()


def scatter_weights(parts, grads, collective):
    block = grads.shape[2:]
    return pl.pallas_call(
        scatter_weights_kernel,
        out_shape=(
            jax.ShapeDtypeStruct(parts.shape[1:], F32),
            jax.ShapeDtypeStruct(block, F32),
        ),
        in_specs=[pl.BlockSpec(memory_space=pltpu.VMEM)] * 2,
        out_specs=(pl.BlockSpec(memory_space=pltpu.VMEM),) * 2,
        scratch_shapes=[
            pltpu.VMEM((sum(SCATTER_ROWS), parts.shape[2]), parts.dtype),
            pltpu.VMEM((15,) + block, grads.dtype),
            pltpu.VMEM(block, F32),
            pltpu.SemaphoreType.DMA((SCATTER_MAILS,)),
            pltpu.SemaphoreType.DMA((SCATTER_MAILS,)),
            pltpu.SemaphoreType.DMA((15,)),
            pltpu.SemaphoreType.DMA((15,)),
        ],
        compiler_params=pltpu.CompilerParams(
            collective_id=collective, has_side_effects=True, vmem_limit_bytes=VMEM_LIMIT
        ),
        name="scatter_weights",
    )(parts, grads)


SUM_ROWS, SUM_NORMS = 72, 64


def sum_kernel(values, total, boxes, sends, receives):
    a, r = Around(), Ring()
    mail = Mail(sends, receives)
    x_peers = r.to_x[1:]
    z_peers = [
        (r.index(1 - r.zh, r.x, r.core), r.tensor),
        (r.index(r.zh, r.x, 1 - r.core), r.tensor),
        (r.index(1 - r.zh, r.x, 1 - r.core), r.tensor),
    ]
    y_peers = [(r.dp, a.up), (r.dp, a.far), (r.dp, a.down)]
    greet(x_peers + z_peers + y_peers + [a.to_across])

    def stage(base, count, mine, sources, peers):
        view = pl.ds(0, count)
        for number, peer in enumerate(peers):
            mail.send(base + number, boxes.at[base + mine, view], boxes.at[base + mine, view], peer)
        for number, source in enumerate(sources):
            mail.landed(base + number, boxes.at[base + source, view], peers[0])
        result = boxes[base, view]
        for k in range(1, len(peers) + 1):
            result = result + boxes[base + k, view]
        return result

    boxes[r.x] = values[...]
    first = stage(0, SUM_ROWS, r.x, [r.xs[3], r.xs[2], r.xs[1]], x_peers)
    place = r.zh * 2 + r.core
    boxes[4 + place] = first
    second = stage(
        4,
        SUM_ROWS,
        place,
        [(1 - r.zh) * 2 + r.core, r.zh * 2 + 1 - r.core, (1 - r.zh) * 2 + 1 - r.core],
        z_peers,
    )
    total[...] = second
    boxes[8 + a.y, pl.ds(0, SUM_NORMS)] = second[:SUM_NORMS]
    third = stage(8, SUM_NORMS, a.y, [a.y_down, a.y_far, a.y_up], y_peers)
    boxes[12 + a.z, pl.ds(0, SUM_NORMS)] = third
    total[pl.ds(0, SUM_NORMS), :] = stage(12, SUM_NORMS, a.z, [1 - a.z], [a.to_across])
    mail.finish()


def sum_all(values, collective):
    return pl.pallas_call(
        sum_kernel,
        out_shape=jax.ShapeDtypeStruct(values.shape, F32),
        in_specs=[pl.BlockSpec(memory_space=pltpu.VMEM)],
        out_specs=pl.BlockSpec(memory_space=pltpu.VMEM),
        scratch_shapes=[
            pltpu.VMEM((14, SUM_ROWS, 128), F32),
            pltpu.SemaphoreType.DMA((13,)),
            pltpu.SemaphoreType.DMA((13,)),
        ],
        compiler_params=pltpu.CompilerParams(
            collective_id=collective, has_side_effects=True, vmem_limit_bytes=VMEM_LIMIT
        ),
        name="sum_all",
    )(values)


def norm_parts(values, gain, shift):
    centred = values - jnp.mean(values, axis=-1, keepdims=True)
    variance = jnp.mean(centred * centred, axis=-1, keepdims=True)
    rinv = lax.rsqrt(variance + EPS)
    normal = centred * rinv
    return (normal * gain + shift, normal, rinv)


def norm_back(incoming, normal, rinv, gain):
    scaled = incoming * gain
    inner = (
        scaled
        - jnp.mean(scaled, axis=-1, keepdims=True)
        - normal * jnp.mean(scaled * normal, axis=-1, keepdims=True)
    )
    return (rinv * inner, jnp.sum(incoming * normal, axis=0), jnp.sum(incoming, axis=0))


def angles(group_ids):
    group = group_ids.shape[0]
    index = jnp.arange(group, dtype=jnp.int32)
    numbers = jnp.arange(DOCS, dtype=jnp.int32)
    before = (group_ids[None, :] >= 0) & (group_ids[None, :] < numbers[:, None])
    starts = jnp.sum(before.astype(jnp.int32), axis=1)
    offset = jnp.sum(jnp.where(group_ids[:, None] == numbers[None, :], starts[None, :], 0), axis=1)
    position = (index - offset).astype(jnp.float32)
    freq = jnp.power(10000.0, -2.0 * jnp.arange(ROT // 2, dtype=jnp.float32) / ROT)
    angle = position[:, None] * freq[None, :]
    return (jnp.cos(angle), jnp.sin(angle))


def rotate(values, cosine, sine):
    half = ROT // 2
    first_part = values[..., :half]
    second_part = values[..., half:ROT]
    cosine = cosine[:, None, :]
    sine = sine[:, None, :]
    return jnp.concatenate(
        [
            first_part * cosine - second_part * sine,
            second_part * cosine + first_part * sine,
            values[..., ROT:],
        ],
        axis=-1,
    )


def allowed_keys(row_ids, row_first, col_ids):
    rows = row_first + jnp.arange(row_ids.shape[0], dtype=jnp.int32)
    cols = jnp.arange(col_ids.shape[0], dtype=jnp.int32)
    same = (
        (row_ids[:, None] == col_ids[None, :])
        & (col_ids[None, :] >= 0)
        & (cols[None, :] < rows[:, None])
    )
    return same | (cols[None, :] == rows[:, None])


def product(spec, left, right):
    return jnp.einsum(spec, left, right, preferred_element_type=F32)


def body(
    tokens,
    doc_ids,
    qkv_weight,
    qkv_bias,
    out_weight,
    norm1_gain,
    norm1_shift,
    norm2_gain,
    norm2_shift,
    gate_up_weight,
    down_weight,
    cotangent,
):
    inputs = tokens.astype(F32)
    group = ROWS * TENSOR
    feed_shard = jnp.concatenate([jnp.swapaxes(gate_up_weight, 1, 2), down_weight[None]])
    feed = lax.all_gather(feed_shard, "dp", axis=2, tiled=True)
    normed1, normal1, rinv1 = norm_parts(inputs, norm1_gain, norm1_shift)
    shard = jnp.concatenate([qkv_weight, out_weight.T[None]])
    rows1, id_rows, projections = gather_weights(
        normed1.astype(BF16), jnp.broadcast_to(doc_ids[None], (8, ROWS)), shard, 0
    )
    rows1 = rows1.reshape(group, WIDTH)
    qkv_full, out_full = projections[:3], projections[3]
    group_ids = jnp.swapaxes(id_rows[:, :, 0], 0, 1).reshape(group)
    local_width = qkv_full.shape[2]
    heads = local_width // HEAD_DIM
    scale = HEAD_DIM ** (-0.5)
    cosine, sine = angles(group_ids)
    projected = product("td,cde->cte", rows1, qkv_full) + qkv_bias[:, None, :]
    query = rotate(projected[0].reshape(group, heads, HEAD_DIM), cosine, sine).astype(BF16)
    keys_all = rotate(projected[1].reshape(group, heads, HEAD_DIM), cosine, sine).astype(BF16)
    values_all = projected[2].reshape(group, heads, HEAD_DIM).astype(BF16)
    block = min(512, group)
    outputs = []
    lse_parts = []
    for first_row in range(0, group, block):
        query_block = query[first_row : first_row + block]
        scores = product("qhd,khd->hqk", query_block, keys_all) * scale
        allow = allowed_keys(group_ids[first_row : first_row + block], first_row, group_ids)
        masked = jnp.where(allow[None], scores, -1e30)
        highest = jnp.max(masked, axis=-1, keepdims=True)
        expon = jnp.exp(masked - highest)
        totals = jnp.sum(expon, axis=-1, keepdims=True)
        probs = expon / totals
        lse_parts.append(highest + jnp.log(totals))
        outputs.append(product("hqk,khd->qhd", probs.astype(BF16), values_all))
    attended = jnp.concatenate(outputs, axis=0).reshape(group, local_width).astype(BF16)
    log_totals = jnp.concatenate(lse_parts, axis=1)
    branch = product("te,de->td", attended, out_full).astype(BF16)
    mixed = inputs + scatter_rows(branch.reshape(TENSOR, ROWS, WIDTH), 1)
    normed2, normal2, rinv2 = norm_parts(mixed, norm2_gain, norm2_shift)
    rows2 = gather_rows(normed2.astype(BF16), 2).reshape(group, WIDTH)
    grad_rows = gather_rows(cotangent, 3).reshape(group, WIDTH)
    gate_up = product("td,cfd->ctf", rows2, feed[:2])
    gate = gate_up[0]
    upward = gate_up[1]
    sigma = jax.nn.sigmoid(gate)
    hidden = (gate * sigma * upward).astype(BF16)
    feed_out = product("tf,fd->td", hidden, feed[2]).astype(BF16)
    grad_hidden = product("td,fd->tf", grad_rows, feed[2])
    grad_gate = grad_hidden * upward * sigma * (1.0 + gate * (1.0 - sigma))
    grad_upward = grad_hidden * (gate * sigma)
    grad_gate_up = jnp.stack([grad_gate, grad_upward]).astype(BF16)
    grad_feed = product("ctf,cfd->td", grad_gate_up, feed[:2]).astype(BF16)
    grad_normed2 = scatter_rows(grad_feed.reshape(TENSOR, ROWS, WIDTH), 4)
    layer_out = (mixed + scatter_rows(feed_out.reshape(TENSOR, ROWS, WIDTH), 5)).astype(BF16)
    down_grad = product("tf,td->fd", hidden, grad_rows).astype(BF16)
    gate_up_grad = product("ctf,td->cfd", grad_gate_up, rows2).astype(BF16)
    units = down_grad.shape[0]
    feed_grad = jnp.concatenate([gate_up_grad, down_grad[None]]).reshape(3 * units, 16, ROWS)
    feed_grad = lax.psum_scatter(
        jnp.swapaxes(feed_grad, 0, 1), "dp", scatter_dimension=0, tiled=False
    ).astype(F32)
    gate_up_shard = jnp.swapaxes(feed_grad[: 2 * units].reshape(2, units, ROWS), 1, 2)
    down_shard = feed_grad[2 * units :]
    back2, gain2_grad, shift2_grad = norm_back(grad_normed2, normal2, rinv2, norm2_gain)
    grad_mixed = cotangent.astype(F32) + back2
    branch_grad = gather_rows(grad_mixed.astype(BF16), 6).reshape(group, WIDTH)
    out_grad = product("td,te->de", branch_grad, attended).astype(BF16)
    grad_attended = product("td,de->te", branch_grad, out_full)
    grad_attended = grad_attended.astype(BF16).reshape(group, heads, HEAD_DIM)
    grad_query_parts = []
    grad_keys = jnp.zeros((group, heads, HEAD_DIM), F32)
    grad_values = jnp.zeros((group, heads, HEAD_DIM), F32)
    for first_row in range(0, group, block):
        query_block = query[first_row : first_row + block]
        scores = product("qhd,khd->hqk", query_block, keys_all) * scale
        allow = allowed_keys(group_ids[first_row : first_row + block], first_row, group_ids)
        probs = jnp.where(
            allow[None], jnp.exp(scores - log_totals[:, first_row : first_row + block]), 0.0
        )
        grad_block = grad_attended[first_row : first_row + block]
        grad_probs = product("qhd,khd->hqk", grad_block, values_all)
        inner = jnp.sum(probs * grad_probs, axis=-1, keepdims=True)
        grad_scores = (probs * (grad_probs - inner)).astype(BF16)
        grad_query_parts.append(product("hqk,khd->qhd", grad_scores, keys_all) * scale)
        grad_keys = grad_keys + product("hqk,qhd->khd", grad_scores, query_block) * scale
        grad_values = grad_values + product("hqk,qhd->khd", probs.astype(BF16), grad_block)
    grad_query = rotate(jnp.concatenate(grad_query_parts, axis=0), cosine, -sine)
    grad_keys = rotate(grad_keys, cosine, -sine)
    grad_pre = (
        jnp.stack([grad_query, grad_keys, grad_values]).reshape(3, group, local_width).astype(BF16)
    )
    bias_part = jnp.sum(grad_pre.astype(F32), axis=1)
    qkv_grad = product("td,cte->cde", rows1, grad_pre).astype(BF16)
    grad_back = product("cte,cde->td", grad_pre, qkv_full).astype(BF16)
    grads = jnp.concatenate([qkv_grad, out_grad[None]]).reshape(4, 8, 2, ROWS, local_width)
    grad_normed1, weight_shard = scatter_weights(
        grad_back.reshape(TENSOR, ROWS, WIDTH), jnp.moveaxis(grads, 0, 2), 7
    )
    qkv_shard, out_shard = weight_shard[:3], weight_shard[3].T
    back1, gain1_grad, shift1_grad = norm_back(grad_normed1, normal1, rinv1, norm1_gain)
    token_grad = (grad_mixed + back1).astype(BF16)
    norms = jnp.concatenate([gain1_grad, shift1_grad, gain2_grad, shift2_grad, bias_part.reshape(-1)])
    sums = sum_all(jnp.pad(norms.reshape(-1, 128), ((0, 2), (0, 0))), 8)
    gain1_sum, shift1_sum, gain2_sum, shift2_sum = sums[:64].reshape(4, WIDTH)
    bias_grad = sums[64:70].reshape(3, local_width)
    return (
        layer_out,
        token_grad,
        qkv_shard,
        bias_grad,
        out_shard,
        gain1_sum,
        shift1_sum,
        gain2_sum,
        shift2_sum,
        gate_up_shard,
        down_shard,
    )


def solution(mesh):
    in_specs = (
        P(("dp", "tensor"), None),
        P(("dp", "tensor")),
        P(None, "dp", "tensor"),
        P(None, "tensor"),
        P("tensor", "dp"),
        P(),
        P(),
        P(),
        P(),
        P(None, "dp", "tensor"),
        P("tensor", "dp"),
        P(("dp", "tensor"), None),
    )
    out_specs = (
        P(("dp", "tensor"), None),
        P(("dp", "tensor"), None),
        P(None, "dp", "tensor"),
        P(None, "tensor"),
        P("tensor", "dp"),
        P(),
        P(),
        P(),
        P(),
        P(None, "dp", "tensor"),
        P("tensor", "dp"),
    )
    return jax.shard_map(body, mesh=mesh, in_specs=in_specs, out_specs=out_specs, check_vma=False)
```

```python
import functools

import jax
import jax.numpy as jnp
from jax import lax
from jax.experimental import pallas as pl
from jax.experimental.pallas import tpu as pltpu
from jax.sharding import PartitionSpec as P

HEAD_DIM = 64
ROT = 16
DOCS = 4
EPS = 1e-05

ROWS = 128
WIDTH = 2048
TENSOR = 8
HALF = ROWS // 2
QUARTER = ROWS // 4
MESH = pl.DeviceIdType.MESH
BF16 = jnp.bfloat16
F32 = jnp.float32
VMEM_LIMIT = 56 * 2**20


def coordinates():
    tensor = lax.axis_index("tensor")
    return lax.axis_index("dp"), tensor // 2, lax.rem(tensor, 2)


class Around:
    def __init__(self):
        dp, y, z = coordinates()
        up, down, far = lax.rem(y + 1, 4), lax.rem(y + 3, 4), lax.rem(y + 2, 4)
        other = 1 - z
        self.me, self.across = y * 2 + z, y * 2 + other
        self.up, self.down, self.far = up * 2 + z, down * 2 + z, far * 2 + z
        self.up_o, self.down_o, self.far_o = up * 2 + other, down * 2 + other, far * 2 + other
        self.y, self.z = y, z
        self.y_up, self.y_down, self.y_far = up, down, far
        self.to_up, self.to_down, self.to_across = (dp, self.up), (dp, self.down), (dp, self.across)

    def peers(self):
        return [self.to_up, self.to_down, self.to_across]


class Ring:
    def __init__(self):
        dp = lax.axis_index("dp")
        tensor = lax.axis_index("tensor")
        zh, x, core = dp // 8, lax.rem(dp // 2, 4), lax.rem(dp, 2)
        self.zh, self.x, self.core, self.dp, self.tensor = zh, x, core, dp, tensor
        self.xs = [lax.rem(x + step, 4) for step in range(4)]
        self.to_x = [(self.index(zh, self.xs[step], core), tensor) for step in range(4)]
        self.to_zh = (self.index(1 - zh, x, core), tensor)
        self.to_core = (self.index(zh, x, 1 - core), tensor)

    def index(self, zh, x, core):
        return zh * 8 + x * 2 + core

    def peers(self):
        return self.to_x[1:] + [self.to_zh, self.to_core]


def greet(peers):
    barrier = pltpu.get_barrier_semaphore()
    for peer in peers:
        pl.semaphore_signal(barrier, inc=1, device_id=peer, device_id_type=MESH)
    pl.semaphore_wait(barrier, len(peers))


class Mail:
    def __init__(self, sends, receives):
        self.sends, self.receives = sends, receives
        self.out = []

    def send(self, number, source, target, device):
        copy = pltpu.make_async_remote_copy(
            src_ref=source,
            dst_ref=target,
            send_sem=self.sends.at[number],
            recv_sem=self.receives.at[number],
            device_id=device,
            device_id_type=MESH,
        )
        copy.start()
        self.out.append(copy)

    def landed(self, number, target, device):
        pltpu.make_async_remote_copy(
            src_ref=target,
            dst_ref=target,
            send_sem=self.sends.at[number],
            recv_sem=self.receives.at[number],
            device_id=device,
            device_id_type=MESH,
        ).wait_recv()

    def finish(self):
        for copy in self.out:
            copy.wait_send()


def gather_steps(around, mail, own, rows):
    a = around

    def part(slot, first, count):
        return rows.at[slot, pl.ds(first, count)]

    def begin():
        for number, first, device in (
            (0, 0, a.to_up),
            (1, HALF, a.to_down),
            (2, HALF, a.to_across),
            (3, HALF, a.to_up),
            (4, 0, a.to_down),
            (5, 0, a.to_across),
        ):
            mail.send(number, own.at[pl.ds(first, HALF)], part(a.me, first, HALF), device)

    def pass_on(number, slot, first, count, device):
        mail.send(number, part(slot, first, count), part(slot, first, count), device)

    def got(number, slot, first, count):
        mail.landed(number, part(slot, first, count), a.to_up)

    def one():
        got(0, a.down, 0, HALF)
        pass_on(6, a.down, 0, HALF, a.to_up)
        pass_on(7, a.down, 0, HALF, a.to_across)
        got(1, a.up, HALF, HALF)
        pass_on(8, a.up, HALF, HALF, a.to_down)
        got(2, a.across, HALF, HALF)
        pass_on(9, a.across, HALF, HALF, a.to_up)
        pass_on(10, a.across, HALF, HALF, a.to_down)

    def two():
        got(4, a.up, 0, HALF)
        pass_on(11, a.up, 0, HALF, a.to_across)
        got(3, a.down, HALF, HALF)
        got(5, a.across, 0, HALF)

    def three():
        got(6, a.far, 0, HALF)
        pass_on(12, a.far, 0, HALF, a.to_across)
        got(8, a.far, HALF, HALF)

    def four():
        got(9, a.down_o, HALF, HALF)
        pass_on(13, a.down_o, HALF, QUARTER, a.to_up)
        got(10, a.up_o, HALF, HALF)
        pass_on(14, a.up_o, HALF + QUARTER, QUARTER, a.to_down)

    def five():
        got(7, a.down_o, 0, HALF)
        got(11, a.up_o, 0, HALF)

    def six():
        got(13, a.far_o, HALF, QUARTER)
        got(14, a.far_o, HALF + QUARTER, QUARTER)
        got(12, a.far_o, 0, HALF)

    return begin, one, two, three, four, five, six


GATHER_MAILS = 15


def spread_steps(ring, mail, shard, block):
    r = ring

    def share(number, zh, x, device):
        mail.send(number, block(zh, x, r.core), block(zh, x, r.core), device)

    def came(number, zh, x, core):
        mail.landed(number, block(zh, x, core), r.to_core)

    def begin():
        mine = block(r.zh, r.x, r.core)
        mail.send(0, shard, mine, r.to_zh)
        for step in (1, 2, 3):
            mail.send(step, shard, mine, r.to_x[step])
        mail.send(7, shard, mine, r.to_core)

    def one():
        came(0, 1 - r.zh, r.x, r.core)
        for step in (1, 2, 3):
            share(3 + step, 1 - r.zh, r.x, r.to_x[step])
        share(8, 1 - r.zh, r.x, r.to_core)

    def two():
        for step in (1, 2, 3):
            came(step, r.zh, r.xs[4 - step], r.core)
            share(8 + step, r.zh, r.xs[4 - step], r.to_core)

    def three():
        for step in (1, 2, 3):
            came(3 + step, 1 - r.zh, r.xs[4 - step], r.core)
            share(11 + step, 1 - r.zh, r.xs[4 - step], r.to_core)

    def four():
        sibling = 1 - r.core
        came(7, r.zh, r.x, sibling)
        came(8, 1 - r.zh, r.x, sibling)
        for step in (1, 2, 3):
            came(8 + step, r.zh, r.xs[4 - step], sibling)
            came(11 + step, 1 - r.zh, r.xs[4 - step], sibling)

    return begin, one, two, three, four


IDS = 4


def gather_weights_kernel(
    own, ids, shard, rows, id_rows, full, sends, receives, w_sends, w_receives, i_sends, i_receives, local
):
    a, r = Around(), Ring()
    mail, wmail, imail = (
        Mail(sends, receives),
        Mail(w_sends, w_receives),
        Mail(i_sends, i_receives),
    )

    def block(zh, x, core):
        first = pl.multiple_of(r.index(zh, x, core) * ROWS, ROWS)
        return full.at[:, pl.ds(first, ROWS), :]

    keeps = [
        pltpu.make_async_copy(own, rows.at[a.me], local.at[0]),
        pltpu.make_async_copy(ids, id_rows.at[a.z, a.y], local.at[1]),
        pltpu.make_async_copy(shard, block(r.zh, r.x, r.core), local.at[2]),
    ]
    for keep in keeps:
        keep.start()
    greet(a.peers() + r.peers())
    steps = gather_steps(a, mail, own, rows)
    spread = spread_steps(r, wmail, shard, block)
    steps[0]()
    imail.send(0, ids, id_rows.at[a.z, a.y], a.to_up)
    imail.send(1, ids, id_rows.at[a.z, a.y], a.to_down)
    spread[0]()
    imail.landed(0, id_rows.at[a.z, a.y_down], a.to_up)
    imail.send(2, id_rows.at[a.z, a.y_down], id_rows.at[a.z, a.y_down], a.to_up)
    imail.landed(1, id_rows.at[a.z, a.y_up], a.to_up)
    imail.landed(2, id_rows.at[a.z, a.y_far], a.to_up)
    keeps[1].wait()
    imail.send(3, id_rows.at[a.z], id_rows.at[a.z], a.to_across)
    steps[1]()
    spread[1]()
    steps[2]()
    spread[2]()
    steps[3]()
    steps[4]()
    spread[3]()
    steps[5]()
    steps[6]()
    spread[4]()
    imail.landed(3, id_rows.at[1 - a.z], a.to_up)
    mail.finish()
    wmail.finish()
    imail.finish()
    keeps[0].wait()
    keeps[2].wait()


WEIGHT_MAILS = 15


def gather_weights(own, ids, shard, collective):
    parts, rows, columns = shard.shape
    return pl.pallas_call(
        gather_weights_kernel,
        out_shape=(
            jax.ShapeDtypeStruct((TENSOR,) + own.shape, own.dtype),
            jax.ShapeDtypeStruct((2, 4) + ids.shape, ids.dtype),
            jax.ShapeDtypeStruct((parts, rows * 16, columns), shard.dtype),
        ),
        in_specs=[pl.BlockSpec(memory_space=pltpu.VMEM)] * 3,
        out_specs=(pl.BlockSpec(memory_space=pl.ANY),) * 3,
        scratch_shapes=[
            pltpu.SemaphoreType.DMA((GATHER_MAILS,)),
            pltpu.SemaphoreType.DMA((GATHER_MAILS,)),
            pltpu.SemaphoreType.DMA((WEIGHT_MAILS,)),
            pltpu.SemaphoreType.DMA((WEIGHT_MAILS,)),
            pltpu.SemaphoreType.DMA((IDS,)),
            pltpu.SemaphoreType.DMA((IDS,)),
            pltpu.SemaphoreType.DMA((3,)),
        ],
        compiler_params=pltpu.CompilerParams(
            collective_id=collective, has_side_effects=True, vmem_limit_bytes=VMEM_LIMIT
        ),
        name="gather_weights",
    )(own, ids, shard)


def added(*terms):
    total = terms[0].astype(F32)
    for term in terms[1:]:
        total = total + term.astype(F32)
    return total


SCATTER_MAILS = 17
SCATTER_ROWS = (32, 32, 64, 64, 64, 64, 32, 32, 64, 64, 64, 32, 32, 64, 64, 64, 64)
SCATTER_FIRST = tuple(sum(SCATTER_ROWS[:k]) for k in range(SCATTER_MAILS))


def scatter_steps(around, mail, parts, total, land):
    a = around

    def part(slot, first, count):
        return parts.at[slot, pl.ds(first, count)]

    def box(number):
        return land.at[pl.ds(SCATTER_FIRST[number], SCATTER_ROWS[number])]

    def direct(number, slot, first, device):
        mail.send(number, part(slot, first, SCATTER_ROWS[number]), box(number), device)

    def got(number):
        mail.landed(number, box(number), a.to_up)

    def fold(stage, slot, first, others=()):
        count = SCATTER_ROWS[stage]
        terms = [part(slot, first, count)[...], box(stage)[...]]
        terms += [box(other)[...] for other in others]
        box(stage)[...] = added(*terms).astype(BF16)

    def begin():
        direct(0, a.far_o, 96, a.to_up)
        direct(1, a.far_o, 64, a.to_down)
        direct(2, a.far_o, 0, a.to_across)
        direct(3, a.far, 64, a.to_up)
        direct(4, a.up_o, 0, a.to_across)
        direct(5, a.down_o, 0, a.to_across)
        direct(6, a.down_o, 96, a.to_down)
        direct(7, a.up_o, 64, a.to_up)
        direct(8, a.down, 64, a.to_down)
        direct(9, a.across, 0, a.to_across)

    def one():
        got(1)
        fold(1, a.down_o, 64)
        mail.send(11, box(1), box(11), a.to_down)
        got(0)
        fold(0, a.up_o, 96)
        mail.send(12, box(0), box(12), a.to_up)
        got(2)
        fold(2, a.far, 0)
        mail.send(10, box(2), box(10), a.to_down)
        got(3)
        fold(3, a.up, 64)
        mail.send(13, box(3), box(13), a.to_up)

    def two():
        got(4)
        fold(4, a.up, 0)
        mail.send(14, box(4), box(14), a.to_up)
        got(5)
        got(10)
        fold(5, a.down, 0, (10,))
        mail.send(15, box(5), box(15), a.to_down)
        got(6)
        got(7)
        got(11)
        got(12)
        upper = added(part(a.across, 64, 32)[...], box(7)[...], box(11)[...]).astype(BF16)
        lower = added(part(a.across, 96, 32)[...], box(6)[...], box(12)[...]).astype(BF16)
        land.at[pl.ds(SCATTER_FIRST[6], 32)][...] = upper
        land.at[pl.ds(SCATTER_FIRST[7], 32)][...] = lower
        both = land.at[pl.ds(SCATTER_FIRST[6], 64)]
        mail.send(16, both, box(16), a.to_across)

    def three():
        got(9)
        got(14)
        got(15)
        total[pl.ds(0, HALF), :] = added(
            part(a.me, 0, HALF)[...], box(9)[...], box(14)[...], box(15)[...]
        )
        got(8)
        got(13)
        got(16)
        total[pl.ds(HALF, HALF), :] = added(
            part(a.me, HALF, HALF)[...], box(8)[...], box(13)[...], box(16)[...]
        )

    return begin, one, two, three


def blocks_steps(ring, mail, grads, land, own_sum, shard):
    r = ring
    blocks = [(side, step) for step in (1, 2, 3, 0) for side in (0, 1)]

    def place(side, step, core):
        zh = r.zh if side == 0 else 1 - r.zh
        return r.index(zh, r.xs[step], core)

    def begin():
        for number, (side, step) in enumerate(blocks):
            mail.send(number, grads.at[place(side, step, 1 - r.core)], land.at[number], r.to_core)

    def one():
        for number, (side, step) in enumerate(blocks):
            mail.landed(number, land.at[number], r.to_core)
            land[number] = added(grads[place(side, step, r.core)], land[number]).astype(BF16)
            if step:
                mail.send(8 + number, land.at[number], land.at[8 + number], r.to_x[step])

    def two():
        for number in (1, 3, 5):
            mail.landed(8 + number, land.at[8 + number], r.to_core)
        land[7] = added(land[7], land[9], land[11], land[13]).astype(BF16)
        mail.send(14, land.at[7], land.at[14], r.to_zh)
        for number in (0, 2, 4):
            mail.landed(8 + number, land.at[8 + number], r.to_core)
        own_sum[...] = added(land[6], land[8], land[10], land[12])

    def three():
        mail.landed(14, land.at[14], r.to_core)
        shard[...] = added(own_sum[...], land[14])

    return begin, one, two, three


BLOCK_MAILS = 15


SUM_ROWS, SUM_NORMS = 72, 64


def sum_kernel(values, total, boxes, sends, receives):
    a, r = Around(), Ring()
    mail = Mail(sends, receives)
    x_peers = r.to_x[1:]
    z_peers = [
        (r.index(1 - r.zh, r.x, r.core), r.tensor),
        (r.index(r.zh, r.x, 1 - r.core), r.tensor),
        (r.index(1 - r.zh, r.x, 1 - r.core), r.tensor),
    ]
    y_peers = [(r.dp, a.up), (r.dp, a.far), (r.dp, a.down)]
    greet(x_peers + z_peers + y_peers + [a.to_across])

    def stage(base, count, mine, sources, peers):
        view = pl.ds(0, count)
        for number, peer in enumerate(peers):
            mail.send(base + number, boxes.at[base + mine, view], boxes.at[base + mine, view], peer)
        for number, source in enumerate(sources):
            mail.landed(base + number, boxes.at[base + source, view], peers[0])
        result = boxes[base, view]
        for k in range(1, len(peers) + 1):
            result = result + boxes[base + k, view]
        return result

    boxes[r.x] = values[...]
    first = stage(0, SUM_ROWS, r.x, [r.xs[3], r.xs[2], r.xs[1]], x_peers)
    place = r.zh * 2 + r.core
    boxes[4 + place] = first
    second = stage(
        4,
        SUM_ROWS,
        place,
        [(1 - r.zh) * 2 + r.core, r.zh * 2 + 1 - r.core, (1 - r.zh) * 2 + 1 - r.core],
        z_peers,
    )
    total[...] = second
    boxes[8 + a.y, pl.ds(0, SUM_NORMS)] = second[:SUM_NORMS]
    third = stage(8, SUM_NORMS, a.y, [a.y_down, a.y_far, a.y_up], y_peers)
    boxes[12 + a.z, pl.ds(0, SUM_NORMS)] = third
    total[pl.ds(0, SUM_NORMS), :] = stage(12, SUM_NORMS, a.z, [1 - a.z], [a.to_across])
    mail.finish()


def sum_all(values, collective):
    return pl.pallas_call(
        sum_kernel,
        out_shape=jax.ShapeDtypeStruct(values.shape, F32),
        in_specs=[pl.BlockSpec(memory_space=pltpu.VMEM)],
        out_specs=pl.BlockSpec(memory_space=pltpu.VMEM),
        scratch_shapes=[
            pltpu.VMEM((14, SUM_ROWS, 128), F32),
            pltpu.SemaphoreType.DMA((13,)),
            pltpu.SemaphoreType.DMA((13,)),
        ],
        compiler_params=pltpu.CompilerParams(
            collective_id=collective, has_side_effects=True, vmem_limit_bytes=VMEM_LIMIT
        ),
        name="sum_all",
    )(values)


HEADS_DEV = 4
LOCAL = HEADS_DEV * HEAD_DIM
GROUP = ROWS * TENSOR
QBLOCK = 256
UNITS = 704
LANES = 128
SCALE = HEAD_DIM ** (-0.5)


def dot(left, right):
    return lax.dot_general(left, right, (((1,), (0,)), ((), ())), preferred_element_type=F32)


def dot_t(left, right):
    return lax.dot_general(left, right, (((1,), (1,)), ((), ())), preferred_element_type=F32)


def turned(values, tables, row, sign):
    rows = pl.ds(row, values.shape[0])
    cosine, minus, plus = tables[0, rows], tables[1, rows], tables[2, rows]
    halves = []
    for first in range(0, LOCAL, LANES):
        part = values[:, first : first + LANES]
        left = pltpu.roll(part, LANES - ROT // 2, 1)
        right = pltpu.roll(part, ROT // 2, 1)
        halves.append(part * cosine + sign * (left * minus + right * plus))
    return jnp.concatenate(halves, axis=1)


def head_lanes(head, rows):
    return lax.broadcasted_iota(jnp.int32, (rows, LOCAL), 1) // HEAD_DIM == head


def only(mask, values):
    return jnp.where(mask, values, jnp.zeros_like(values))


def attention_kernel(
    rows,
    weights,
    bias,
    tables,
    start,
    own,
    shard,
    total,
    gathered,
    feed,
    acts,
    attended,
    logs,
    parts,
    land,
    sends,
    receives,
    g_sends,
    g_receives,
    w_sends,
    w_receives,
    local,
):
    a, r = Around(), Ring()
    mail, gmail, wmail = Mail(sends, receives), Mail(g_sends, g_receives), Mail(w_sends, w_receives)

    def block(zh, x, core):
        return feed.at[r.index(zh, x, core)]

    keeps = [
        pltpu.make_async_copy(own, gathered.at[a.me], local.at[0]),
        pltpu.make_async_copy(shard, block(r.zh, r.x, r.core), local.at[1]),
    ]
    for keep in keeps:
        keep.start()
    greet(a.peers() + r.peers())
    gather = gather_steps(a, gmail, own, gathered)
    spread = spread_steps(r, wmail, shard, block)
    scatter = scatter_steps(a, mail, parts, total, land)
    gather[0]()
    spread[0]()

    def project(index, carry):
        first = pl.multiple_of(index * QBLOCK, QBLOCK)
        chunk = rows[pl.ds(first, QBLOCK), :]
        for c in range(3):
            pre = dot(chunk, weights[c]) + bias[pl.ds(c, 1), :]
            if c < 2:
                pre = turned(pre, tables, first, 1.0)
            acts[c, pl.ds(first, QBLOCK), :] = pre.astype(BF16)
        return carry

    lax.fori_loop(0, GROUP // QBLOCK, project, 0)
    spread[1]()

    def attend(first):
        count = first + QBLOCK
        query = acts[0, pl.ds(first, QBLOCK), :] * BF16(SCALE)
        row = first + lax.broadcasted_iota(jnp.int32, (QBLOCK, count), 0)
        column = lax.broadcasted_iota(jnp.int32, (QBLOCK, count), 1)
        allow = (column <= row) & (column >= start[pl.ds(first, QBLOCK), :])
        lane = lax.broadcasted_iota(jnp.int32, (QBLOCK, LANES), 1)

        def one_head(head, carry):
            out, log = carry
            masked = only(head_lanes(head, QBLOCK), query)
            scores = dot_t(masked, acts[1, pl.ds(0, count), :])
            scores = jnp.where(allow, scores, -1e30)
            highest = jnp.max(scores, axis=1, keepdims=True)
            expon = jnp.exp(scores - highest)
            sums = jnp.sum(expon, axis=1, keepdims=True)
            values = only(head_lanes(head, count), acts[2, pl.ds(0, count), :])
            out = out + dot(expon.astype(BF16), values) / sums
            log = jnp.where(lane == head, highest + jnp.log(sums), log)
            return out, log

        out, log = lax.fori_loop(
            0,
            HEADS_DEV,
            one_head,
            (jnp.zeros((QBLOCK, LOCAL), F32), jnp.zeros((QBLOCK, LANES), F32)),
        )
        attended[pl.ds(first, QBLOCK), :] = out.astype(BF16)
        logs[:, pl.ds(first, QBLOCK)] = log.T[:8]
        branch = dot_t(out.astype(BF16), weights[3]).astype(BF16)
        slot = first // ROWS
        parts[slot] = branch[:ROWS]
        parts[slot + 1] = branch[ROWS:]

    attend(0)
    attend(QBLOCK)
    gather[1]()
    attend(2 * QBLOCK)
    attend(3 * QBLOCK)
    scatter[0]()
    gather[2]()
    spread[2]()
    gather[3]()
    scatter[1]()
    gather[4]()
    scatter[2]()
    spread[3]()
    gather[5]()
    gather[6]()
    scatter[3]()
    spread[4]()
    mail.finish()
    gmail.finish()
    wmail.finish()
    for keep in keeps:
        keep.wait()


def vmem(count):
    return [pl.BlockSpec(memory_space=pltpu.VMEM)] * count


def anywhere(count):
    return [pl.BlockSpec(memory_space=pl.ANY)] * count


def pairs(count):
    return [pltpu.SemaphoreType.DMA((count,)), pltpu.SemaphoreType.DMA((count,))]


def params(collective):
    return pltpu.CompilerParams(
        collective_id=collective, has_side_effects=True, vmem_limit_bytes=VMEM_LIMIT
    )


def attention_forward(rows, weights, bias, tables, start, own, shard, collective):
    return pl.pallas_call(
        attention_kernel,
        out_shape=(
            jax.ShapeDtypeStruct((ROWS, WIDTH), F32),
            jax.ShapeDtypeStruct((TENSOR, ROWS, WIDTH), BF16),
            jax.ShapeDtypeStruct((16,) + shard.shape, BF16),
            jax.ShapeDtypeStruct((3, GROUP, LOCAL), BF16),
            jax.ShapeDtypeStruct((GROUP, LOCAL), BF16),
            jax.ShapeDtypeStruct((8, GROUP), F32),
        ),
        in_specs=vmem(7),
        out_specs=tuple(vmem(1) + anywhere(2) + vmem(3)),
        scratch_shapes=[
            pltpu.VMEM((TENSOR, ROWS, WIDTH), BF16),
            pltpu.VMEM((sum(SCATTER_ROWS), WIDTH), BF16),
            *pairs(SCATTER_MAILS),
            *pairs(GATHER_MAILS),
            *pairs(WEIGHT_MAILS),
            pltpu.SemaphoreType.DMA((2,)),
        ],
        compiler_params=params(collective),
        name="attention_forward",
    )(rows, weights, bias, tables, start, own, shard)


def feed_kernel(
    own,
    gathered,
    feed,
    total,
    outs,
    grads,
    rows,
    cots,
    weights,
    parts,
    acts,
    land,
    sends,
    receives,
    g_sends,
    g_receives,
    w_local,
    local,
):
    a = Around()
    mail, gmail = Mail(sends, receives), Mail(g_sends, g_receives)
    loads = [
        pltpu.make_async_copy(feed.at[n], weights.at[:, pl.ds(n * ROWS, ROWS)], w_local.at[n])
        for n in range(16)
    ]
    keeps = [
        pltpu.make_async_copy(own, rows.at[a.me], local.at[0]),
        pltpu.make_async_copy(gathered, cots, local.at[1]),
    ]
    for copy in keeps[:1] + loads + keeps[1:]:
        copy.start()
    greet(a.peers())
    gather = gather_steps(a, gmail, own, rows)
    scatter = scatter_steps(a, mail, parts, total, land)
    gather[0]()
    for copy in loads + keeps:
        copy.wait()

    def pair(y):
        slots = pl.ds(2 * y, 2)
        x = rows[slots].reshape(2 * ROWS, WIDTH)
        gate = dot_t(x, weights[pl.ds(0, UNITS), :])
        upward = dot_t(x, weights[pl.ds(UNITS, UNITS), :])
        grad_hidden = dot_t(
            cots[slots].reshape(2 * ROWS, WIDTH), weights[pl.ds(2 * UNITS, UNITS), :]
        )
        sigma = jax.nn.sigmoid(gate)
        silu = gate * sigma
        hidden = (silu * upward).astype(BF16)
        grad_gate = (grad_hidden * upward * (sigma + silu * (1.0 - sigma))).astype(BF16)
        grad_up = (grad_hidden * silu).astype(BF16)
        out = dot(hidden, weights[pl.ds(2 * UNITS, UNITS), :]).astype(BF16)
        outs[slots] = out.reshape(2, ROWS, WIDTH)
        back = dot(grad_gate, weights[pl.ds(0, UNITS), :])
        back = back + dot(grad_up, weights[pl.ds(UNITS, UNITS), :])
        parts[slots] = back.astype(BF16).reshape(2, ROWS, WIDTH)
        lanes = pl.ds(pl.multiple_of(y * 2 * ROWS, 2 * ROWS), 2 * ROWS)
        acts[pl.ds(0, UNITS), lanes] = grad_gate.T
        acts[pl.ds(UNITS, UNITS), lanes] = grad_up.T
        acts[pl.ds(2 * UNITS, UNITS), lanes] = hidden.T

    gather[1]()
    gather[2]()
    pair(a.y)
    gather[3]()
    gather[4]()
    gather[5]()
    pair(a.y_down)
    gather[6]()
    pair(a.y_far)
    pair(a.y_up)
    scatter[0]()

    def weight_grad(index, carry):
        columns = pl.ds(pl.multiple_of(index * 2 * ROWS, 2 * ROWS), 2 * ROWS)
        both = dot(acts[pl.ds(0, 2 * UNITS), :], rows[:, :, columns].reshape(GROUP, 2 * ROWS))
        down = dot(acts[pl.ds(2 * UNITS, UNITS), :], cots[:, :, columns].reshape(GROUP, 2 * ROWS))
        for side in range(2):
            lanes = slice(side * ROWS, (side + 1) * ROWS)
            grads[2 * index + side, pl.ds(0, 2 * UNITS), :] = both[:, lanes].astype(BF16)
            grads[2 * index + side, pl.ds(2 * UNITS, UNITS), :] = down[:, lanes].astype(BF16)
        return carry

    lax.fori_loop(0, 3, weight_grad, 0)
    scatter[1]()
    lax.fori_loop(3, 6, weight_grad, 0)
    scatter[2]()
    lax.fori_loop(6, 8, weight_grad, 0)
    scatter[3]()
    mail.finish()
    gmail.finish()


def feed_forward(own, gathered, feed, collective):
    group = (TENSOR, ROWS, WIDTH)
    return pl.pallas_call(
        feed_kernel,
        out_shape=(
            jax.ShapeDtypeStruct((ROWS, WIDTH), F32),
            jax.ShapeDtypeStruct(group, BF16),
            jax.ShapeDtypeStruct((16, 3 * UNITS, ROWS), BF16),
        ),
        in_specs=vmem(1) + anywhere(2),
        out_specs=tuple(vmem(3)),
        scratch_shapes=[
            pltpu.VMEM(group, BF16),
            pltpu.VMEM(group, BF16),
            pltpu.VMEM((3 * UNITS, WIDTH), BF16),
            pltpu.VMEM(group, BF16),
            pltpu.VMEM((3 * UNITS, GROUP), BF16),
            pltpu.VMEM((sum(SCATTER_ROWS), WIDTH), BF16),
            *pairs(SCATTER_MAILS),
            *pairs(GATHER_MAILS),
            pltpu.SemaphoreType.DMA((16,)),
            pltpu.SemaphoreType.DMA((2,)),
        ],
        compiler_params=params(collective),
        name="feed_forward",
    )(own, gathered, feed)


def attention_back_kernel(
    own,
    weights,
    tables,
    start,
    acts,
    attended,
    logs,
    first_rows,
    outs,
    total,
    out_total,
    shard,
    bias_sum,
    rows,
    before,
    grad_out,
    grads_qkv,
    keys_turned,
    turns,
    parts,
    out_parts,
    grads,
    land,
    out_land,
    w_land,
    w_sum,
    sends,
    receives,
    g_sends,
    g_receives,
    o_sends,
    o_receives,
    w_sends,
    w_receives,
    local,
):
    a, r = Around(), Ring()
    mail, gmail, omail, wmail = (
        Mail(sends, receives),
        Mail(g_sends, g_receives),
        Mail(o_sends, o_receives),
        Mail(w_sends, w_receives),
    )
    keeps = [
        pltpu.make_async_copy(own, rows.at[a.me], local.at[0]),
        pltpu.make_async_copy(first_rows, before, local.at[1]),
        pltpu.make_async_copy(outs, out_parts, local.at[2]),
    ]
    for keep in keeps:
        keep.start()
    greet(a.peers() + r.peers())
    gather = gather_steps(a, gmail, own, rows)
    out_scatter = scatter_steps(a, omail, out_parts, out_total, out_land)
    scatter = scatter_steps(a, mail, parts, total, land)
    blocks = blocks_steps(r, wmail, grads, w_land, w_sum, shard)
    gather[0]()
    keys_turned[...] = acts[1].T
    turns[pl.ds(3 * LOCAL, LOCAL), :] = attended[...].T
    for keep in keeps:
        keep.wait()
    gather[1]()
    gather[2]()
    gather[3]()
    gather[4]()
    gather[5]()
    out_scatter[0]()
    gather[6]()

    def back_project(index, carry):
        chunk = rows[pl.ds(2 * index, 2)].reshape(QBLOCK, WIDTH)
        first = pl.multiple_of(index * QBLOCK, QBLOCK)
        grad_out[pl.ds(first, QBLOCK), :] = dot(chunk, weights[3]).astype(BF16)
        return carry

    lax.fori_loop(0, GROUP // QBLOCK, back_project, 0)

    def attend(first):
        count = first + QBLOCK
        span = pl.ds(first, QBLOCK)
        query = acts[0, span, :] * BF16(SCALE)
        given = grad_out[span, :]
        row = lax.broadcasted_iota(jnp.int32, (count, QBLOCK), 0)
        column = first + lax.broadcasted_iota(jnp.int32, (count, QBLOCK), 1)
        allow = (row <= column) & (row >= start[:, span])
        overlap = given.astype(F32) * attended[span, :].astype(F32)
        lane = lax.broadcasted_iota(jnp.int32, (QBLOCK, LANES), 1)
        inner = jnp.zeros((QBLOCK, LANES), F32)
        for head in range(HEADS_DEV):
            summed = jnp.sum(only(head_lanes(head, QBLOCK), overlap), axis=1, keepdims=True)
            inner = jnp.where(lane == head, summed, inner)
        inner = inner.T[:8]
        head_row = lax.broadcasted_iota(jnp.int32, (8, QBLOCK), 0)
        head_rows = lax.broadcasted_iota(jnp.int32, (LOCAL, count), 0) // HEAD_DIM

        def one_head(head, turned_query):
            mask = head_lanes(head, QBLOCK)
            masked, masked_given = only(mask, query), only(mask, given)
            log = jnp.sum(only(head_row == head, logs[:, span]), axis=0, keepdims=True)
            mean = jnp.sum(only(head_row == head, inner), axis=0, keepdims=True)
            scores = dot_t(acts[1, pl.ds(0, count), :], masked)
            probs = only(allow, jnp.exp(scores - log))
            grad_probs = dot_t(acts[2, pl.ds(0, count), :], masked_given)
            grad_scores = (probs * (grad_probs - mean)).astype(BF16)
            grads_qkv[2, pl.ds(0, count), :] += dot(probs.astype(BF16), masked_given)
            grads_qkv[1, pl.ds(0, count), :] += dot(grad_scores, masked)
            keys = only(head_rows == head, keys_turned[:, pl.ds(0, count)])
            return turned_query + dot(keys, grad_scores)

        turned_query = lax.fori_loop(0, HEADS_DEV, one_head, jnp.zeros((LOCAL, QBLOCK), F32))
        grads_qkv[0, span, :] = turned_query.T * SCALE

    grads_qkv[1] = jnp.zeros((GROUP, LOCAL), F32)
    grads_qkv[2] = jnp.zeros((GROUP, LOCAL), F32)
    attend(0)
    attend(QBLOCK)
    out_scatter[1]()
    attend(2 * QBLOCK)
    out_scatter[2]()
    attend(3 * QBLOCK)

    def input_grad(index, sums):
        first = pl.multiple_of(index * QBLOCK, QBLOCK)
        span = pl.ds(first, QBLOCK)
        back = jnp.zeros((QBLOCK, WIDTH), F32)
        added_sums = []
        for c in range(3):
            pre = grads_qkv[c, span, :]
            if c < 2:
                pre = turned(pre, tables, first, -1.0)
            pre = pre.astype(BF16)
            added_sums.append(jnp.sum(pre.astype(F32), axis=0, keepdims=True))
            back = back + dot_t(pre, weights[c])
            turns[pl.ds(c * LOCAL, LOCAL), span] = pre.T
        parts[pl.ds(2 * index, 2)] = back.astype(BF16).reshape(2, ROWS, WIDTH)
        return sums + jnp.concatenate(added_sums, axis=0)

    bias_sum[...] = lax.fori_loop(
        0, GROUP // QBLOCK, input_grad, jnp.zeros((3, LOCAL), F32)
    )
    scatter[0]()

    def weight_grad(index, carry):
        columns = pl.ds(pl.multiple_of(index * 2 * ROWS, 2 * ROWS), 2 * ROWS)
        three = dot(turns[pl.ds(0, 3 * LOCAL), :], before[:, columns])
        last = dot(turns[pl.ds(3 * LOCAL, LOCAL), :], rows[:, :, columns].reshape(GROUP, 2 * ROWS))
        for side in range(2):
            lanes = slice(side * ROWS, (side + 1) * ROWS)
            grads[2 * index + side, pl.ds(0, 3 * LOCAL), :] = three[:, lanes].astype(BF16)
            grads[2 * index + side, pl.ds(3 * LOCAL, LOCAL), :] = last[:, lanes].astype(BF16)
        return carry

    lax.fori_loop(0, 8, weight_grad, 0)
    blocks[0]()
    out_scatter[3]()
    scatter[1]()
    blocks[1]()
    scatter[2]()
    blocks[2]()
    scatter[3]()
    blocks[3]()
    mail.finish()
    gmail.finish()
    omail.finish()
    wmail.finish()


def attention_backward(own, weights, tables, start, acts, attended, logs, first_rows, outs, collective):
    group = (TENSOR, ROWS, WIDTH)
    block = (4 * LOCAL, ROWS)
    landing = (sum(SCATTER_ROWS), WIDTH)
    return pl.pallas_call(
        attention_back_kernel,
        out_shape=(
            jax.ShapeDtypeStruct((ROWS, WIDTH), F32),
            jax.ShapeDtypeStruct((ROWS, WIDTH), F32),
            jax.ShapeDtypeStruct(block, F32),
            jax.ShapeDtypeStruct((3, LOCAL), F32),
        ),
        in_specs=vmem(7) + anywhere(2),
        out_specs=tuple(vmem(4)),
        scratch_shapes=[
            pltpu.VMEM(group, BF16),
            pltpu.VMEM((GROUP, WIDTH), BF16),
            pltpu.VMEM((GROUP, LOCAL), BF16),
            pltpu.VMEM((3, GROUP, LOCAL), F32),
            pltpu.VMEM((LOCAL, GROUP), BF16),
            pltpu.VMEM((4 * LOCAL, GROUP), BF16),
            pltpu.VMEM(group, BF16),
            pltpu.VMEM(group, BF16),
            pltpu.VMEM((16,) + block, BF16),
            pltpu.VMEM(landing, BF16),
            pltpu.VMEM(landing, BF16),
            pltpu.VMEM((BLOCK_MAILS,) + block, BF16),
            pltpu.VMEM(block, F32),
            *pairs(SCATTER_MAILS),
            *pairs(GATHER_MAILS),
            *pairs(SCATTER_MAILS),
            *pairs(BLOCK_MAILS),
            pltpu.SemaphoreType.DMA((3,)),
        ],
        compiler_params=params(collective),
        name="attention_backward",
    )(own, weights, tables, start, acts, attended, logs, first_rows, outs)


def norm_parts(values, gain, shift):
    centred = values - jnp.mean(values, axis=-1, keepdims=True)
    variance = jnp.mean(centred * centred, axis=-1, keepdims=True)
    rinv = lax.rsqrt(variance + EPS)
    normal = centred * rinv
    return (normal * gain + shift, normal, rinv)


def norm_back(incoming, normal, rinv, gain):
    scaled = incoming * gain
    inner = (
        scaled
        - jnp.mean(scaled, axis=-1, keepdims=True)
        - normal * jnp.mean(scaled * normal, axis=-1, keepdims=True)
    )
    return (rinv * inner, jnp.sum(incoming * normal, axis=0), jnp.sum(incoming, axis=0))


def places(group_ids):
    group = group_ids.shape[0]
    index = jnp.arange(group, dtype=jnp.int32)
    numbers = jnp.arange(DOCS, dtype=jnp.int32)
    before = (group_ids[None, :] >= 0) & (group_ids[None, :] < numbers[:, None])
    starts = jnp.sum(before.astype(jnp.int32), axis=1)
    offset = jnp.sum(jnp.where(group_ids[:, None] == numbers[None, :], starts[None, :], 0), axis=1)
    position = (index - offset).astype(F32)
    freq = jnp.power(10000.0, -2.0 * jnp.arange(ROT // 2, dtype=F32) / ROT)
    angle = position[:, None] * freq[None, :]
    cosine, sine = jnp.cos(angle), jnp.sin(angle)
    rest = HEAD_DIM - ROT
    none = jnp.zeros_like(sine)
    tables = jnp.stack(
        [
            jnp.concatenate([cosine, cosine, jnp.ones((group, rest), F32)], axis=1),
            jnp.concatenate([-sine, none, jnp.zeros((group, rest), F32)], axis=1),
            jnp.concatenate([none, sine, jnp.zeros((group, rest), F32)], axis=1),
        ]
    )
    return jnp.where(group_ids >= 0, offset, index), jnp.tile(tables, (1, 1, 2))


def body(
    tokens,
    doc_ids,
    qkv_weight,
    qkv_bias,
    out_weight,
    norm1_gain,
    norm1_shift,
    norm2_gain,
    norm2_shift,
    gate_up_weight,
    down_weight,
    cotangent,
):
    inputs = tokens.astype(F32)
    normed1, normal1, rinv1 = norm_parts(inputs, norm1_gain, norm1_shift)
    shard = jnp.concatenate([qkv_weight, out_weight.T[None]])
    rows1, id_rows, projections = gather_weights(
        normed1.astype(BF16), jnp.broadcast_to(doc_ids[None], (8, ROWS)), shard, 0
    )
    rows1 = rows1.reshape(GROUP, WIDTH)
    group_ids = jnp.swapaxes(id_rows[:, :, 0], 0, 1).reshape(GROUP)
    start, tables = places(group_ids)
    feed_shard = jnp.concatenate(
        [jnp.swapaxes(gate_up_weight, 1, 2).reshape(2 * UNITS, ROWS), down_weight]
    )
    branch, grad_rows, feed, acts, attended, logs = attention_forward(
        rows1, projections, qkv_bias, tables, start[:, None], cotangent, feed_shard, 1
    )
    mixed = inputs + branch
    normed2, normal2, rinv2 = norm_parts(mixed, norm2_gain, norm2_shift)
    grad_normed2, feed_out, feed_grad = feed_forward(normed2.astype(BF16), grad_rows, feed, 2)
    feed_grad = lax.psum_scatter(feed_grad, "dp", scatter_dimension=0, tiled=False).astype(F32)
    gate_up_shard = jnp.swapaxes(feed_grad[: 2 * UNITS].reshape(2, UNITS, ROWS), 1, 2)
    down_shard = feed_grad[2 * UNITS :]
    back2, gain2_grad, shift2_grad = norm_back(grad_normed2, normal2, rinv2, norm2_gain)
    grad_mixed = cotangent.astype(F32) + back2
    grad_normed1, feed_sum, weight_shard, bias_part = attention_backward(
        grad_mixed.astype(BF16),
        projections,
        tables,
        start[None, :],
        acts,
        attended,
        logs,
        rows1,
        feed_out,
        3,
    )
    layer_out = (mixed + feed_sum).astype(BF16)
    qkv_shard = jnp.swapaxes(weight_shard[: 3 * LOCAL].reshape(3, LOCAL, ROWS), 1, 2)
    out_shard = weight_shard[3 * LOCAL :]
    back1, gain1_grad, shift1_grad = norm_back(grad_normed1, normal1, rinv1, norm1_gain)
    token_grad = (grad_mixed + back1).astype(BF16)
    norms = jnp.concatenate([gain1_grad, shift1_grad, gain2_grad, shift2_grad, bias_part.reshape(-1)])
    sums = sum_all(jnp.pad(norms.reshape(-1, 128), ((0, 2), (0, 0))), 4)
    gain1_sum, shift1_sum, gain2_sum, shift2_sum = sums[:64].reshape(4, WIDTH)
    bias_grad = sums[64:70].reshape(3, LOCAL)
    return (
        layer_out,
        token_grad,
        qkv_shard,
        bias_grad,
        out_shard,
        gain1_sum,
        shift1_sum,
        gain2_sum,
        shift2_sum,
        gate_up_shard,
        down_shard,
    )


def solution(mesh):
    in_specs = (
        P(("dp", "tensor"), None),
        P(("dp", "tensor")),
        P(None, "dp", "tensor"),
        P(None, "tensor"),
        P("tensor", "dp"),
        P(),
        P(),
        P(),
        P(),
        P(None, "dp", "tensor"),
        P("tensor", "dp"),
        P(("dp", "tensor"), None),
    )
    out_specs = (
        P(("dp", "tensor"), None),
        P(("dp", "tensor"), None),
        P(None, "dp", "tensor"),
        P(None, "tensor"),
        P("tensor", "dp"),
        P(),
        P(),
        P(),
        P(),
        P(None, "dp", "tensor"),
        P("tensor", "dp"),
    )
    return jax.shard_map(body, mesh=mesh, in_specs=in_specs, out_specs=out_specs, check_vma=False)
```

```python
import jax
import jax.numpy as jnp
from jax import lax
from jax.experimental import pallas as pl
from jax.experimental.pallas import tpu as pltpu
from jax.sharding import PartitionSpec as P

HEAD_DIM = 64
ROT = 16
DOCS = 4
EPS = 1e-05
SCALE = HEAD_DIM ** (-0.5)

ROWS = 128
WIDTH = 2048
TENSOR = 8
GROUP = ROWS * TENSOR
HALF = ROWS // 2
HEADS_DEV = 4
LOCAL = HEADS_DEV * HEAD_DIM
QBLOCK = 256
UNITS = 704
LANES = 128
MESH = pl.DeviceIdType.MESH
BF16 = jnp.bfloat16
F32 = jnp.float32
VMEM_LIMIT = 62 * 2**20


class Around:
    def __init__(self):
        dp, tensor = lax.axis_index("dp"), lax.axis_index("tensor")
        y, z = tensor // 2, lax.rem(tensor, 2)
        up, down, far = lax.rem(y + 1, 4), lax.rem(y + 3, 4), lax.rem(y + 2, 4)
        other = 1 - z
        self.me, self.across = y * 2 + z, y * 2 + other
        self.up, self.down, self.far = up * 2 + z, down * 2 + z, far * 2 + z
        self.up_o, self.down_o, self.far_o = up * 2 + other, down * 2 + other, far * 2 + other
        self.y, self.z = y, z
        self.y_up, self.y_down, self.y_far = up, down, far
        self.to_up, self.to_down, self.to_across = (dp, self.up), (dp, self.down), (dp, self.across)
        self.to_rest = [(dp, slot) for slot in (self.far, self.up_o, self.down_o, self.far_o)]

    def peers(self):
        return [self.to_up, self.to_down, self.to_across]


class Ring:
    def __init__(self):
        dp, tensor = lax.axis_index("dp"), lax.axis_index("tensor")
        zh, x, core = dp // 8, lax.rem(dp // 2, 4), lax.rem(dp, 2)
        self.zh, self.x, self.core, self.dp, self.tensor = zh, x, core, dp, tensor
        self.xs = [lax.rem(x + step, 4) for step in range(4)]
        self.to_x = [(self.index(zh, self.xs[step], core), tensor) for step in range(4)]
        self.to_zh = (self.index(1 - zh, x, core), tensor)
        self.to_core = (self.index(zh, x, 1 - core), tensor)
        self.to_zh_core = (self.index(1 - zh, x, 1 - core), tensor)

    def index(self, zh, x, core):
        return zh * 8 + x * 2 + core

    def peers(self):
        return self.to_x[1:] + [self.to_zh, self.to_core]


def hail(peers):
    barrier = pltpu.get_barrier_semaphore()
    for peer in peers:
        pl.semaphore_signal(barrier, inc=1, device_id=peer, device_id_type=MESH)


def hear(peers):
    pl.semaphore_wait(pltpu.get_barrier_semaphore(), len(peers))


class Mail:
    def __init__(self, sends, receives):
        self.sends, self.receives = sends, receives
        self.out = []

    def copy(self, number, source, target, device):
        return pltpu.make_async_remote_copy(
            src_ref=source,
            dst_ref=target,
            send_sem=self.sends.at[number],
            recv_sem=self.receives.at[number],
            device_id=device,
            device_id_type=MESH,
        )

    def send(self, number, source, target, device):
        copy = self.copy(number, source, target, device)
        copy.start()
        self.out.append(copy)

    def landed(self, number, target, device):
        self.copy(number, target, target, device).wait_recv()

    def finish(self):
        for copy in self.out:
            copy.wait_send()
        self.out = []


MIDDLE = {48: 96, 32: 80}
GATHER_MAILS = 15


def gather_steps(around, mail, rows, top):
    a, middle = around, MIDDLE[top]

    def part(slot, first, last):
        return rows.at[slot, pl.ds(first, last - first)]

    def send(number, slot, first, last, device):
        mail.send(number, part(slot, first, last), part(slot, first, last), device)

    def got(number, slot, first, last):
        mail.landed(number, part(slot, first, last), a.to_up)

    def begin():
        send(0, a.me, 0, HALF, a.to_up)
        send(1, a.me, HALF, ROWS, a.to_down)
        send(2, a.me, top, ROWS, a.to_across)
        send(3, a.me, HALF, ROWS, a.to_up)
        send(4, a.me, 0, HALF, a.to_down)
        send(5, a.me, 0, top, a.to_across)

    def one():
        got(0, a.down, 0, HALF)
        send(6, a.down, 0, HALF, a.to_up)
        send(7, a.down, 0, top, a.to_across)
        got(1, a.up, HALF, ROWS)
        send(8, a.up, HALF, ROWS, a.to_down)
        got(2, a.across, top, ROWS)
        send(9, a.across, top, ROWS, a.to_up)
        send(10, a.across, top, ROWS, a.to_down)

    def two():
        got(4, a.up, 0, HALF)
        send(11, a.up, 0, top, a.to_across)
        got(3, a.down, HALF, ROWS)
        got(5, a.across, 0, top)

    def three():
        got(6, a.far, 0, HALF)
        send(12, a.far, 0, top, a.to_across)
        got(8, a.far, HALF, ROWS)

    def four():
        got(9, a.down_o, top, ROWS)
        send(13, a.down_o, top, middle, a.to_up)
        got(10, a.up_o, top, ROWS)
        send(14, a.up_o, middle, ROWS, a.to_down)

    def five():
        got(7, a.down_o, 0, top)
        got(11, a.up_o, 0, top)

    def six():
        got(13, a.far_o, top, middle)
        got(14, a.far_o, middle, ROWS)
        got(12, a.far_o, 0, top)

    return begin, one, two, three, four, five, six


def added(*terms):
    total = terms[0].astype(F32)
    for term in terms[1:]:
        total = total + term.astype(F32)
    return total


SCATTER_MAILS = 20


def scatter_boxes(top):
    middle = MIDDLE[top]
    last, inner, rest = ROWS - middle, middle - top, HALF - top
    counts = (last, inner, top, HALF, top, top, last, inner, HALF, top)
    counts += (top, inner, last, HALF, top, top, ROWS - top, rest, rest, rest, ROWS - top)
    return counts, tuple(sum(counts[:k]) for k in range(len(counts)))


def scatter_rows_needed(top):
    return sum(scatter_boxes(top)[0])


class Scatter:
    def __init__(self, around, mail, parts, land, top):
        self.a, self.mail, self.parts, self.land, self.top = around, mail, parts, land, top
        self.middle = MIDDLE[top]
        self.counts, self.firsts = scatter_boxes(top)

    def part(self, slot, first, last):
        return self.parts.at[slot, pl.ds(first, last - first)]

    def box(self, number):
        return self.land.at[pl.ds(self.firsts[number], self.counts[number])]

    def direct(self, number, slot, first, device):
        source = self.part(slot, first, first + self.counts[number])
        self.mail.send(number, source, self.box(number), device)

    def got(self, number):
        self.mail.landed(number, self.box(number), self.a.to_up)

    def fold(self, stage, slot, first, *others):
        terms = [self.part(slot, first, first + self.counts[stage])[...], self.box(stage)[...]]
        terms += [self.box(other)[...] for other in others]
        self.box(stage)[...] = added(*terms).astype(BF16)

    def from_far_o(self):
        a = self.a
        self.direct(0, a.far_o, self.middle, a.to_up)
        self.direct(1, a.far_o, self.top, a.to_down)
        self.direct(2, a.far_o, 0, a.to_across)

    def from_far(self):
        a = self.a
        self.direct(3, a.far, HALF, a.to_up)
        self.direct(17, a.far, self.top, a.to_down)

    def from_up_o(self):
        a = self.a
        self.direct(4, a.up_o, 0, a.to_across)
        self.direct(7, a.up_o, self.top, a.to_up)

    def from_down_o(self):
        a = self.a
        self.direct(5, a.down_o, 0, a.to_across)
        self.direct(6, a.down_o, self.middle, a.to_down)

    def from_up(self):
        self.direct(18, self.a.up, self.top, self.a.to_up)

    def from_down(self):
        self.direct(8, self.a.down, HALF, self.a.to_down)

    def from_across(self):
        self.direct(9, self.a.across, 0, self.a.to_across)

    def one(self):
        a, send, box = self.a, self.mail.send, self.box
        self.got(1)
        self.fold(1, a.down_o, self.top)
        send(11, box(1), box(11), a.to_down)
        self.got(0)
        self.fold(0, a.up_o, self.middle)
        send(12, box(0), box(12), a.to_up)
        self.got(2)
        self.fold(2, a.far, 0)
        send(10, box(2), box(10), a.to_down)
        self.got(3)
        self.fold(3, a.up, HALF)
        send(13, box(3), box(13), a.to_up)

    def two(self):
        a, send, box = self.a, self.mail.send, self.box
        self.got(17)
        self.fold(17, a.down, self.top)
        send(19, box(17), box(19), a.to_down)
        self.got(4)
        self.fold(4, a.up, 0)
        send(14, box(4), box(14), a.to_up)
        for number in (6, 7, 11, 12):
            self.got(number)
        inner, last = self.middle - self.top, ROWS - self.middle
        made = self.firsts[20]
        self.land[pl.ds(made, inner), :] = added(
            self.part(a.across, self.top, self.middle)[...], box(7)[...], box(11)[...]
        ).astype(BF16)
        self.land[pl.ds(made + inner, last), :] = added(
            self.part(a.across, self.middle, ROWS)[...], box(6)[...], box(12)[...]
        ).astype(BF16)
        send(16, box(20), box(16), a.to_across)
        self.got(5)
        self.got(10)
        self.fold(5, a.down, 0, 10)
        send(15, box(5), box(15), a.to_down)

    def three(self, total):
        a, top = self.a, self.top
        for number in (8, 9, 13, 14, 18, 19, 16, 15):
            self.got(number)

        def boxed(number, first, last):
            return self.land[pl.ds(self.firsts[number] + first, last - first), :]

        total[pl.ds(0, top), :] = added(
            self.part(a.me, 0, top)[...], *(self.box(k)[...] for k in (9, 14, 15))
        )
        total[pl.ds(top, HALF - top), :] = added(
            self.part(a.me, top, HALF)[...],
            self.box(18)[...],
            self.box(19)[...],
            boxed(16, 0, HALF - top),
        )
        total[pl.ds(HALF, HALF), :] = added(
            self.part(a.me, HALF, ROWS)[...],
            self.box(8)[...],
            self.box(13)[...],
            boxed(16, HALF - top, ROWS - top),
        )


def spread_steps(ring, mail, block):
    r = ring

    def share(number, zh, x, device):
        mail.send(number, block(zh, x, r.core), block(zh, x, r.core), device)

    def came(number, zh, x, core):
        mail.landed(number, block(zh, x, core), r.to_core)

    def begin():
        share(0, r.zh, r.x, r.to_zh)
        for step in (1, 3, 2):
            share(step, r.zh, r.x, r.to_x[step])
        share(7, r.zh, r.x, r.to_core)

    def one():
        came(0, 1 - r.zh, r.x, r.core)
        for step in (1, 3, 2):
            share(3 + step, 1 - r.zh, r.x, r.to_x[step])
        share(8, 1 - r.zh, r.x, r.to_core)

    def two():
        for step in (1, 3, 2):
            came(step, r.zh, r.xs[4 - step], r.core)
            share(8 + step, r.zh, r.xs[4 - step], r.to_core)

    def three():
        for step in (1, 3, 2):
            came(3 + step, 1 - r.zh, r.xs[4 - step], r.core)
            share(11 + step, 1 - r.zh, r.xs[4 - step], r.to_core)

    def four():
        sibling = 1 - r.core
        came(7, r.zh, r.x, sibling)
        came(8, 1 - r.zh, r.x, sibling)
        for step in (1, 3, 2):
            came(8 + step, r.zh, r.xs[4 - step], sibling)
            came(11 + step, 1 - r.zh, r.xs[4 - step], sibling)

    return begin, one, two, three, four


SPREAD_MAILS = 15
FOLDS = [(side, step) for step in (1, 3, 2, 0) for side in (1, 0)]


class Fold:
    def __init__(self, ring, mail, grads, own, land):
        self.r, self.mail, self.grads, self.own, self.land = ring, mail, grads, own, land

    def place(self, side, step):
        zh = 1 - self.r.zh if side else self.r.zh
        return zh * 4 + self.r.xs[step]

    def send(self, number):
        side, step = FOLDS[number]
        source = self.grads.at[self.place(side, step)]
        self.mail.send(number, source, self.land.at[number], self.r.to_x[step])

    def cross(self):
        for number in (0, 2, 4):
            self.mail.landed(number, self.land.at[number], self.r.to_core)
        self.land[0] = added(self.own(1), self.land[0], self.land[2], self.land[4]).astype(BF16)
        self.mail.send(6, self.land.at[0], self.land.at[6], self.r.to_zh)

    def near(self):
        for number in (1, 3, 5):
            self.mail.landed(number, self.land.at[number], self.r.to_core)

    def result(self):
        self.mail.landed(6, self.land.at[6], self.r.to_core)
        land = self.land
        return added(self.own(0), land[1], land[3], land[5], land[6])


FOLD_MAILS = 7

SUM_ROWS, SUM_NORMS = 72, 64
SUM_BOXES, SUM_MAILS = 14, 13


def sum_everywhere(a, r, mail, boxes, values):
    def stage(base, count, mine, sources, peers):
        view = pl.ds(0, count)
        for number, peer in enumerate(peers):
            mail.send(base + number, boxes.at[base + mine, view], boxes.at[base + mine, view], peer)
        for number, source in enumerate(sources):
            mail.landed(base + number, boxes.at[base + source, view], peers[0])
        result = boxes[base, view]
        for k in range(1, len(peers) + 1):
            result = result + boxes[base + k, view]
        return result

    boxes[r.x] = values
    first = stage(0, SUM_ROWS, r.x, [r.xs[3], r.xs[2], r.xs[1]], r.to_x[1:])
    place = r.zh * 2 + r.core
    boxes[4 + place] = first
    second = stage(
        4,
        SUM_ROWS,
        place,
        [(1 - r.zh) * 2 + r.core, r.zh * 2 + 1 - r.core, (1 - r.zh) * 2 + 1 - r.core],
        [r.to_zh, r.to_core, r.to_zh_core],
    )
    boxes[8 + a.y, pl.ds(0, SUM_NORMS)] = second[:SUM_NORMS]
    y_peers = [a.to_up, a.to_rest[0], a.to_down]
    third = stage(8, SUM_NORMS, a.y, [a.y_down, a.y_far, a.y_up], y_peers)
    boxes[12 + a.z, pl.ds(0, SUM_NORMS)] = third
    fourth = stage(12, SUM_NORMS, a.z, [1 - a.z], [a.to_across])
    return jnp.concatenate([fourth, second[SUM_NORMS:]], axis=0)


def dot(left, right):
    return lax.dot_general(left, right, (((1,), (0,)), ((), ())), preferred_element_type=F32)


def dot_t(left, right):
    return lax.dot_general(left, right, (((1,), (1,)), ((), ())), preferred_element_type=F32)


def normalized(values):
    centred = values - jnp.mean(values, axis=1, keepdims=True)
    variance = jnp.mean(centred * centred, axis=1, keepdims=True)
    rinv = lax.rsqrt(variance + EPS)
    return centred * rinv, rinv


def norm_back(incoming, normal, rinv, gain):
    scaled = incoming * gain
    inner = scaled - jnp.mean(scaled, axis=1, keepdims=True)
    inner = inner - normal * jnp.mean(scaled * normal, axis=1, keepdims=True)
    gain_grad = jnp.sum(incoming * normal, axis=0, keepdims=True)
    return rinv * inner, gain_grad, jnp.sum(incoming, axis=0, keepdims=True)


def turned(values, tables, first, sign):
    rows = pl.ds(first, values.shape[0])
    cosine, minus, plus = tables[0, rows], tables[1, rows], tables[2, rows]
    halves = []
    for lane in range(0, LOCAL, LANES):
        part = values[:, lane : lane + LANES]
        left = pltpu.roll(part, LANES - ROT // 2, 1)
        right = pltpu.roll(part, ROT // 2, 1)
        halves.append(part * cosine + sign * (left * minus + right * plus))
    return jnp.concatenate(halves, axis=1)


def head_lanes(head, rows):
    return lax.broadcasted_iota(jnp.int32, (rows, LOCAL), 1) // HEAD_DIM == head


def only(mask, values):
    return jnp.where(mask, values, jnp.zeros_like(values))


def place_rows(id_rows, frequency, tables, start_rows, start_lanes):
    ids = jnp.max(id_rows[...], axis=1)
    shape = (TENSOR, ROWS)
    index = lax.broadcasted_iota(jnp.int32, shape, 0) * ROWS
    index = (index + lax.broadcasted_iota(jnp.int32, shape, 1)).astype(F32)
    offset = jnp.zeros(shape, F32)
    for number in range(1, DOCS):
        before = ((ids >= 0) & (ids < number)).astype(F32)
        count = jnp.sum(jnp.sum(before, axis=1, keepdims=True), axis=0, keepdims=True)
        offset = jnp.where(ids == number, count, offset)
    start = jnp.where(ids >= 0, offset, index)
    position = index - offset

    def along(values):
        return jnp.concatenate([values[t : t + 1] for t in range(TENSOR)], axis=1)

    angle = frequency[:, :1] * along(position)
    cosine, sine = jnp.cos(angle), jnp.sin(angle)
    none = jnp.zeros_like(sine)
    rest = (HEAD_DIM - ROT) // 8
    columns = (
        [cosine, cosine] + [jnp.ones_like(sine)] * rest,
        [-sine, none] + [none] * rest,
        [none, sine] + [none] * rest,
    )
    for number, parts in enumerate(columns):
        tables[number] = jnp.concatenate(parts + parts, axis=0).T
    lanes = jnp.broadcast_to(along(start), (8, GROUP))
    start_lanes[...] = lanes
    start_rows[...] = jnp.concatenate([lanes] * (LANES // 8), axis=0).T


def vmem(count):
    return [pl.BlockSpec(memory_space=pltpu.VMEM)] * count


def anywhere(count):
    return [pl.BlockSpec(memory_space=pl.ANY)] * count


def pairs(count):
    return [pltpu.SemaphoreType.DMA((count,)), pltpu.SemaphoreType.DMA((count,))]


def params(collective):
    return pltpu.CompilerParams(
        collective_id=collective, has_side_effects=True, vmem_limit_bytes=VMEM_LIMIT
    )


TOP_ROWS, TOP_COTS, TOP_BRANCH = 48, 32, 48


def attention_kernel(
    tokens,
    ids,
    bias,
    out_shard,
    gain1,
    shift1,
    gain2,
    shift2,
    frequency,
    qkv_shard,
    gate_up,
    down,
    own_cots,
    normed2,
    mixed,
    tables,
    start_lanes,
    acts,
    attended,
    logs,
    rows_kept,
    weights_kept,
    cots,
    feed,
    rows,
    weights,
    id_rows,
    start_rows,
    parts,
    land,
    total,
    r_sends,
    r_receives,
    c_sends,
    c_receives,
    b_sends,
    b_receives,
    w_sends,
    w_receives,
    f_sends,
    f_receives,
    i_sends,
    i_receives,
    local,
):
    a, r = Around(), Ring()
    rmail, cmail, bmail = Mail(r_sends, r_receives), Mail(c_sends, c_receives), Mail(b_sends, b_receives)
    wmail, fmail, imail = Mail(w_sends, w_receives), Mail(f_sends, f_receives), Mail(i_sends, i_receives)
    peers = a.peers() + a.to_rest + r.peers()
    hail(peers)

    def weight_block(zh, x, core):
        first = pl.multiple_of(r.index(zh, x, core) * ROWS, ROWS)
        return weights.at[:, pl.ds(first, ROWS), :]

    def feed_block(zh, x, core):
        return feed.at[r.index(zh, x, core)]

    mine = pl.multiple_of(r.dp * ROWS, ROWS)
    copies = [
        pltpu.make_async_copy(qkv_shard, weights.at[pl.ds(0, 3), pl.ds(mine, ROWS)], local.at[0]),
        pltpu.make_async_copy(gate_up, feed.at[r.dp, pl.ds(0, 2 * UNITS)], local.at[1]),
        pltpu.make_async_copy(down, feed.at[r.dp, pl.ds(2 * UNITS, UNITS)], local.at[2]),
        pltpu.make_async_copy(own_cots, cots.at[a.me], local.at[3]),
    ]
    for copy in copies:
        copy.start()
    id_rows[a.me] = jnp.broadcast_to(ids[...], (8, ROWS))
    weights[3, pl.ds(mine, ROWS), :] = out_shard[...].T
    normal, _ = normalized(tokens[...].astype(F32))
    rows[a.me] = (normal * gain1[...] + shift1[...]).astype(BF16)
    hear(peers)

    group = [
        (0, a.to_up, a.down),
        (1, a.to_down, a.up),
        (2, a.to_across, a.across),
        (3, a.to_rest[0], a.far),
        (4, a.to_rest[1], a.down_o),
        (5, a.to_rest[2], a.up_o),
        (6, a.to_rest[3], a.far_o),
    ]
    for number, device, _ in group:
        imail.send(number, id_rows.at[a.me], id_rows.at[a.me], device)
    gather = gather_steps(a, rmail, rows, TOP_ROWS)
    others = gather_steps(a, cmail, cots, TOP_COTS)
    spread = spread_steps(r, wmail, weight_block)
    feeds = spread_steps(r, fmail, feed_block)
    scatter = Scatter(a, bmail, parts, land, TOP_BRANCH)
    gather[0]()
    for copy in copies:
        copy.wait()
    spread[0]()
    for number, _, slot in group:
        imail.landed(number, id_rows.at[slot], a.to_up)
    place_rows(id_rows, frequency, tables, start_rows, start_lanes)
    spread[1]()
    gather[1]()
    gather[2]()
    spread[2]()
    spread[3]()
    gather[3]()
    feeds[0]()
    gather[4]()
    others[0]()
    spread[4]()

    def project(y):
        first = pl.multiple_of(y * QBLOCK, QBLOCK)
        chunk = rows[pl.ds(2 * y, 2)].reshape(QBLOCK, WIDTH)
        for c in range(3):
            pre = dot(chunk, weights[c]) + bias[pl.ds(c, 1), :]
            if c < 2:
                pre = turned(pre, tables, first, 1.0)
            acts[c, pl.ds(first, QBLOCK), :] = pre.astype(BF16)

    project(a.y)
    gather[5]()
    project(a.y_down)
    project(a.y_up)
    gather[6]()
    project(a.y_far)
    keeps = [
        pltpu.make_async_copy(rows, rows_kept, local.at[4]),
        pltpu.make_async_copy(weights, weights_kept, local.at[5]),
    ]
    for keep in keeps:
        keep.start()

    def attend(first):
        count = first + QBLOCK
        query = acts[0, pl.ds(first, QBLOCK), :] * BF16(SCALE)
        row = first + lax.broadcasted_iota(jnp.int32, (QBLOCK, count), 0)
        column = lax.broadcasted_iota(jnp.int32, (QBLOCK, count), 1)
        start = start_rows[pl.ds(first, QBLOCK), pl.ds(0, 1)]
        allow = (column <= row) & (column.astype(F32) >= start)
        lane = lax.broadcasted_iota(jnp.int32, (QBLOCK, LANES), 1)

        def one_head(head, carry):
            out, log = carry
            masked = only(head_lanes(head, QBLOCK), query)
            scores = dot_t(masked, acts[1, pl.ds(0, count), :])
            scores = jnp.where(allow, scores, -1e30)
            highest = jnp.max(scores, axis=1, keepdims=True)
            expon = jnp.exp(scores - highest)
            sums = jnp.sum(expon, axis=1, keepdims=True)
            values = only(head_lanes(head, count), acts[2, pl.ds(0, count), :])
            out = out + dot(expon.astype(BF16), values) / sums
            log = jnp.where(lane == head, highest + jnp.log(sums), log)
            return out, log

        out, log = lax.fori_loop(
            0,
            HEADS_DEV,
            one_head,
            (jnp.zeros((QBLOCK, LOCAL), F32), jnp.zeros((QBLOCK, LANES), F32)),
        )
        out = out.astype(BF16)
        attended[pl.ds(first, QBLOCK), :] = out
        logs[:, pl.ds(first, QBLOCK)] = log.T[:8]
        branch = dot_t(out, weights[3]).astype(BF16)
        parts[first // ROWS] = branch[:ROWS]
        parts[first // ROWS + 1] = branch[ROWS:]

    attend(0)
    others[1]()
    attend(QBLOCK)
    others[2]()
    attend(2 * QBLOCK)
    others[3]()
    feeds[1]()
    attend(3 * QBLOCK)
    scatter.from_far_o()
    scatter.from_far()
    scatter.from_up_o()
    scatter.from_down_o()
    scatter.from_up()
    scatter.from_down()
    scatter.from_across()
    others[4]()
    feeds[2]()
    scatter.one()
    scatter.two()
    feeds[3]()
    others[5]()
    others[6]()
    scatter.three(total)
    after = tokens[...].astype(F32) + total[...]
    mixed[...] = after
    normal, _ = normalized(after)
    normed2[...] = (normal * gain2[...] + shift2[...]).astype(BF16)
    feeds[4]()
    for mail in (rmail, cmail, bmail, wmail, fmail, imail):
        mail.finish()
    for keep in keeps:
        keep.wait()


def attention_forward(tokens, ids, bias, out_shard, norms, frequency, qkv_shard, gate_up, down, cots):
    group = (TENSOR, ROWS, WIDTH)
    weights = (4, WIDTH, LOCAL)
    return pl.pallas_call(
        attention_kernel,
        out_shape=(
            jax.ShapeDtypeStruct((ROWS, WIDTH), BF16),
            jax.ShapeDtypeStruct((ROWS, WIDTH), F32),
            jax.ShapeDtypeStruct((3, GROUP, LANES), F32),
            jax.ShapeDtypeStruct((8, GROUP), F32),
            jax.ShapeDtypeStruct((3, GROUP, LOCAL), BF16),
            jax.ShapeDtypeStruct((GROUP, LOCAL), BF16),
            jax.ShapeDtypeStruct((8, GROUP), F32),
            jax.ShapeDtypeStruct(group, BF16),
            jax.ShapeDtypeStruct(weights, BF16),
            jax.ShapeDtypeStruct(group, BF16),
            jax.ShapeDtypeStruct((16, 3 * UNITS, ROWS), BF16),
        ),
        in_specs=vmem(9) + anywhere(4),
        out_specs=tuple(vmem(7) + anywhere(4)),
        scratch_shapes=[
            pltpu.VMEM(group, BF16),
            pltpu.VMEM(weights, BF16),
            pltpu.VMEM((TENSOR, 8, ROWS), jnp.int32),
            pltpu.VMEM((GROUP, LANES), F32),
            pltpu.VMEM(group, BF16),
            pltpu.VMEM((scatter_rows_needed(TOP_BRANCH), WIDTH), BF16),
            pltpu.VMEM((ROWS, WIDTH), F32),
            *pairs(GATHER_MAILS),
            *pairs(GATHER_MAILS),
            *pairs(SCATTER_MAILS),
            *pairs(SPREAD_MAILS),
            *pairs(SPREAD_MAILS),
            *pairs(7),
            pltpu.SemaphoreType.DMA((6,)),
        ],
        compiler_params=params(0),
        name="attention_forward",
    )(tokens, ids, bias, out_shard, *norms, frequency, qkv_shard, gate_up, down, cots)


TOP_FEED = 48


def feed_kernel(
    own,
    mixed,
    own_cots,
    gain2,
    cots_in,
    feed,
    grad_mixed,
    branch_grad,
    norm_grads,
    halves,
    outs_kept,
    rows,
    cots,
    weights,
    parts,
    outs,
    acts,
    grads,
    land,
    core_land,
    total,
    g_sends,
    g_receives,
    s_sends,
    s_receives,
    w_sends,
    w_receives,
    w_local,
    local,
):
    a, r = Around(), Ring()
    gmail, mail, wmail = Mail(g_sends, g_receives), Mail(s_sends, s_receives), Mail(w_sends, w_receives)
    peers = a.peers() + [r.to_core]
    hail(peers)
    loads = [
        pltpu.make_async_copy(feed.at[n], weights.at[:, pl.ds(n * ROWS, ROWS)], w_local.at[n])
        for n in range(16)
    ]
    keep = pltpu.make_async_copy(cots_in, cots, local.at[0])
    for copy in loads + [keep]:
        copy.start()
    rows[a.me] = own[...]
    hear(peers)
    gather = gather_steps(a, gmail, rows, TOP_FEED)
    scatter = Scatter(a, mail, parts, land, TOP_FEED)
    gather[0]()
    for copy in loads + [keep]:
        copy.wait()

    def pair(*slots):
        x = jnp.concatenate([rows[slot] for slot in slots], axis=0)
        given = jnp.concatenate([cots[slot] for slot in slots], axis=0)
        gate = dot_t(x, weights[pl.ds(0, UNITS), :])
        upward = dot_t(x, weights[pl.ds(UNITS, UNITS), :])
        grad_hidden = dot_t(given, weights[pl.ds(2 * UNITS, UNITS), :])
        sigma = jax.nn.sigmoid(gate)
        silu = gate * sigma
        hidden = (silu * upward).astype(BF16)
        grad_gate = (grad_hidden * upward * (sigma + silu * (1.0 - sigma))).astype(BF16)
        grad_up = (grad_hidden * silu).astype(BF16)
        back = dot(grad_gate, weights[pl.ds(0, UNITS), :])
        back = (back + dot(grad_up, weights[pl.ds(UNITS, UNITS), :])).astype(BF16)
        for number, slot in enumerate(slots):
            parts[slot] = back[number * ROWS : (number + 1) * ROWS]
        return hidden, grad_gate, grad_up

    def rest(kept, *slots):
        hidden, grad_gate, grad_up = kept
        out = dot(hidden, weights[pl.ds(2 * UNITS, UNITS), :]).astype(BF16)
        for number, slot in enumerate(slots):
            chunk = slice(number * ROWS, (number + 1) * ROWS)
            outs[slot] = out[chunk]
            lanes = pl.ds(pl.multiple_of(slot * ROWS, ROWS), ROWS)
            acts[pl.ds(0, UNITS), lanes] = grad_gate[chunk].T
            acts[pl.ds(UNITS, UNITS), lanes] = grad_up[chunk].T
            acts[pl.ds(2 * UNITS, UNITS), lanes] = hidden[chunk].T

    gather[1]()
    gather[2]()
    rest(pair(a.me, a.across), a.me, a.across)
    gather[3]()
    kept = pair(a.down, a.up)
    gather[4]()
    rest(kept, a.down, a.up)
    gather[5]()
    scatter.from_across()
    scatter.from_up()
    scatter.from_down()
    kept = pair(a.far, a.down_o)
    scatter.from_far()
    scatter.from_down_o()
    gather[6]()
    last = pair(a.far_o, a.up_o)
    scatter.from_far_o()
    scatter.from_up_o()
    rest(kept, a.far, a.down_o)
    rest(last, a.far_o, a.up_o)
    outs_copy = pltpu.make_async_copy(outs, outs_kept, local.at[1])
    outs_copy.start()
    scatter.one()

    def to_sibling(index):
        return wmail.copy(index, grads.at[index, 1 - r.core], core_land.at[index], r.to_core)

    def weight_grad(index, carry):
        columns = pl.ds(pl.multiple_of(index * 2 * ROWS, 2 * ROWS), 2 * ROWS)
        both = dot(acts[pl.ds(0, 2 * UNITS), :], rows[:, :, columns].reshape(GROUP, 2 * ROWS))
        low = dot(acts[pl.ds(2 * UNITS, UNITS), :], cots[:, :, columns].reshape(GROUP, 2 * ROWS))
        for core in range(2):
            lanes = slice(core * ROWS, (core + 1) * ROWS)
            grads[index, core, pl.ds(0, 2 * UNITS), :] = both[:, lanes].astype(BF16)
            grads[index, core, pl.ds(2 * UNITS, UNITS), :] = low[:, lanes].astype(BF16)
        to_sibling(index).start()
        return carry

    def core_sum(index, carry):
        to_sibling(index).wait()
        core_land[index] = added(grads[index, r.core], core_land[index]).astype(BF16)
        return carry

    lax.fori_loop(0, 4, weight_grad, 0)
    scatter.two()
    lax.fori_loop(4, 8, weight_grad, 0)
    lax.fori_loop(0, 8, core_sum, 0)
    halves_copy = pltpu.make_async_copy(core_land, halves, local.at[2])
    halves_copy.start()
    scatter.three(total)
    normal, rinv = normalized(mixed[...])
    back, gain_grad, shift_grad = norm_back(total[...], normal, rinv, gain2[...])
    back = own_cots[...].astype(F32) + back
    grad_mixed[...] = back
    branch_grad[...] = back.astype(BF16)
    norm_grads[...] = jnp.concatenate([gain_grad, shift_grad], axis=0)
    gmail.finish()
    mail.finish()
    outs_copy.wait()
    halves_copy.wait()


def feed_forward(own, mixed, own_cots, gain2, cots, feed):
    group = (TENSOR, ROWS, WIDTH)
    blocks = (8, 3 * UNITS, ROWS)
    return pl.pallas_call(
        feed_kernel,
        out_shape=(
            jax.ShapeDtypeStruct((ROWS, WIDTH), F32),
            jax.ShapeDtypeStruct((ROWS, WIDTH), BF16),
            jax.ShapeDtypeStruct((2, WIDTH), F32),
            jax.ShapeDtypeStruct(blocks, BF16),
            jax.ShapeDtypeStruct(group, BF16),
        ),
        in_specs=vmem(4) + anywhere(2),
        out_specs=tuple(vmem(3) + anywhere(2)),
        scratch_shapes=[
            pltpu.VMEM(group, BF16),
            pltpu.VMEM(group, BF16),
            pltpu.VMEM((3 * UNITS, WIDTH), BF16),
            pltpu.VMEM(group, BF16),
            pltpu.VMEM(group, BF16),
            pltpu.VMEM((3 * UNITS, GROUP), BF16),
            pltpu.VMEM((8, 2, 3 * UNITS, ROWS), BF16),
            pltpu.VMEM((scatter_rows_needed(TOP_FEED), WIDTH), BF16),
            pltpu.VMEM(blocks, BF16),
            pltpu.VMEM((ROWS, WIDTH), F32),
            *pairs(GATHER_MAILS),
            *pairs(SCATTER_MAILS),
            *pairs(8),
            pltpu.SemaphoreType.DMA((16,)),
            pltpu.SemaphoreType.DMA((3,)),
        ],
        compiler_params=params(1),
        name="feed_forward",
    )(own, mixed, own_cots, gain2, cots, feed)


TOP_GRADS, TOP_OUTS, TOP_BACK = 48, 32, 48


def attention_back_kernel(
    own,
    grad_mixed,
    mixed,
    tokens,
    gain1,
    norm2_grads,
    tables,
    start_lanes,
    acts,
    attended,
    logs,
    weights,
    halves,
    first_rows,
    outs,
    layer_out,
    token_grad,
    qkv_grad,
    out_grad,
    gate_up_grad,
    down_grad,
    sums,
    rows,
    before,
    grad_out,
    grads_qkv,
    keys_turned,
    turns,
    parts,
    out_parts,
    grads,
    land,
    out_land,
    core_land,
    w_land,
    f_land,
    own_halves,
    total,
    boxes,
    g_sends,
    g_receives,
    s_sends,
    s_receives,
    o_sends,
    o_receives,
    k_sends,
    k_receives,
    w_sends,
    w_receives,
    f_sends,
    f_receives,
    a_sends,
    a_receives,
    local,
):
    a, r = Around(), Ring()
    gmail, mail, omail = Mail(g_sends, g_receives), Mail(s_sends, s_receives), Mail(o_sends, o_receives)
    kmail, wmail, fmail = Mail(k_sends, k_receives), Mail(w_sends, w_receives), Mail(f_sends, f_receives)
    amail = Mail(a_sends, a_receives)
    peers = a.peers() + a.to_rest[:1] + r.peers() + [r.to_zh_core]
    hail(peers)
    loads = [
        pltpu.make_async_copy(first_rows, before, local.at[0]),
        pltpu.make_async_copy(outs, out_parts, local.at[1]),
        pltpu.make_async_copy(halves.at[r.zh * 4 + r.x], own_halves.at[0], local.at[2]),
        pltpu.make_async_copy(halves.at[(1 - r.zh) * 4 + r.x], own_halves.at[1], local.at[3]),
    ]
    for copy in loads:
        copy.start()
    rows[a.me] = own[...]
    hear(peers)
    gather = gather_steps(a, gmail, rows, TOP_GRADS)
    out_scatter = Scatter(a, omail, out_parts, out_land, TOP_OUTS)
    scatter = Scatter(a, mail, parts, land, TOP_BACK)
    feed_fold = Fold(r, fmail, halves, lambda side: own_halves[side], f_land)
    fold = Fold(r, wmail, core_land, lambda side: core_land[fold.place(side, 0)], w_land)
    gather[0]()
    for number in range(6):
        feed_fold.send(number)
    keys_turned[...] = acts[1].T
    turns[pl.ds(3 * LOCAL, LOCAL), :] = attended[...].T
    for copy in loads:
        copy.wait()
    gather[1]()
    gather[2]()
    gather[3]()
    gather[4]()

    def back_project(y):
        chunk = rows[pl.ds(2 * y, 2)].reshape(QBLOCK, WIDTH)
        first = pl.multiple_of(y * QBLOCK, QBLOCK)
        grad_out[pl.ds(first, QBLOCK), :] = dot(chunk, weights[3]).astype(BF16)

    out_scatter.from_far_o()
    out_scatter.from_far()
    out_scatter.from_up_o()
    out_scatter.from_down_o()
    out_scatter.from_up()
    out_scatter.from_down()
    out_scatter.from_across()
    back_project(a.y)
    gather[5]()
    back_project(a.y_up)
    back_project(a.y_down)
    gather[6]()
    back_project(a.y_far)

    def attend(first):
        count = first + QBLOCK
        span = pl.ds(first, QBLOCK)
        query = acts[0, span, :] * BF16(SCALE)
        given = grad_out[span, :]
        row = lax.broadcasted_iota(jnp.int32, (count, QBLOCK), 0)
        column = first + lax.broadcasted_iota(jnp.int32, (count, QBLOCK), 1)
        allow = (row <= column) & (row.astype(F32) >= start_lanes[pl.ds(0, 1), span])
        overlap = given.astype(F32) * attended[span, :].astype(F32)
        lane = lax.broadcasted_iota(jnp.int32, (QBLOCK, LANES), 1)
        inner = jnp.zeros((QBLOCK, LANES), F32)
        for head in range(HEADS_DEV):
            summed = jnp.sum(only(head_lanes(head, QBLOCK), overlap), axis=1, keepdims=True)
            inner = jnp.where(lane == head, summed, inner)
        inner = inner.T[:8]
        head_row = lax.broadcasted_iota(jnp.int32, (8, QBLOCK), 0)
        head_rows = lax.broadcasted_iota(jnp.int32, (LOCAL, count), 0) // HEAD_DIM

        def one_head(head, turned_query):
            mask = head_lanes(head, QBLOCK)
            masked, masked_given = only(mask, query), only(mask, given)
            log = jnp.sum(only(head_row == head, logs[:, span]), axis=0, keepdims=True)
            mean = jnp.sum(only(head_row == head, inner), axis=0, keepdims=True)
            scores = dot_t(acts[1, pl.ds(0, count), :], masked)
            probs = only(allow, jnp.exp(scores - log))
            grad_probs = dot_t(acts[2, pl.ds(0, count), :], masked_given)
            grad_scores = (probs * (grad_probs - mean)).astype(BF16)
            grads_qkv[2, pl.ds(0, count), :] += dot(probs.astype(BF16), masked_given)
            grads_qkv[1, pl.ds(0, count), :] += dot(grad_scores, masked)
            keys = only(head_rows == head, keys_turned[:, pl.ds(0, count)])
            return turned_query + dot(keys, grad_scores)

        turned_query = lax.fori_loop(0, HEADS_DEV, one_head, jnp.zeros((LOCAL, QBLOCK), F32))
        grads_qkv[0, span, :] = turned_query.T * SCALE

    grads_qkv[1] = jnp.zeros((GROUP, LOCAL), F32)
    grads_qkv[2] = jnp.zeros((GROUP, LOCAL), F32)
    attend(0)
    attend(QBLOCK)
    out_scatter.one()
    attend(2 * QBLOCK)
    out_scatter.two()
    feed_fold.cross()
    attend(3 * QBLOCK)

    def input_grad(y, sums_so_far):
        first = pl.multiple_of(y * QBLOCK, QBLOCK)
        span = pl.ds(first, QBLOCK)
        back = jnp.zeros((QBLOCK, WIDTH), F32)
        new = []
        for c in range(3):
            pre = grads_qkv[c, span, :]
            if c < 2:
                pre = turned(pre, tables, first, -1.0)
            pre = pre.astype(BF16)
            new.append(jnp.sum(pre.astype(F32), axis=0, keepdims=True))
            back = back + dot_t(pre, weights[c])
            turns[pl.ds(c * LOCAL, LOCAL), span] = pre.T
        parts[pl.ds(2 * y, 2)] = back.astype(BF16).reshape(2, ROWS, WIDTH)
        return sums_so_far + jnp.concatenate(new, axis=0)

    bias_sums = input_grad(a.y_far, jnp.zeros((3, LOCAL), F32))
    scatter.from_far_o()
    scatter.from_far()
    bias_sums = input_grad(a.y_up, bias_sums)
    scatter.from_up_o()
    scatter.from_up()
    bias_sums = input_grad(a.y_down, bias_sums)
    scatter.from_down_o()
    scatter.from_down()
    bias_sums = input_grad(a.y, bias_sums)
    scatter.from_across()

    def to_sibling(index):
        return kmail.copy(index, grads.at[index, 1 - r.core], core_land.at[index], r.to_core)

    def weight_grad(index, carry):
        columns = pl.ds(pl.multiple_of(index * 2 * ROWS, 2 * ROWS), 2 * ROWS)
        three = dot(
            turns[pl.ds(0, 3 * LOCAL), :], before[:, :, columns].reshape(GROUP, 2 * ROWS)
        )
        last = dot(turns[pl.ds(3 * LOCAL, LOCAL), :], rows[:, :, columns].reshape(GROUP, 2 * ROWS))
        for core in range(2):
            lanes = slice(core * ROWS, (core + 1) * ROWS)
            grads[index, core, pl.ds(0, 3 * LOCAL), :] = three[:, lanes].astype(BF16)
            grads[index, core, pl.ds(3 * LOCAL, LOCAL), :] = last[:, lanes].astype(BF16)
        to_sibling(index).start()
        return carry

    def core_sum(index, carry):
        to_sibling(index).wait()
        core_land[index] = added(grads[index, r.core], core_land[index]).astype(BF16)
        return carry

    lax.fori_loop(0, 8, weight_grad, 0)
    scatter.one()
    lax.fori_loop(0, 8, core_sum, 0)
    for number in range(6):
        fold.send(number)
    feed_fold.near()
    feed_sum = feed_fold.result()
    gate_up_grad[...] = feed_sum[: 2 * UNITS]
    down_grad[...] = feed_sum[2 * UNITS :]
    scatter.two()
    out_scatter.three(total)
    layer_out[...] = (mixed[...] + total[...]).astype(BF16)
    fold.cross()
    fold.near()
    scatter.three(total)
    normal, rinv = normalized(tokens[...].astype(F32))
    back, gain_grad, shift_grad = norm_back(total[...], normal, rinv, gain1[...])
    token_grad[...] = (grad_mixed[...] + back).astype(BF16)
    values = jnp.concatenate([gain_grad, shift_grad, norm2_grads[...]], axis=0)
    values = jnp.concatenate([values[:, k : k + LANES] for k in range(0, WIDTH, LANES)], axis=0)
    biases = jnp.concatenate([bias_sums[:, k : k + LANES] for k in range(0, LOCAL, LANES)], axis=0)
    values = jnp.concatenate([values, biases, jnp.zeros((2, LANES), F32)], axis=0)
    sums[...] = sum_everywhere(a, r, amail, boxes, values)
    shard = fold.result()
    for c in range(3):
        qkv_grad[c] = shard[c * LOCAL : (c + 1) * LOCAL].T
    out_grad[...] = shard[3 * LOCAL :]
    for some in (gmail, mail, omail, kmail, wmail, fmail, amail):
        some.finish()


def attention_backward(*operands):
    group = (TENSOR, ROWS, WIDTH)
    block, feed_block = (4 * LOCAL, ROWS), (3 * UNITS, ROWS)
    return pl.pallas_call(
        attention_back_kernel,
        out_shape=(
            jax.ShapeDtypeStruct((ROWS, WIDTH), BF16),
            jax.ShapeDtypeStruct((ROWS, WIDTH), BF16),
            jax.ShapeDtypeStruct((3, ROWS, LOCAL), F32),
            jax.ShapeDtypeStruct((LOCAL, ROWS), F32),
            jax.ShapeDtypeStruct((2 * UNITS, ROWS), F32),
            jax.ShapeDtypeStruct((UNITS, ROWS), F32),
            jax.ShapeDtypeStruct((SUM_ROWS, LANES), F32),
        ),
        in_specs=vmem(12) + anywhere(3),
        out_specs=tuple(vmem(7)),
        scratch_shapes=[
            pltpu.VMEM(group, BF16),
            pltpu.VMEM(group, BF16),
            pltpu.VMEM((GROUP, LOCAL), BF16),
            pltpu.VMEM((3, GROUP, LOCAL), F32),
            pltpu.VMEM((LOCAL, GROUP), BF16),
            pltpu.VMEM((4 * LOCAL, GROUP), BF16),
            pltpu.VMEM(group, BF16),
            pltpu.VMEM(group, BF16),
            pltpu.VMEM((8, 2) + block, BF16),
            pltpu.VMEM((scatter_rows_needed(TOP_BACK), WIDTH), BF16),
            pltpu.VMEM((scatter_rows_needed(TOP_OUTS), WIDTH), BF16),
            pltpu.VMEM((8,) + block, BF16),
            pltpu.VMEM((FOLD_MAILS,) + block, BF16),
            pltpu.VMEM((FOLD_MAILS,) + feed_block, BF16),
            pltpu.VMEM((2,) + feed_block, BF16),
            pltpu.VMEM((ROWS, WIDTH), F32),
            pltpu.VMEM((SUM_BOXES, SUM_ROWS, LANES), F32),
            *pairs(GATHER_MAILS),
            *pairs(SCATTER_MAILS),
            *pairs(SCATTER_MAILS),
            *pairs(8),
            *pairs(FOLD_MAILS),
            *pairs(FOLD_MAILS),
            *pairs(SUM_MAILS),
            pltpu.SemaphoreType.DMA((4,)),
        ],
        compiler_params=params(2),
        name="attention_backward",
    )(*operands)


def body(
    tokens,
    doc_ids,
    qkv_weight,
    qkv_bias,
    out_weight,
    norm1_gain,
    norm1_shift,
    norm2_gain,
    norm2_shift,
    gate_up_weight,
    down_weight,
    cotangent,
):
    norms = [item[None] for item in (norm1_gain, norm1_shift, norm2_gain, norm2_shift)]
    frequency = jnp.power(10000.0, -2.0 * jnp.arange(ROT // 2, dtype=F32) / ROT)
    frequency = jnp.broadcast_to(frequency[:, None], (ROT // 2, LANES))
    gate_up = jnp.swapaxes(gate_up_weight, 1, 2).reshape(2 * UNITS, ROWS)
    normed2, mixed, tables, start, acts, attended, logs, rows, weights, cots, feed = attention_forward(
        tokens,
        doc_ids[None],
        qkv_bias,
        out_weight,
        norms,
        frequency,
        qkv_weight,
        gate_up,
        down_weight,
        cotangent,
    )
    grad_mixed, branch_grad, norm2_grads, halves, outs = feed_forward(
        normed2, mixed, cotangent, norms[2], cots, feed
    )
    layer_out, token_grad, qkv_grad, out_grad, gate_up_grad, down_grad, sums = attention_backward(
        branch_grad,
        grad_mixed,
        mixed,
        tokens,
        norms[0],
        norm2_grads,
        tables,
        start,
        acts,
        attended,
        logs,
        weights,
        halves,
        rows,
        outs,
    )
    norm_sums = jnp.swapaxes(sums[:SUM_NORMS].reshape(WIDTH // LANES, 4, LANES), 0, 1)
    gain1_sum, shift1_sum, gain2_sum, shift2_sum = norm_sums.reshape(4, WIDTH)
    biases = sums[SUM_NORMS : SUM_NORMS + 6].reshape(LOCAL // LANES, 3, LANES)
    return (
        layer_out,
        token_grad,
        qkv_grad,
        jnp.swapaxes(biases, 0, 1).reshape(3, LOCAL),
        out_grad,
        gain1_sum,
        shift1_sum,
        gain2_sum,
        shift2_sum,
        jnp.swapaxes(gate_up_grad.reshape(2, UNITS, ROWS), 1, 2),
        down_grad,
    )


def solution(mesh):
    in_specs = (
        P(("dp", "tensor"), None),
        P(("dp", "tensor")),
        P(None, "dp", "tensor"),
        P(None, "tensor"),
        P("tensor", "dp"),
        P(),
        P(),
        P(),
        P(),
        P(None, "dp", "tensor"),
        P("tensor", "dp"),
        P(("dp", "tensor"), None),
    )
    out_specs = (
        P(("dp", "tensor"), None),
        P(("dp", "tensor"), None),
        P(None, "dp", "tensor"),
        P(None, "tensor"),
        P("tensor", "dp"),
        P(),
        P(),
        P(),
        P(),
        P(None, "dp", "tensor"),
        P("tensor", "dp"),
    )
    return jax.shard_map(body, mesh=mesh, in_specs=in_specs, out_specs=out_specs, check_vma=False)
```

```python
from functools import partial

import jax
import jax.numpy as jnp
from jax import lax
from jax.experimental import pallas as pl
from jax.experimental.pallas import tpu as pltpu
from jax.sharding import PartitionSpec as P

HEAD_DIM = 64
ROT = 16
DOCS = 4
EPS = 1e-05
SCALE = HEAD_DIM ** (-0.5)

ROWS = 128
WIDTH = 2048
TENSOR = 8
GROUP = ROWS * TENSOR
HALF = ROWS // 2
HEADS_DEV = 4
LOCAL = HEADS_DEV * HEAD_DIM
QBLOCK = 256
UNITS = 704
LANES = 128
MESH = pl.DeviceIdType.MESH
BF16 = jnp.bfloat16
F32 = jnp.float32
VMEM_LIMIT = 62 * 2**20


class Around:
    def __init__(self):
        dp, tensor = lax.axis_index("dp"), lax.axis_index("tensor")
        y, z = tensor // 2, lax.rem(tensor, 2)
        up, down, far = lax.rem(y + 1, 4), lax.rem(y + 3, 4), lax.rem(y + 2, 4)
        other = 1 - z
        self.me, self.across = y * 2 + z, y * 2 + other
        self.up, self.down, self.far = up * 2 + z, down * 2 + z, far * 2 + z
        self.up_o, self.down_o, self.far_o = up * 2 + other, down * 2 + other, far * 2 + other
        self.y, self.z = y, z
        self.y_up, self.y_down, self.y_far = up, down, far
        self.to_up, self.to_down, self.to_across = (dp, self.up), (dp, self.down), (dp, self.across)
        self.to_rest = [(dp, slot) for slot in (self.far, self.up_o, self.down_o, self.far_o)]

    def peers(self):
        return [self.to_up, self.to_down, self.to_across]


class Ring:
    def __init__(self):
        dp, tensor = lax.axis_index("dp"), lax.axis_index("tensor")
        zh, x, core = dp // 8, lax.rem(dp // 2, 4), lax.rem(dp, 2)
        self.zh, self.x, self.core, self.dp, self.tensor = zh, x, core, dp, tensor
        self.xs = [lax.rem(x + step, 4) for step in range(4)]
        self.to_x = [(self.index(zh, self.xs[step], core), tensor) for step in range(4)]
        self.to_zh = (self.index(1 - zh, x, core), tensor)
        self.to_core = (self.index(zh, x, 1 - core), tensor)
        self.to_zh_core = (self.index(1 - zh, x, 1 - core), tensor)

    def index(self, zh, x, core):
        return zh * 8 + x * 2 + core

    def peers(self):
        return self.to_x[1:] + [self.to_zh, self.to_core]


def hail(peers):
    barrier = pltpu.get_barrier_semaphore()
    for peer in peers:
        pl.semaphore_signal(barrier, inc=1, device_id=peer, device_id_type=MESH)


def hear(peers):
    pl.semaphore_wait(pltpu.get_barrier_semaphore(), len(peers))


class Mail:
    def __init__(self, sends, receives):
        self.sends, self.receives = sends, receives
        self.out = []

    def copy(self, number, source, target, device):
        return pltpu.make_async_remote_copy(
            src_ref=source,
            dst_ref=target,
            send_sem=self.sends.at[number],
            recv_sem=self.receives.at[number],
            device_id=device,
            device_id_type=MESH,
        )

    def send(self, number, source, target, device):
        copy = self.copy(number, source, target, device)
        copy.start()
        self.out.append(copy)

    def landed(self, number, target, device):
        self.copy(number, target, target, device).wait_recv()

    def finish(self):
        for copy in self.out:
            copy.wait_send()
        self.out = []


MIDDLE = {64: 96, 48: 96, 32: 80}
GATHER_MAILS = 17


class Gather:
    def __init__(self, around, mail, rows, top, own=None):
        a, middle = around, MIDDLE[top]
        self.mail, self.rows, self.own = mail, rows, own
        self.messages = [
            (a.to_up, a.me, 0, HALF, a.down),
            (a.to_down, a.me, HALF, ROWS, a.up),
            (a.to_across, a.me, top, ROWS, a.across),
            (a.to_up, a.me, HALF, ROWS, a.down),
            (a.to_down, a.me, 0, HALF, a.up),
            (a.to_across, a.me, 0, top, a.across),
            (a.to_up, a.down, 0, HALF, a.far),
            (a.to_across, a.down, 0, top, a.down_o),
            (a.to_down, a.up, HALF, ROWS, a.far),
            (a.to_up, a.across, top, middle, a.down_o),
            (a.to_down, a.across, middle, ROWS, a.up_o),
            (a.to_across, a.up, 0, top, a.up_o),
            (a.to_across, a.far, 0, top, a.far_o),
            (a.to_up, a.down_o, top, middle, a.far_o),
            (a.to_down, a.up_o, middle, ROWS, a.far_o),
            (a.to_up, a.across, middle, ROWS, a.down_o),
            (a.to_down, a.across, top, middle, a.up_o),
        ]

    def part(self, slot, first, last):
        return self.rows.at[slot, pl.ds(first, last - first)]

    def send(self, *numbers):
        for number in numbers:
            device, slot, first, last, _ = self.messages[number]
            target = source = self.part(slot, first, last)
            if number < 6 and self.own is not None:
                source = self.own.at[pl.ds(first, last - first)]
            self.mail.send(number, source, target, device)

    def step(self, number):
        return partial(self.on, number)

    def on(self, number):
        device, _, first, last, slot = self.messages[number]
        self.mail.landed(number, self.part(slot, first, last), device)
        followers = {0: (6, 7), 1: (8,), 2: (9, 10, 15, 16), 4: (11,), 6: (12,), 9: (13,), 10: (14,)}
        self.send(*followers.get(number, ()))


def added(*terms):
    total = terms[0].astype(F32)
    for term in terms[1:]:
        total = total + term.astype(F32)
    return total


SCATTER_MAILS = 21


def scatter_boxes(top):
    middle = MIDDLE[top]
    last, inner, rest = ROWS - middle, middle - top, HALF - top
    counts = (last, inner, top, HALF, top, top, last, inner, HALF, top)
    counts += (top, inner, last, HALF, top, top, inner, rest, rest, rest, last, inner, last)
    order = [*range(17), 20, 17, 18, 19, 21, 22]
    firsts = [0] * len(counts)
    for before, number in zip(order, order[1:]):
        firsts[number] = firsts[before] + counts[before]
    return counts, tuple(firsts)


def scatter_rows_needed(top):
    return sum(scatter_boxes(top)[0])


class Scatter:
    def __init__(self, around, mail, parts, land, top):
        self.a, self.mail, self.parts, self.land, self.top = around, mail, parts, land, top
        self.middle = MIDDLE[top]
        self.counts, self.firsts = scatter_boxes(top)

    def part(self, slot, first, last):
        return self.parts.at[slot, pl.ds(first, last - first)]

    def box(self, number):
        return self.land.at[pl.ds(self.firsts[number], self.counts[number])]

    def got(self, number):
        self.mail.landed(number, self.box(number), self.a.to_up)

    def fold(self, stage, slot, first, *others):
        terms = [self.part(slot, first, first + self.counts[stage])[...], self.box(stage)[...]]
        terms += [self.box(other)[...] for other in others]
        self.box(stage)[...] = added(*terms).astype(BF16)

    def direct(self, *numbers):
        a, top, middle = self.a, self.top, self.middle
        messages = {
            0: (a.far_o, middle, a.to_up),
            1: (a.far_o, top, a.to_down),
            2: (a.far_o, 0, a.to_across),
            3: (a.far, HALF, a.to_up),
            17: (a.far, top, a.to_down),
            4: (a.up_o, 0, a.to_across),
            7: (a.up_o, top, a.to_up),
            5: (a.down_o, 0, a.to_across),
            6: (a.down_o, middle, a.to_down),
            18: (a.up, top, a.to_up),
            8: (a.down, HALF, a.to_down),
            9: (a.across, 0, a.to_across),
        }
        for number in numbers:
            slot, first, device = messages[number]
            source = self.part(slot, first, first + self.counts[number])
            self.mail.send(number, source, self.box(number), device)

    def from_far_pair(self):
        self.direct(0, 1, 2, 3, 17)

    def from_up_pair(self):
        self.direct(7, 4, 18)

    def from_down_pair(self):
        self.direct(6, 5, 8)

    def from_across(self):
        self.direct(9)

    def direct_up(self):
        self.direct(0, 3, 7, 18)

    def direct_down(self):
        self.direct(1, 17, 6, 8)

    def direct_across(self):
        self.direct(2, 4, 5, 9)

    def step(self, number):
        return partial(self.on, number)

    def on(self, number):
        a, box = self.a, self.box
        follower, slot, first, device, *others = {
            1: (11, a.down_o, self.top, a.to_down),
            0: (12, a.up_o, self.middle, a.to_up),
            2: (10, a.far, 0, a.to_down),
            3: (13, a.up, HALF, a.to_up),
            17: (19, a.down, self.top, a.to_down),
            4: (14, a.up, 0, a.to_up),
            5: (15, a.down, 0, a.to_down, 10),
        }[number]
        for other in (number, *others):
            self.got(other)
        self.fold(number, slot, first, *others)
        self.mail.send(follower, box(number), box(follower), device)

    def over(self, number, made, first, *landed):
        for other in landed:
            self.got(other)
        own = self.part(self.a.across, first, first + self.counts[number])
        terms = [own[...]] + [self.box(other)[...] for other in landed]
        self.box(made)[...] = added(*terms).astype(BF16)
        self.mail.send(number, self.box(made), self.box(number), self.a.to_across)

    def over_inner(self):
        self.over(16, 21, self.top, 7, 11)

    def over_last(self):
        self.over(20, 22, self.middle, 6, 12)

    def all_direct(self):
        self.direct(0, 1, 2, 3, 17, 7, 4, 6, 5, 18, 8, 9)

    def finish(self, total):
        a, top = self.a, self.top
        for number in (8, 9, 13, 14, 18, 19, 16, 20, 15):
            self.got(number)

        def boxed(number, first, last):
            return self.land[pl.ds(self.firsts[number] + first, last - first), :]

        total[pl.ds(0, top), :] = added(
            self.part(a.me, 0, top)[...], *(self.box(k)[...] for k in (9, 14, 15))
        )
        total[pl.ds(top, HALF - top), :] = added(
            self.part(a.me, top, HALF)[...],
            self.box(18)[...],
            self.box(19)[...],
            boxed(16, 0, HALF - top),
        )
        total[pl.ds(HALF, HALF), :] = added(
            self.part(a.me, HALF, ROWS)[...],
            self.box(8)[...],
            self.box(13)[...],
            boxed(16, HALF - top, ROWS - top),
        )


class Spread:
    def __init__(self, ring, mail, block, own_shard=None):
        r = self.r = ring
        self.mail, self.block, self.own = mail, block, own_shard
        own, cross = (r.zh, r.x), (1 - r.zh, r.x)
        self.messages = [(r.to_zh, own, cross)]
        self.messages += [(r.to_x[k], own, (r.zh, r.xs[4 - k])) for k in (1, 2, 3)]
        self.messages += [(r.to_x[k], cross, (1 - r.zh, r.xs[4 - k])) for k in (1, 2, 3)]
        self.messages += [(r.to_core, own, own), (r.to_core, cross, cross)]
        self.messages += [(r.to_core, self.messages[k][2], self.messages[k][2]) for k in range(1, 7)]

    def send(self, number):
        device, place, _ = self.messages[number]
        block = self.block(*place, self.r.core)
        source = self.own if self.own is not None and number in (0, 1, 2, 3, 7) else block
        self.mail.send(number, source, block, device)

    def step(self, number):
        return partial(self.on, number)

    def begin(self):
        for number in (0, 1, 3, 2, 7):
            self.send(number)

    def on(self, number):
        device, _, place = self.messages[number]
        core = self.r.core if number < 7 else 1 - self.r.core
        self.mail.landed(number, self.block(*place, core), device)
        if number == 0:
            for follower in (4, 6, 5, 8):
                self.send(follower)
        elif number < 7:
            self.send(number + 8)

    def finish(self):
        for number in range(7, SPREAD_MAILS):
            self.on(number)


SPREAD_MAILS = 15
FOLDS = [(side, step) for step in (1, 3, 2, 0) for side in (1, 0)]


class Fold:
    def __init__(self, ring, mail, grads, own, land):
        self.r, self.mail, self.grads, self.own, self.land = ring, mail, grads, own, land

    def place(self, side, step):
        zh = 1 - self.r.zh if side else self.r.zh
        return zh * 4 + self.r.xs[step]

    def send(self, *numbers):
        for number in numbers:
            side, step = FOLDS[number]
            source = self.grads.at[self.place(side, step)]
            self.mail.send(number, source, self.land.at[number], self.r.to_x[step])

    def cross(self):
        for number in (0, 2, 4):
            self.mail.landed(number, self.land.at[number], self.r.to_core)
        self.land[0] = added(self.own(1), self.land[0], self.land[2], self.land[4]).astype(BF16)
        self.mail.send(6, self.land.at[0], self.land.at[6], self.r.to_zh)

    def near(self):
        for number in (1, 3, 5):
            self.mail.landed(number, self.land.at[number], self.r.to_core)

    def result(self):
        self.mail.landed(6, self.land.at[6], self.r.to_core)
        land = self.land
        return added(self.own(0), land[1], land[3], land[5], land[6])


FOLD_MAILS = 7

EARLY_ROWS, NORM_ROWS = 40, 32
SUM_BOXES, SUM_MAILS = 14, 13


class EverySum:
    def __init__(self, a, r, mail, boxes, rows, norms):
        self.norms, self.mail, self.boxes = norms, mail, boxes
        crossed = 1 - r.zh
        place = r.zh * 2 + r.core
        z_sources = [crossed * 2 + r.core, r.zh * 2 + 1 - r.core, crossed * 2 + 1 - r.core]
        z_peers = [r.to_zh, r.to_core, r.to_zh_core]
        y_peers = [a.to_up, a.to_rest[0], a.to_down]
        self.stages = [
            (0, rows, r.x, [r.xs[3], r.xs[2], r.xs[1]], r.to_x[1:]),
            (4, rows, place, z_sources, z_peers),
            (8, norms, a.y, [a.y_down, a.y_far, a.y_up], y_peers),
            (12, norms, a.z, [1 - a.z], [a.to_across]),
        ]

    def give(self, stage, values):
        base, count, mine, _, peers = self.stages[stage]
        view = pl.ds(0, count)
        self.boxes[base + mine, view] = values
        for number, peer in enumerate(peers):
            box = self.boxes.at[base + mine, view]
            self.mail.send(base + number, box, box, peer)

    def take(self, stage):
        base, count, _, sources, peers = self.stages[stage]
        view = pl.ds(0, count)
        for number, source in enumerate(sources):
            self.mail.landed(base + number, self.boxes.at[base + source, view], peers[0])
        result = self.boxes[base, view]
        for k in range(1, len(peers) + 1):
            result = result + self.boxes[base + k, view]
        return result

    def first(self, values):
        self.give(0, values)

    def second(self):
        self.give(1, self.take(0))

    def third(self):
        self.over_dp = self.take(1)
        self.give(2, self.over_dp[: self.norms])

    def fourth(self):
        self.give(3, self.take(2))

    def result(self):
        total = self.take(3)
        if self.norms == self.over_dp.shape[0]:
            return total
        return jnp.concatenate([total, self.over_dp[self.norms :]], axis=0)


def dot(left, right):
    return lax.dot_general(left, right, (((1,), (0,)), ((), ())), preferred_element_type=F32)


def dot_t(left, right):
    return lax.dot_general(left, right, (((1,), (1,)), ((), ())), preferred_element_type=F32)


def normalized(values):
    centred = values - jnp.mean(values, axis=1, keepdims=True)
    variance = jnp.mean(centred * centred, axis=1, keepdims=True)
    rinv = lax.rsqrt(variance + EPS)
    return centred * rinv, rinv


def norm_back(incoming, normal, rinv, gain):
    scaled = incoming * gain
    inner = scaled - jnp.mean(scaled, axis=1, keepdims=True)
    inner = inner - normal * jnp.mean(scaled * normal, axis=1, keepdims=True)
    gain_grad = jnp.sum(incoming * normal, axis=0, keepdims=True)
    return rinv * inner, gain_grad, jnp.sum(incoming, axis=0, keepdims=True)


def turned(values, tables, first, sign):
    rows = pl.ds(first, values.shape[0])
    cosine, minus, plus = tables[0, rows], tables[1, rows], tables[2, rows]
    halves = []
    for lane in range(0, LOCAL, LANES):
        part = values[:, lane : lane + LANES]
        left = pltpu.roll(part, LANES - ROT // 2, 1)
        right = pltpu.roll(part, ROT // 2, 1)
        halves.append(part * cosine + sign * (left * minus + right * plus))
    return jnp.concatenate(halves, axis=1)


def head_lanes(head, rows):
    return lax.broadcasted_iota(jnp.int32, (rows, LOCAL), 1) // HEAD_DIM == head


def only(mask, values):
    return jnp.where(mask, values, jnp.zeros_like(values))


def place_rows(id_rows, frequency, tables, start_rows, start_lanes):
    ids = jnp.max(id_rows[...], axis=1)
    shape = (TENSOR, ROWS)
    index = lax.broadcasted_iota(jnp.int32, shape, 0) * ROWS
    index = (index + lax.broadcasted_iota(jnp.int32, shape, 1)).astype(F32)
    offset = jnp.zeros(shape, F32)
    for number in range(1, DOCS):
        before = ((ids >= 0) & (ids < number)).astype(F32)
        count = jnp.sum(jnp.sum(before, axis=1, keepdims=True), axis=0, keepdims=True)
        offset = jnp.where(ids == number, count, offset)
    start = jnp.where(ids >= 0, offset, index)
    position = index - offset

    def along(values):
        return jnp.concatenate([values[t : t + 1] for t in range(TENSOR)], axis=1)

    angle = frequency[:, :1] * along(position)
    cosine, sine = jnp.cos(angle), jnp.sin(angle)
    none = jnp.zeros_like(sine)
    rest = (HEAD_DIM - ROT) // 8
    columns = (
        [cosine, cosine] + [jnp.ones_like(sine)] * rest,
        [-sine, none] + [none] * rest,
        [none, sine] + [none] * rest,
    )
    for number, parts in enumerate(columns):
        tables[number] = jnp.concatenate(parts + parts, axis=0).T
    lanes = jnp.broadcast_to(along(start), (8, GROUP))
    start_lanes[...] = lanes
    start_rows[...] = jnp.concatenate([lanes] * (LANES // 8), axis=0).T


def vmem(count):
    return [pl.BlockSpec(memory_space=pltpu.VMEM)] * count


def anywhere(count):
    return [pl.BlockSpec(memory_space=pl.ANY)] * count


def pairs(count):
    return [pltpu.SemaphoreType.DMA((count,)), pltpu.SemaphoreType.DMA((count,))]


def params(collective):
    return pltpu.CompilerParams(
        collective_id=collective, has_side_effects=True, vmem_limit_bytes=VMEM_LIMIT
    )


TOP_ROWS, TOP_COTS, TOP_BRANCH = 48, 32, 48


def attention_kernel(
    tokens,
    ids,
    bias,
    out_shard,
    gain1,
    shift1,
    gain2,
    shift2,
    frequency,
    qkv_shard,
    gate_up,
    down,
    own_cots,
    normed2,
    start_lanes,
    logs,
    mixed_kept,
    tables_kept,
    acts_kept,
    attended_kept,
    rows_kept,
    weights_kept,
    cots,
    feed,
    rows,
    weights,
    feed_own,
    cots_own,
    tables,
    acts,
    attended,
    mixed,
    id_rows,
    start_rows,
    parts,
    land,
    total,
    r_sends,
    r_receives,
    c_sends,
    c_receives,
    b_sends,
    b_receives,
    w_sends,
    w_receives,
    f_sends,
    f_receives,
    i_sends,
    i_receives,
    local,
):
    a, r = Around(), Ring()
    rmail, cmail, bmail = Mail(r_sends, r_receives), Mail(c_sends, c_receives), Mail(b_sends, b_receives)
    wmail, fmail, imail = Mail(w_sends, w_receives), Mail(f_sends, f_receives), Mail(i_sends, i_receives)
    peers = a.peers() + a.to_rest + r.peers()
    hail(peers)

    def weight_block(zh, x, core):
        first = pl.multiple_of(r.index(zh, x, core) * ROWS, ROWS)
        return weights.at[:, pl.ds(first, ROWS), :]

    mine = pl.multiple_of(r.dp * ROWS, ROWS)
    loads = [
        pltpu.make_async_copy(qkv_shard, weights.at[pl.ds(0, 3), pl.ds(mine, ROWS)], local.at[0]),
        pltpu.make_async_copy(gate_up, feed_own.at[pl.ds(0, 2 * UNITS)], local.at[1]),
        pltpu.make_async_copy(down, feed_own.at[pl.ds(2 * UNITS, UNITS)], local.at[2]),
        pltpu.make_async_copy(own_cots, cots_own, local.at[3]),
    ]
    for copy in loads:
        copy.start()
    id_rows[a.me] = jnp.broadcast_to(ids[...], (8, ROWS))
    weights[3, pl.ds(mine, ROWS), :] = out_shard[...].T
    normal, _ = normalized(tokens[...].astype(F32))
    rows[a.me] = (normal * gain1[...] + shift1[...]).astype(BF16)
    hear(peers)

    group = [
        (0, a.to_up, a.down),
        (1, a.to_down, a.up),
        (2, a.to_across, a.across),
        (3, a.to_rest[0], a.far),
        (4, a.to_rest[1], a.down_o),
        (5, a.to_rest[2], a.up_o),
        (6, a.to_rest[3], a.far_o),
    ]
    gather = Gather(a, rmail, rows, TOP_ROWS)
    others = Gather(a, cmail, cots, TOP_COTS, cots_own)
    spread = Spread(r, wmail, weight_block)
    feeds = Spread(r, fmail, lambda zh, x, core: feed.at[r.index(zh, x, core)], feed_own)
    scatter = Scatter(a, bmail, parts, land, TOP_BRANCH)
    started = []

    def keep(source, target, number):
        copy = pltpu.make_async_copy(source, target, local.at[number])
        copy.start()
        started.append(copy)

    def begin():
        for number, device, _ in group:
            imail.send(number, id_rows.at[a.me], id_rows.at[a.me], device)
        for number in (0, 1, 2):
            gather.send(number)
        loads[0].wait()
        spread.begin()
        for number in (3, 4, 5):
            gather.send(number)
        for copy in loads[1:]:
            copy.wait()
        keep(feed_own, feed.at[r.dp], 4)
        keep(cots_own, cots.at[a.me], 5)

    def place():
        for number, _, slot in group:
            imail.landed(number, id_rows.at[slot], a.to_up)
        place_rows(id_rows, frequency, tables, start_rows, start_lanes)
        keep(tables, tables_kept, 6)

    def P(y):
        return partial(project, y)

    def project(y):
        first = pl.multiple_of(y * QBLOCK, QBLOCK)
        chunk = rows[pl.ds(2 * y, 2)].reshape(QBLOCK, WIDTH)
        for c in range(3):
            pre = dot(chunk, weights[c]) + bias[pl.ds(c, 1), :]
            if c < 2:
                pre = turned(pre, tables, first, 1.0)
            acts[c, pl.ds(first, QBLOCK), :] = pre.astype(BF16)

    state = {}

    def A(q, *heads):
        return partial(attend, q * QBLOCK, heads)

    def attend(first, heads):
        count = first + QBLOCK
        query = acts[0, pl.ds(first, QBLOCK), :] * BF16(SCALE)
        row = first + lax.broadcasted_iota(jnp.int32, (QBLOCK, count), 0)
        column = lax.broadcasted_iota(jnp.int32, (QBLOCK, count), 1)
        start = start_rows[pl.ds(first, QBLOCK), pl.ds(0, 1)]
        allow = (column <= row) & (column.astype(F32) >= start)
        lane = lax.broadcasted_iota(jnp.int32, (QBLOCK, LANES), 1)

        def one_head(head, carry):
            out, log = carry
            masked = only(head_lanes(head, QBLOCK), query)
            scores = dot_t(masked, acts[1, pl.ds(0, count), :])
            scores = jnp.where(allow, scores, -1e30)
            highest = jnp.max(scores, axis=1, keepdims=True)
            expon = jnp.exp(scores - highest)
            sums = jnp.sum(expon, axis=1, keepdims=True)
            values = only(head_lanes(head, count), acts[2, pl.ds(0, count), :])
            out = out + dot(expon.astype(BF16), values) / sums
            log = jnp.where(lane == head, highest + jnp.log(sums), log)
            return out, log

        zeros = (jnp.zeros((QBLOCK, LOCAL), F32), jnp.zeros((QBLOCK, LANES), F32))
        carry = lax.fori_loop(*heads, one_head, state.pop("attend", zeros))
        if heads[1] < HEADS_DEV:
            state["attend"] = carry
            return
        out = carry[0].astype(BF16)
        attended[pl.ds(first, QBLOCK), :] = out
        logs[:, pl.ds(first, QBLOCK)] = carry[1].T[:8]
        branch = dot_t(out, weights[3]).astype(BF16)
        parts[first // ROWS] = branch[:ROWS]
        parts[first // ROWS + 1] = branch[ROWS:]

    def branch_sums():
        keep(rows, rows_kept, 7)
        keep(weights, weights_kept, 8)
        keep(acts, acts_kept, 9)
        keep(attended, attended_kept, 10)
        scatter.all_direct()

    def second_norm():
        scatter.finish(total)
        after = tokens[...].astype(F32) + total[...]
        mixed[...] = after
        keep(mixed, mixed_kept, 11)
        normal, _ = normalized(after)
        normed2[...] = (normal * gain2[...] + shift2[...]).astype(BF16)

    R, C, B, w, f = gather.step, others.step, scatter.step, spread.step, feeds.step
    C_up, C_down, C_across = (partial(others.send, *two) for two in ((0, 3), (1, 4), (2, 5)))
    for step in (
        begin, place, R(0), R(1), w(1), w(3), R(2), R(3), R(4), w(2), w(0), R(6), R(8), C_across,
        R(5), feeds.begin, R(10), C_down, w(4), w(6), R(9), C_up, R(7), R(15), R(16), R(11), R(14),
        w(5), R(13), R(12), spread.finish, P(a.y_down), P(a.y_far), C(1), P(a.y), P(a.y_up),
        A(0, 0, 4), A(1, 0, 2), C(4), C(2), f(1), f(3), A(1, 2, 4), A(2, 0, 1), A(2, 1, 2), C(5),
        A(2, 2, 3), A(2, 3, 4), C(9), A(3, 0, 1), A(3, 1, 2), A(3, 2, 3), C(10), C(15), A(3, 3, 4),
        branch_sums, f(2), C(3), C(8), C(0), C(16), C(13), f(0), C(11), B(0), C(14), B(2), B(1),
        B(3), B(17), B(4), f(4), f(6), C(6), B(5), C(7), scatter.over_last, C(12),
        scatter.over_inner, f(5), feeds.finish, second_norm,
    ):
        step()
    for mail in (rmail, cmail, bmail, wmail, fmail, imail):
        mail.finish()
    for copy in started:
        copy.wait()


def attention_forward(tokens, ids, bias, out_shard, norms, frequency, qkv_shard, gate_up, down, cots):
    group = (TENSOR, ROWS, WIDTH)
    weights = (4, WIDTH, LOCAL)
    tables, acts = (3, GROUP, LANES), (3, GROUP, LOCAL)
    return pl.pallas_call(
        attention_kernel,
        out_shape=(
            jax.ShapeDtypeStruct((ROWS, WIDTH), BF16),
            jax.ShapeDtypeStruct((8, GROUP), F32),
            jax.ShapeDtypeStruct((8, GROUP), F32),
            jax.ShapeDtypeStruct((ROWS, WIDTH), F32),
            jax.ShapeDtypeStruct(tables, F32),
            jax.ShapeDtypeStruct(acts, BF16),
            jax.ShapeDtypeStruct((GROUP, LOCAL), BF16),
            jax.ShapeDtypeStruct(group, BF16),
            jax.ShapeDtypeStruct(weights, BF16),
            jax.ShapeDtypeStruct(group, BF16),
            jax.ShapeDtypeStruct((16, 3 * UNITS, ROWS), BF16),
        ),
        in_specs=vmem(9) + anywhere(4),
        out_specs=tuple(vmem(3) + anywhere(8)),
        scratch_shapes=[
            pltpu.VMEM(group, BF16),
            pltpu.VMEM(weights, BF16),
            pltpu.VMEM((3 * UNITS, ROWS), BF16),
            pltpu.VMEM((ROWS, WIDTH), BF16),
            pltpu.VMEM(tables, F32),
            pltpu.VMEM(acts, BF16),
            pltpu.VMEM((GROUP, LOCAL), BF16),
            pltpu.VMEM((ROWS, WIDTH), F32),
            pltpu.VMEM((TENSOR, 8, ROWS), jnp.int32),
            pltpu.VMEM((GROUP, LANES), F32),
            pltpu.VMEM(group, BF16),
            pltpu.VMEM((scatter_rows_needed(TOP_BRANCH), WIDTH), BF16),
            pltpu.VMEM((ROWS, WIDTH), F32),
            *pairs(GATHER_MAILS),
            *pairs(GATHER_MAILS),
            *pairs(SCATTER_MAILS),
            *pairs(SPREAD_MAILS),
            *pairs(SPREAD_MAILS),
            *pairs(7),
            pltpu.SemaphoreType.DMA((12,)),
        ],
        compiler_params=params(0),
        name="attention_forward",
    )(tokens, ids, bias, out_shard, *norms, frequency, qkv_shard, gate_up, down, cots)


TOP_FEED, TOP_FEED_BACK = 64, 48

def feed_kernel(
    gain2,
    own,
    mixed_in,
    cots_own,
    cots_in,
    feed,
    grad_mixed,
    branch_grad,
    norm_grads,
    halves,
    outs_kept,
    rows,
    cots,
    weights,
    parts,
    outs,
    acts,
    grads,
    land,
    core_land,
    mixed,
    own_cots,
    total,
    g_sends,
    g_receives,
    s_sends,
    s_receives,
    w_sends,
    w_receives,
    w_local,
    local,
):
    a, r = Around(), Ring()
    gmail, mail, wmail = Mail(g_sends, g_receives), Mail(s_sends, s_receives), Mail(w_sends, w_receives)
    peers = a.peers() + [r.to_core]
    hail(peers)
    first_load = pltpu.make_async_copy(own, rows.at[a.me], local.at[0])
    loads = [
        pltpu.make_async_copy(feed.at[n], weights.at[:, pl.ds(n * ROWS, ROWS)], w_local.at[n])
        for n in range(16)
    ]
    loads.append(pltpu.make_async_copy(cots_in, cots, local.at[1]))
    late_loads = [
        pltpu.make_async_copy(mixed_in, mixed, local.at[2]),
        pltpu.make_async_copy(cots_own, own_cots, local.at[3]),
    ]
    for copy in [first_load] + loads + late_loads:
        copy.start()
    first_load.wait()
    hear(peers)
    gather = Gather(a, gmail, rows, TOP_FEED)
    scatter = Scatter(a, mail, parts, land, TOP_FEED_BACK)
    started = []

    def keep(source, target, number):
        copy = pltpu.make_async_copy(source, target, local.at[number])
        copy.start()
        started.append(copy)

    def load():
        for copy in loads:
            copy.wait()

    state = {}

    def pair(index, *slots):
        x = jnp.concatenate([rows[slot] for slot in slots], axis=0)
        given = jnp.concatenate([cots[slot] for slot in slots], axis=0)
        gate = dot_t(x, weights[pl.ds(0, UNITS), :])
        upward = dot_t(x, weights[pl.ds(UNITS, UNITS), :])
        grad_hidden = dot_t(given, weights[pl.ds(2 * UNITS, UNITS), :])
        sigma = jax.nn.sigmoid(gate)
        silu = gate * sigma
        hidden = (silu * upward).astype(BF16)
        grad_gate = (grad_hidden * upward * (sigma + silu * (1.0 - sigma))).astype(BF16)
        grad_up = (grad_hidden * silu).astype(BF16)
        state[index] = hidden, grad_gate, grad_up

    def pair_back(index, *slots):
        _, grad_gate, grad_up = state[index]
        back = dot(grad_gate, weights[pl.ds(0, UNITS), :])
        back = (back + dot(grad_up, weights[pl.ds(UNITS, UNITS), :])).astype(BF16)
        for number, slot in enumerate(slots):
            parts[slot] = back[number * ROWS : (number + 1) * ROWS]

    def rest(index, *slots):
        hidden, grad_gate, grad_up = state[index]
        out = dot(hidden, weights[pl.ds(2 * UNITS, UNITS), :]).astype(BF16)
        for number, slot in enumerate(slots):
            chunk = slice(number * ROWS, (number + 1) * ROWS)
            outs[slot] = out[chunk]
            lanes = pl.ds(pl.multiple_of(slot * ROWS, ROWS), ROWS)
            acts[pl.ds(0, UNITS), lanes] = grad_gate[chunk].T
            acts[pl.ds(UNITS, UNITS), lanes] = grad_up[chunk].T
            acts[pl.ds(2 * UNITS, UNITS), lanes] = hidden[chunk].T

    def to_sibling(index):
        return wmail.copy(index, grads.at[index, 1 - r.core], core_land.at[index], r.to_core)

    def weight_grad(index, carry):
        columns = pl.ds(pl.multiple_of(index * 2 * ROWS, 2 * ROWS), 2 * ROWS)
        both = dot(acts[pl.ds(0, 2 * UNITS), :], rows[:, :, columns].reshape(GROUP, 2 * ROWS))
        low = dot(acts[pl.ds(2 * UNITS, UNITS), :], cots[:, :, columns].reshape(GROUP, 2 * ROWS))
        for core in range(2):
            lanes = slice(core * ROWS, (core + 1) * ROWS)
            grads[index, core, pl.ds(0, 2 * UNITS), :] = both[:, lanes].astype(BF16)
            grads[index, core, pl.ds(2 * UNITS, UNITS), :] = low[:, lanes].astype(BF16)
        to_sibling(index).start()
        return carry

    def core_sum(index, carry):
        to_sibling(index).wait()
        core_land[index] = added(grads[index, r.core], core_land[index]).astype(BF16)
        return carry

    def core_sums(first, last):
        lax.fori_loop(first, last, core_sum, 0)
        keep(core_land.at[pl.ds(first, last - first)], halves.at[pl.ds(first, last - first)], 4 + first // 4)

    def keep_outs():
        keep(outs, outs_kept, 6)

    def norm():
        for copy in late_loads:
            copy.wait()
        scatter.finish(total)
        normal, rinv = normalized(mixed[...])
        back, gain_grad, shift_grad = norm_back(total[...], normal, rinv, gain2[...])
        back = own_cots[...].astype(F32) + back
        grad_mixed[...] = back
        branch_grad[...] = back.astype(BF16)
        norm_grads[...] = jnp.concatenate([gain_grad, shift_grad], axis=0)

    couples = [(a.me, a.across), (a.down, a.up), (a.far, a.down_o), (a.far_o, a.up_o)]
    directs = [(9,), (18, 8), (3, 17, 6, 5), (0, 1, 2, 7, 4)]
    G, S = gather.step, scatter.step

    def P(index):
        return partial(pair, index, *couples[index])

    def Q(index):
        return partial(pair_back, index, *couples[index])

    def T(index):
        return partial(rest, index, *couples[index])

    def D(index):
        return partial(scatter.direct, *directs[index])

    def W(index):
        return partial(lax.fori_loop, 2 * index, 2 * index + 2, weight_grad, 0)

    def K(index):
        return partial(core_sums, 4 * index, 4 * index + 4)

    for step in (
        partial(gather.send, *range(6)), load, G(0), G(2), G(1), G(3), G(4), P(1), T(1), G(10),
        Q(1), D(1), G(5), P(0), G(16), G(6), G(7), Q(0), D(0), T(0), G(9), G(15), G(8), P(2), T(2),
        G(14), Q(2), D(2), G(13), G(11), G(12), P(3), Q(3), D(3), T(3), S(17), keep_outs, W(0),
        S(3), W(1), S(0), W(2), S(1), W(3), S(2), K(0), S(4), scatter.over_inner, K(1),
        scatter.over_last, S(5), norm,
    ):
        step()
    gmail.finish()
    mail.finish()
    for copy in started:
        copy.wait()


def feed_forward(gain2, own, mixed, own_cots, cots, feed):
    group = (TENSOR, ROWS, WIDTH)
    blocks = (8, 3 * UNITS, ROWS)
    return pl.pallas_call(
        feed_kernel,
        out_shape=(
            jax.ShapeDtypeStruct((ROWS, WIDTH), F32),
            jax.ShapeDtypeStruct((ROWS, WIDTH), BF16),
            jax.ShapeDtypeStruct((2, WIDTH), F32),
            jax.ShapeDtypeStruct(blocks, BF16),
            jax.ShapeDtypeStruct(group, BF16),
        ),
        in_specs=vmem(1) + anywhere(5),
        out_specs=tuple(vmem(3) + anywhere(2)),
        scratch_shapes=[
            pltpu.VMEM(group, BF16),
            pltpu.VMEM(group, BF16),
            pltpu.VMEM((3 * UNITS, WIDTH), BF16),
            pltpu.VMEM(group, BF16),
            pltpu.VMEM(group, BF16),
            pltpu.VMEM((3 * UNITS, GROUP), BF16),
            pltpu.VMEM((8, 2, 3 * UNITS, ROWS), BF16),
            pltpu.VMEM((scatter_rows_needed(TOP_FEED_BACK), WIDTH), BF16),
            pltpu.VMEM(blocks, BF16),
            pltpu.VMEM((ROWS, WIDTH), F32),
            pltpu.VMEM((ROWS, WIDTH), BF16),
            pltpu.VMEM((ROWS, WIDTH), F32),
            *pairs(GATHER_MAILS),
            *pairs(SCATTER_MAILS),
            *pairs(8),
            pltpu.SemaphoreType.DMA((16,)),
            pltpu.SemaphoreType.DMA((7,)),
        ],
        compiler_params=params(1),
        name="feed_forward",
    )(gain2, own, mixed, own_cots, cots, feed)


TOP_GRADS, TOP_OUTS, TOP_BACK = 48, 32, 48

def attention_back_kernel(
    gain1,
    norm2_grads,
    own,
    grad_mixed_in,
    mixed_in,
    tokens_in,
    tables_in,
    start_in,
    acts_in,
    attended_in,
    logs_in,
    weights_in,
    halves,
    first_rows,
    outs,
    layer_out,
    token_grad,
    qkv_grad,
    out_grad,
    gate_up_grad,
    down_grad,
    early_out,
    late_out,
    grad_mixed,
    mixed,
    tokens,
    tables,
    start_lanes,
    acts,
    attended,
    logs,
    weights,
    rows,
    before,
    grad_out,
    grads_qkv,
    keys_turned,
    turns,
    parts,
    out_parts,
    grads,
    land,
    out_land,
    core_land,
    w_land,
    f_land,
    own_halves,
    total,
    boxes,
    late_boxes,
    g_sends,
    g_receives,
    s_sends,
    s_receives,
    o_sends,
    o_receives,
    k_sends,
    k_receives,
    w_sends,
    w_receives,
    f_sends,
    f_receives,
    a_sends,
    a_receives,
    l_sends,
    l_receives,
    local,
):
    a, r = Around(), Ring()
    gmail, mail, omail = Mail(g_sends, g_receives), Mail(s_sends, s_receives), Mail(o_sends, o_receives)
    kmail, wmail, fmail = Mail(k_sends, k_receives), Mail(w_sends, w_receives), Mail(f_sends, f_receives)
    amail, lmail = Mail(a_sends, a_receives), Mail(l_sends, l_receives)
    peers = a.peers() + a.to_rest[:1] + r.peers() + [r.to_zh_core]
    hail(peers)
    loads = {}
    for number, (name, source, target) in enumerate(
        (
            ("own", own, rows.at[a.me]),
            ("acts", acts_in, acts),
            ("attended", attended_in, attended),
            ("outs", outs, out_parts),
            ("weights", weights_in, weights),
            ("logs", logs_in, logs),
            ("start", start_in, start_lanes),
            ("half", halves.at[r.zh * 4 + r.x], own_halves.at[0]),
            ("other", halves.at[(1 - r.zh) * 4 + r.x], own_halves.at[1]),
            ("tables", tables_in, tables),
            ("before", first_rows, before),
            ("mixed", mixed_in, mixed),
            ("tokens", tokens_in, tokens),
            ("grad_mixed", grad_mixed_in, grad_mixed),
        )
    ):
        loads[name] = pltpu.make_async_copy(source, target, local.at[number])
        loads[name].start()

    def loaded(*names):
        for name in names:
            loads.pop(name).wait()

    loaded("own")
    hear(peers)
    gather = Gather(a, gmail, rows, TOP_GRADS)
    out_scatter = Scatter(a, omail, out_parts, out_land, TOP_OUTS)
    scatter = Scatter(a, mail, parts, land, TOP_BACK)
    early = EverySum(a, r, amail, boxes, EARLY_ROWS, NORM_ROWS)
    late = EverySum(a, r, lmail, late_boxes, NORM_ROWS, NORM_ROWS)
    feed_fold = Fold(r, fmail, halves, lambda side: own_halves[side], f_land)
    fold = Fold(r, wmail, core_land, lambda side: core_land[fold.place(side, 0)], w_land)

    def turn():
        loaded("acts", "attended")
        keys_turned[...] = acts[1].T
        turns[pl.ds(3 * LOCAL, LOCAL), :] = attended[...].T
        grads_qkv[1] = jnp.zeros((GROUP, LOCAL), F32)
        grads_qkv[2] = jnp.zeros((GROUP, LOCAL), F32)
        loaded("outs", "weights", "logs", "start")

    def back_project(y):
        chunk = rows[pl.ds(2 * y, 2)].reshape(QBLOCK, WIDTH)
        first = pl.multiple_of(y * QBLOCK, QBLOCK)
        grad_out[pl.ds(first, QBLOCK), :] = dot(chunk, weights[3]).astype(BF16)

    state = {}

    def attend(first, heads):
        count = first + QBLOCK
        span = pl.ds(first, QBLOCK)
        query = acts[0, span, :] * BF16(SCALE)
        given = grad_out[span, :]
        row = lax.broadcasted_iota(jnp.int32, (count, QBLOCK), 0)
        column = first + lax.broadcasted_iota(jnp.int32, (count, QBLOCK), 1)
        allow = (row <= column) & (row.astype(F32) >= start_lanes[pl.ds(0, 1), span])
        overlap = given.astype(F32) * attended[span, :].astype(F32)
        lane = lax.broadcasted_iota(jnp.int32, (QBLOCK, LANES), 1)
        inner = jnp.zeros((QBLOCK, LANES), F32)
        for head in range(*heads):
            summed = jnp.sum(only(head_lanes(head, QBLOCK), overlap), axis=1, keepdims=True)
            inner = jnp.where(lane == head, summed, inner)
        inner = inner.T[:8]
        head_row = lax.broadcasted_iota(jnp.int32, (8, QBLOCK), 0)
        head_rows = lax.broadcasted_iota(jnp.int32, (LOCAL, count), 0) // HEAD_DIM

        def one_head(head, turned_query):
            mask = head_lanes(head, QBLOCK)
            masked, masked_given = only(mask, query), only(mask, given)
            log = jnp.sum(only(head_row == head, logs[:, span]), axis=0, keepdims=True)
            mean = jnp.sum(only(head_row == head, inner), axis=0, keepdims=True)
            scores = dot_t(acts[1, pl.ds(0, count), :], masked)
            probs = only(allow, jnp.exp(scores - log))
            grad_probs = dot_t(acts[2, pl.ds(0, count), :], masked_given)
            grad_scores = (probs * (grad_probs - mean)).astype(BF16)
            grads_qkv[2, pl.ds(0, count), :] += dot(probs.astype(BF16), masked_given)
            grads_qkv[1, pl.ds(0, count), :] += dot(grad_scores, masked)
            keys = only(head_rows == head, keys_turned[:, pl.ds(0, count)])
            return turned_query + dot(keys, grad_scores)

        so_far = state.pop("attend", jnp.zeros((LOCAL, QBLOCK), F32))
        so_far = lax.fori_loop(*heads, one_head, so_far)
        if heads[1] < HEADS_DEV:
            state["attend"] = so_far
        else:
            grads_qkv[0, span, :] = so_far.T * SCALE

    def input_grad(y):
        if "tables" in loads:
            loaded("tables")
        first = pl.multiple_of(y * QBLOCK, QBLOCK)
        span = pl.ds(first, QBLOCK)
        back = jnp.zeros((QBLOCK, WIDTH), F32)
        new = []
        for c in range(3):
            pre = grads_qkv[c, span, :]
            if c < 2:
                pre = turned(pre, tables, first, -1.0)
            pre = pre.astype(BF16)
            new.append(jnp.sum(pre.astype(F32), axis=0, keepdims=True))
            back = back + dot_t(pre, weights[c])
            turns[pl.ds(c * LOCAL, LOCAL), span] = pre.T
        parts[pl.ds(2 * y, 2)] = back.astype(BF16).reshape(2, ROWS, WIDTH)
        state["bias"] = state.get("bias", 0.0) + jnp.concatenate(new, axis=0)

    def to_sibling(index):
        return kmail.copy(index, grads.at[index, 1 - r.core], core_land.at[index], r.to_core)

    def weight_grad(index, carry):
        columns = pl.ds(pl.multiple_of(index * 2 * ROWS, 2 * ROWS), 2 * ROWS)
        three = dot(
            turns[pl.ds(0, 3 * LOCAL), :], before[:, :, columns].reshape(GROUP, 2 * ROWS)
        )
        last = dot(turns[pl.ds(3 * LOCAL, LOCAL), :], rows[:, :, columns].reshape(GROUP, 2 * ROWS))
        for core in range(2):
            lanes = slice(core * ROWS, (core + 1) * ROWS)
            grads[index, core, pl.ds(0, 3 * LOCAL), :] = three[:, lanes].astype(BF16)
            grads[index, core, pl.ds(3 * LOCAL, LOCAL), :] = last[:, lanes].astype(BF16)
        to_sibling(index).start()
        return carry

    def weight_grads(first):
        if "before" in loads:
            loaded("before")
        lax.fori_loop(first, first + 2, weight_grad, 0)

    def core_sum(index, carry):
        to_sibling(index).wait()
        core_land[index] = added(grads[index, r.core], core_land[index]).astype(BF16)
        return carry

    def feed_cross():
        loaded("other")
        feed_fold.cross()

    def feed_result():
        loaded("half")
        feed_fold.near()
        feed_sum = feed_fold.result()
        gate_up_grad[...] = feed_sum[: 2 * UNITS]
        down_grad[...] = feed_sum[2 * UNITS :]

    def weight_result():
        fold.near()
        shard = fold.result()
        for c in range(3):
            qkv_grad[c] = shard[c * LOCAL : (c + 1) * LOCAL].T
        out_grad[...] = shard[3 * LOCAL :]

    def layer_result():
        loaded("mixed")
        out_scatter.finish(total)
        layer_out[...] = (mixed[...] + total[...]).astype(BF16)

    def norm():
        loaded("tokens", "grad_mixed")
        scatter.finish(total)
        normal, rinv = normalized(tokens[...].astype(F32))
        back, gain_grad, shift_grad = norm_back(total[...], normal, rinv, gain1[...])
        late.first(by_lanes(gain_grad, shift_grad))
        token_grad[...] = (grad_mixed[...] + back).astype(BF16)

    def by_lanes(*values):
        values = jnp.concatenate(values, axis=0)
        width = values.shape[1]
        return jnp.concatenate([values[:, k : k + LANES] for k in range(0, width, LANES)], axis=0)

    def early_sums():
        spare = jnp.zeros((EARLY_ROWS - NORM_ROWS - 3 * LOCAL // LANES, LANES), F32)
        parts_now = [by_lanes(norm2_grads[...]), by_lanes(state["bias"]), spare]
        early.first(jnp.concatenate(parts_now, axis=0))

    def early_result():
        early_out[...] = early.result()

    def late_result():
        late_out[...] = late.result()

    G, O, S = gather.step, out_scatter.step, scatter.step

    def P(y):
        return partial(back_project, y)

    def A(q, *heads):
        return partial(attend, q * QBLOCK, heads)

    def I(y):
        return partial(input_grad, y)

    def W(index):
        return partial(weight_grads, 2 * index)

    def K(index):
        return partial(lax.fori_loop, 4 * index, 4 * index + 4, core_sum, 0)

    for step in (
        partial(gather.send, *range(6)), partial(feed_fold.send, *range(6)), turn, G(0), G(1), G(2),
        G(3), G(4), G(5), P(a.y), G(7), G(6), out_scatter.direct_across, G(8), G(10), G(11),
        out_scatter.direct_down, G(9), out_scatter.direct_up, G(15), G(16), G(12), P(a.y_down),
        P(a.y_up), G(14), O(2), G(13), P(a.y_far), A(0, 0, 4), A(1, 0, 2), A(1, 2, 4), O(0),
        A(2, 0, 1), O(17), A(2, 1, 2), A(2, 2, 3), feed_cross, O(4), A(2, 3, 4), O(3), A(3, 0, 1),
        A(3, 1, 2), A(3, 2, 3), A(3, 3, 4), I(a.y_far), scatter.from_far_pair, I(a.y_up),
        scatter.from_up_pair, I(a.y_down), scatter.from_down_pair, I(a.y), O(5),
        scatter.from_across, W(0), out_scatter.over_last, W(1), W(2), S(1), W(3), S(17), S(2), K(0),
        feed_result, O(1), K(1), S(4), partial(fold.send, *range(6)), early_sums, S(0), S(3),
        scatter.over_inner, S(5), scatter.over_last, fold.cross, out_scatter.over_inner, norm,
        early.second, weight_result, late.second, layer_result, early.third, late.third,
        early.fourth, late.fourth, early_result, late_result,
    ):
        step()
    for some in (gmail, mail, omail, kmail, wmail, fmail, amail, lmail):
        some.finish()


def attention_backward(*operands):
    group = (TENSOR, ROWS, WIDTH)
    block, feed_block = (4 * LOCAL, ROWS), (3 * UNITS, ROWS)
    return pl.pallas_call(
        attention_back_kernel,
        out_shape=(
            jax.ShapeDtypeStruct((ROWS, WIDTH), BF16),
            jax.ShapeDtypeStruct((ROWS, WIDTH), BF16),
            jax.ShapeDtypeStruct((3, ROWS, LOCAL), F32),
            jax.ShapeDtypeStruct((LOCAL, ROWS), F32),
            jax.ShapeDtypeStruct((2 * UNITS, ROWS), F32),
            jax.ShapeDtypeStruct((UNITS, ROWS), F32),
            jax.ShapeDtypeStruct((EARLY_ROWS, LANES), F32),
            jax.ShapeDtypeStruct((NORM_ROWS, LANES), F32),
        ),
        in_specs=vmem(2) + anywhere(13),
        out_specs=tuple(vmem(8)),
        scratch_shapes=[
            pltpu.VMEM((ROWS, WIDTH), F32),
            pltpu.VMEM((ROWS, WIDTH), F32),
            pltpu.VMEM((ROWS, WIDTH), BF16),
            pltpu.VMEM((3, GROUP, LANES), F32),
            pltpu.VMEM((8, GROUP), F32),
            pltpu.VMEM((3, GROUP, LOCAL), BF16),
            pltpu.VMEM((GROUP, LOCAL), BF16),
            pltpu.VMEM((8, GROUP), F32),
            pltpu.VMEM((4, WIDTH, LOCAL), BF16),
            pltpu.VMEM(group, BF16),
            pltpu.VMEM(group, BF16),
            pltpu.VMEM((GROUP, LOCAL), BF16),
            pltpu.VMEM((3, GROUP, LOCAL), F32),
            pltpu.VMEM((LOCAL, GROUP), BF16),
            pltpu.VMEM((4 * LOCAL, GROUP), BF16),
            pltpu.VMEM(group, BF16),
            pltpu.VMEM(group, BF16),
            pltpu.VMEM((8, 2) + block, BF16),
            pltpu.VMEM((scatter_rows_needed(TOP_BACK), WIDTH), BF16),
            pltpu.VMEM((scatter_rows_needed(TOP_OUTS), WIDTH), BF16),
            pltpu.VMEM((8,) + block, BF16),
            pltpu.VMEM((FOLD_MAILS,) + block, BF16),
            pltpu.VMEM((FOLD_MAILS,) + feed_block, BF16),
            pltpu.VMEM((2,) + feed_block, BF16),
            pltpu.VMEM((ROWS, WIDTH), F32),
            pltpu.VMEM((SUM_BOXES, EARLY_ROWS, LANES), F32),
            pltpu.VMEM((SUM_BOXES, NORM_ROWS, LANES), F32),
            *pairs(GATHER_MAILS),
            *pairs(SCATTER_MAILS),
            *pairs(SCATTER_MAILS),
            *pairs(8),
            *pairs(FOLD_MAILS),
            *pairs(FOLD_MAILS),
            *pairs(SUM_MAILS),
            *pairs(SUM_MAILS),
            pltpu.SemaphoreType.DMA((14,)),
        ],
        compiler_params=params(2),
        name="attention_backward",
    )(*operands)


def results_kernel(
    layer_in, token_in, qkv_in, out_in, gate_up_in, down_in, early, late, layer, token, qkv, out, gate_up, down, *norms
):
    bias = norms[4]
    for source, target in (
        (layer_in, layer),
        (token_in, token),
        (qkv_in, qkv),
        (out_in, out),
        (gate_up_in, gate_up),
        (down_in, down),
    ):
        target[...] = source[...]
    for k in range(WIDTH // LANES):
        for number in range(2):
            norms[number][pl.ds(k, 1), :] = late[pl.ds(2 * k + number, 1), :]
            norms[2 + number][pl.ds(k, 1), :] = early[pl.ds(2 * k + number, 1), :]
    for k in range(LOCAL // LANES):
        bias[:, pl.ds(k * LANES, LANES)] = early[pl.ds(NORM_ROWS + 3 * k, 3), :]


def results(*values):
    shapes = [jax.ShapeDtypeStruct(item.shape, item.dtype) for item in values[:6]]
    shapes += [jax.ShapeDtypeStruct((WIDTH // LANES, LANES), F32)] * 4
    shapes.append(jax.ShapeDtypeStruct((3, LOCAL), F32))
    return pl.pallas_call(
        results_kernel,
        out_shape=tuple(shapes),
        in_specs=vmem(8),
        out_specs=tuple(vmem(len(shapes))),
        name="results",
    )(*values)


def body(
    tokens,
    doc_ids,
    qkv_weight,
    qkv_bias,
    out_weight,
    norm1_gain,
    norm1_shift,
    norm2_gain,
    norm2_shift,
    gate_up_weight,
    down_weight,
    cotangent,
):
    norms = [item[None] for item in (norm1_gain, norm1_shift, norm2_gain, norm2_shift)]
    frequency = jnp.power(10000.0, -2.0 * jnp.arange(ROT // 2, dtype=F32) / ROT)
    frequency = jnp.broadcast_to(frequency[:, None], (ROT // 2, LANES))
    gate_up = jnp.swapaxes(gate_up_weight, 1, 2).reshape(2 * UNITS, ROWS)
    normed2, start, logs, mixed, tables, acts, attended, rows, weights, cots, feed = attention_forward(
        tokens,
        doc_ids[None],
        qkv_bias,
        out_weight,
        norms,
        frequency,
        qkv_weight,
        gate_up,
        down_weight,
        cotangent,
    )
    grad_mixed, branch_grad, norm2_grads, halves, outs = feed_forward(
        norms[2], normed2, mixed, cotangent, cots, feed
    )
    backward = attention_backward(
        norms[0],
        norm2_grads,
        branch_grad,
        grad_mixed,
        mixed,
        tokens,
        tables,
        start,
        acts,
        attended,
        logs,
        weights,
        halves,
        rows,
        outs,
    )
    layer_out, token_grad, qkv_grad, out_grad, gate_up_grad, down_grad, *sums = results(*backward)
    return (
        layer_out,
        token_grad,
        qkv_grad,
        sums[4],
        out_grad,
        sums[0].reshape(WIDTH),
        sums[1].reshape(WIDTH),
        sums[2].reshape(WIDTH),
        sums[3].reshape(WIDTH),
        jnp.swapaxes(gate_up_grad.reshape(2, UNITS, ROWS), 1, 2),
        down_grad,
    )


def solution(mesh):
    in_specs = (
        P(("dp", "tensor"), None),
        P(("dp", "tensor")),
        P(None, "dp", "tensor"),
        P(None, "tensor"),
        P("tensor", "dp"),
        P(),
        P(),
        P(),
        P(),
        P(None, "dp", "tensor"),
        P("tensor", "dp"),
        P(("dp", "tensor"), None),
    )
    out_specs = (
        P(("dp", "tensor"), None),
        P(("dp", "tensor"), None),
        P(None, "dp", "tensor"),
        P(None, "tensor"),
        P("tensor", "dp"),
        P(),
        P(),
        P(),
        P(),
        P(None, "dp", "tensor"),
        P("tensor", "dp"),
    )
    return jax.shard_map(body, mesh=mesh, in_specs=in_specs, out_specs=out_specs, check_vma=False)
```

```python
from functools import partial

import jax
import jax.numpy as jnp
import numpy as np
from jax import lax
from jax.experimental import pallas as pl
from jax.experimental.pallas import tpu as pltpu
from jax.sharding import PartitionSpec as P

HEAD_DIM = 64
ROT = 16
DOCS = 4
EPS = 1e-05
SCALE = HEAD_DIM ** (-0.5)

ROWS = 128
WIDTH = 2048
TENSOR = 8
GROUP = ROWS * TENSOR
HALF = ROWS // 2
HEADS_DEV = 4
LOCAL = HEADS_DEV * HEAD_DIM
QBLOCK = 256
UNITS = 704
LANES = 128
MESH = pl.DeviceIdType.MESH
BF16 = jnp.bfloat16
F32 = jnp.float32
VMEM_LIMIT = 62 * 2**20


class Around:
    def __init__(self):
        dp, tensor = lax.axis_index("dp"), lax.axis_index("tensor")
        y, z = tensor // 2, lax.rem(tensor, 2)
        up, down, far = lax.rem(y + 1, 4), lax.rem(y + 3, 4), lax.rem(y + 2, 4)
        other = 1 - z
        self.me, self.across = y * 2 + z, y * 2 + other
        self.up, self.down, self.far = up * 2 + z, down * 2 + z, far * 2 + z
        self.up_o, self.down_o, self.far_o = up * 2 + other, down * 2 + other, far * 2 + other
        self.y, self.z = y, z
        self.y_up, self.y_down, self.y_far = up, down, far
        self.to_up, self.to_down, self.to_across = (dp, self.up), (dp, self.down), (dp, self.across)
        self.to_rest = [(dp, slot) for slot in (self.far, self.up_o, self.down_o, self.far_o)]

    def peers(self):
        return [self.to_up, self.to_down, self.to_across]


class Ring:
    def __init__(self):
        dp, tensor = lax.axis_index("dp"), lax.axis_index("tensor")
        zh, x, core = dp // 8, lax.rem(dp // 2, 4), lax.rem(dp, 2)
        self.zh, self.x, self.core, self.dp, self.tensor = zh, x, core, dp, tensor
        self.xs = [lax.rem(x + step, 4) for step in range(4)]
        self.to_x = [(self.index(zh, self.xs[step], core), tensor) for step in range(4)]
        self.to_zh = (self.index(1 - zh, x, core), tensor)
        self.to_core = (self.index(zh, x, 1 - core), tensor)
        self.to_zh_core = (self.index(1 - zh, x, 1 - core), tensor)

    def index(self, zh, x, core):
        return zh * 8 + x * 2 + core

    def peers(self):
        return self.to_x[1:] + [self.to_zh, self.to_core]


def hail(peers):
    barrier = pltpu.get_barrier_semaphore()
    for peer in peers:
        pl.semaphore_signal(barrier, inc=1, device_id=peer, device_id_type=MESH)


def hear(peers):
    pl.semaphore_wait(pltpu.get_barrier_semaphore(), len(peers))


class Mail:
    def __init__(self, sends, receives):
        self.sends, self.receives = sends, receives
        self.out = []

    def copy(self, number, source, target, device):
        return pltpu.make_async_remote_copy(
            src_ref=source,
            dst_ref=target,
            send_sem=self.sends.at[number],
            recv_sem=self.receives.at[number],
            device_id=device,
            device_id_type=MESH,
        )

    def send(self, number, source, target, device):
        copy = self.copy(number, source, target, device)
        copy.start()
        self.out.append(copy)

    def landed(self, number, target, device):
        self.copy(number, target, target, device).wait_recv()

    def finish(self):
        for copy in self.out:
            copy.wait_send()
        self.out = []


MIDDLE = {64: 96, 48: 96, 32: 80}
GATHER_MAILS = 17


class Gather:
    def __init__(self, around, mail, rows, top, own=None):
        a, middle = around, MIDDLE[top]
        self.mail, self.rows, self.own = mail, rows, own
        self.messages = [
            (a.to_up, a.me, 0, HALF, a.down),
            (a.to_down, a.me, HALF, ROWS, a.up),
            (a.to_across, a.me, top, ROWS, a.across),
            (a.to_up, a.me, HALF, ROWS, a.down),
            (a.to_down, a.me, 0, HALF, a.up),
            (a.to_across, a.me, 0, top, a.across),
            (a.to_up, a.down, 0, HALF, a.far),
            (a.to_across, a.down, 0, top, a.down_o),
            (a.to_down, a.up, HALF, ROWS, a.far),
            (a.to_up, a.across, top, middle, a.down_o),
            (a.to_down, a.across, middle, ROWS, a.up_o),
            (a.to_across, a.up, 0, top, a.up_o),
            (a.to_across, a.far, 0, top, a.far_o),
            (a.to_up, a.down_o, top, middle, a.far_o),
            (a.to_down, a.up_o, middle, ROWS, a.far_o),
            (a.to_up, a.across, middle, ROWS, a.down_o),
            (a.to_down, a.across, top, middle, a.up_o),
        ]

    def part(self, slot, first, last):
        return self.rows.at[slot, pl.ds(first, last - first)]

    def send(self, *numbers):
        for number in numbers:
            device, slot, first, last, _ = self.messages[number]
            target = source = self.part(slot, first, last)
            if number < 6 and self.own is not None:
                source = self.own.at[pl.ds(first, last - first)]
            self.mail.send(number, source, target, device)

    def step(self, number):
        return partial(self.on, number)

    def on(self, number):
        device, _, first, last, slot = self.messages[number]
        self.mail.landed(number, self.part(slot, first, last), device)
        followers = {0: (6, 7), 1: (8,), 2: (9, 10, 15, 16), 4: (11,), 6: (12,), 9: (13,), 10: (14,)}
        self.send(*followers.get(number, ()))


def added(*terms):
    total = terms[0].astype(F32)
    for term in terms[1:]:
        total = total + term.astype(F32)
    return total


SCATTER_MAILS = 21


def scatter_boxes(top):
    middle = MIDDLE[top]
    last, inner, rest = ROWS - middle, middle - top, HALF - top
    counts = (last, inner, top, HALF, top, top, last, inner, HALF, top)
    counts += (top, inner, last, HALF, top, top, inner, rest, rest, rest, last, inner, last)
    order = [*range(17), 20, 17, 18, 19, 21, 22]
    firsts = [0] * len(counts)
    for before, number in zip(order, order[1:]):
        firsts[number] = firsts[before] + counts[before]
    return counts, tuple(firsts)


def scatter_rows_needed(top):
    return sum(scatter_boxes(top)[0])


class Scatter:
    def __init__(self, around, mail, parts, land, top):
        self.a, self.mail, self.parts, self.land, self.top = around, mail, parts, land, top
        self.middle = MIDDLE[top]
        self.counts, self.firsts = scatter_boxes(top)
        self.crossed = False

    def part(self, slot, first, last):
        return self.parts.at[slot, pl.ds(first, last - first)]

    def box(self, number):
        return self.land.at[pl.ds(self.firsts[number], self.counts[number])]

    def got(self, number):
        self.mail.landed(number, self.box(number), self.a.to_up)

    def fold(self, stage, slot, first, *others):
        terms = [self.part(slot, first, first + self.counts[stage])[...], self.box(stage)[...]]
        terms += [self.box(other)[...] for other in others]
        self.box(stage)[...] = added(*terms).astype(BF16)

    def direct(self, *numbers):
        a, top, middle = self.a, self.top, self.middle
        messages = {
            0: (a.far_o, middle, a.to_up),
            1: (a.far_o, top, a.to_down),
            2: (a.far_o, 0, a.to_across),
            3: (a.far, HALF, a.to_up),
            17: (a.far, top, a.to_down),
            4: (a.up_o, 0, a.to_across),
            7: (a.up_o, top, a.to_up),
            5: (a.down_o, 0, a.to_across),
            6: (a.down_o, middle, a.to_down),
            18: (a.up, top, a.to_up),
            8: (a.down, HALF, a.to_down),
            9: (a.across, 0, a.to_across),
        }
        for number in numbers:
            slot, first, device = messages[number]
            source = self.part(slot, first, first + self.counts[number])
            self.mail.send(number, source, self.box(number), device)

    def from_far_pair(self):
        self.direct(0, 1, 2, 3, 17)

    def from_up_pair(self):
        self.direct(7, 4, 18)

    def from_down_pair(self):
        self.direct(6, 5, 8)

    def from_across(self):
        self.direct(9)

    def direct_up(self):
        self.direct(0, 3, 7, 18)

    def direct_down(self):
        self.direct(1, 17, 6, 8)

    def direct_across(self):
        self.direct(2, 4, 5, 9)

    def step(self, number):
        return partial(self.on, number)

    def on(self, number):
        a, box = self.a, self.box
        follower, slot, first, device, *others = {
            1: (11, a.down_o, self.top, a.to_down),
            0: (12, a.up_o, self.middle, a.to_up),
            2: (10, a.far, 0, a.to_down),
            3: (13, a.up, HALF, a.to_up),
            17: (19, a.down, self.top, a.to_down),
            4: (14, a.up, 0, a.to_up),
            5: (15, a.down, 0, a.to_down, 10),
        }[number]
        for other in (number, *others):
            self.got(other)
        self.fold(number, slot, first, *others)
        self.mail.send(follower, box(number), box(follower), device)

    def over(self, number, made, first, *landed):
        for other in landed:
            self.got(other)
        own = self.part(self.a.across, first, first + self.counts[number])
        terms = [own[...]] + [self.box(other)[...] for other in landed]
        self.box(made)[...] = added(*terms).astype(BF16)
        self.mail.send(number, self.box(made), self.box(number), self.a.to_across)

    def over_inner(self):
        self.over(16, 21, self.top, 7, 11)

    def over_last(self):
        self.over(20, 22, self.middle, 6, 12)

    def all_direct(self):
        self.direct(0, 1, 2, 3, 17, 7, 4, 6, 5, 18, 8, 9)

    def boxed(self, number, first, last):
        return self.land[pl.ds(self.firsts[number] + first, last - first), :]

    def finish_top(self, total):
        a, top = self.a, self.top
        for number in (9, 14, 15, 18, 19):
            self.got(number)
        if not self.crossed:
            self.got(16)
            self.crossed = True
        total[pl.ds(0, top), :] = added(
            self.part(a.me, 0, top)[...], *(self.box(k)[...] for k in (9, 14, 15))
        )
        total[pl.ds(top, HALF - top), :] = added(
            self.part(a.me, top, HALF)[...],
            self.box(18)[...],
            self.box(19)[...],
            self.boxed(16, 0, HALF - top),
        )

    def finish_low(self, total):
        for number in (8, 13, 20):
            self.got(number)
        if not self.crossed:
            self.got(16)
            self.crossed = True
        total[pl.ds(HALF, HALF), :] = added(
            self.part(self.a.me, HALF, ROWS)[...],
            self.box(8)[...],
            self.box(13)[...],
            self.boxed(16, HALF - self.top, ROWS - self.top),
        )


class Spread:
    def __init__(self, ring, mail, block, own_shard=None):
        r = self.r = ring
        self.mail, self.block, self.own = mail, block, own_shard
        own, cross = (r.zh, r.x), (1 - r.zh, r.x)
        self.messages = [(r.to_zh, own, cross)]
        self.messages += [(r.to_x[k], own, (r.zh, r.xs[4 - k])) for k in (1, 2, 3)]
        self.messages += [(r.to_x[k], cross, (1 - r.zh, r.xs[4 - k])) for k in (1, 2, 3)]
        self.messages += [(r.to_core, own, own), (r.to_core, cross, cross)]
        self.messages += [(r.to_core, self.messages[k][2], self.messages[k][2]) for k in range(1, 7)]

    def send(self, number):
        device, place, _ = self.messages[number]
        block = self.block(*place, self.r.core)
        source = self.own if self.own is not None and number in (0, 1, 2, 3, 7) else block
        self.mail.send(number, source, block, device)

    def step(self, number):
        return partial(self.on, number)

    def begin(self):
        for number in (0, 1, 3, 2, 7):
            self.send(number)

    def on(self, number):
        device, _, place = self.messages[number]
        core = self.r.core if number < 7 else 1 - self.r.core
        self.mail.landed(number, self.block(*place, core), device)
        if number == 0:
            for follower in (4, 6, 5, 8):
                self.send(follower)
        elif number < 7:
            self.send(number + 8)

    def finish(self):
        for number in range(7, SPREAD_MAILS):
            self.on(number)


SPREAD_MAILS = 15
FOLDS = [(side, step) for step in (1, 3, 2, 0) for side in (1, 0)]


class Fold:
    def __init__(self, ring, mail, grads, own, land):
        self.r, self.mail, self.grads, self.own, self.land = ring, mail, grads, own, land

    def place(self, side, step):
        zh = 1 - self.r.zh if side else self.r.zh
        return zh * 4 + self.r.xs[step]

    def send(self, *numbers):
        for number in numbers:
            side, step = FOLDS[number]
            source = self.grads.at[self.place(side, step)]
            self.mail.send(number, source, self.land.at[number], self.r.to_x[step])

    def cross(self):
        for number in (0, 2, 4):
            self.mail.landed(number, self.land.at[number], self.r.to_core)
        self.land[0] = added(self.own(1), self.land[0], self.land[2], self.land[4]).astype(BF16)
        self.mail.send(6, self.land.at[0], self.land.at[6], self.r.to_zh)

    def near(self):
        for number in (1, 3, 5):
            self.mail.landed(number, self.land.at[number], self.r.to_core)

    def result(self):
        self.mail.landed(6, self.land.at[6], self.r.to_core)
        land = self.land
        return added(self.own(0), land[1], land[3], land[5], land[6])


FOLD_MAILS = 7

SUM_ROWS, NORM_ROWS = 72, 64
SUM_BOXES, SUM_MAILS = 14, 13


class EverySum:
    def __init__(self, mail, boxes, stages):
        self.mail, self.boxes, self.stages = mail, boxes, stages

    def give(self, stage, values):
        base, count, mine, _, peers = self.stages[stage]
        view = pl.ds(0, count)
        self.boxes[base + mine, view] = values
        for number, peer in enumerate(peers):
            box = self.boxes.at[base + mine, view]
            self.mail.send(base + number, box, box, peer)

    def take(self, stage):
        base, count, _, sources, peers = self.stages[stage]
        view = pl.ds(0, count)
        for number, source in enumerate(sources):
            self.mail.landed(base + number, self.boxes.at[base + source, view], peers[0])
        result = self.boxes[base, view]
        for k in range(1, len(peers) + 1):
            result = result + self.boxes[base + k, view]
        return result

    def first(self, values):
        self.give(0, values)

    def second(self):
        self.give(1, self.take(0))

    def third(self):
        self.kept = self.take(1)
        self.give(2, self.kept[: self.stages[2][1]])

    def fourth(self):
        self.give(3, self.take(2))


def sum_stages(a, r):
    crossed = 1 - r.zh
    place = r.zh * 2 + r.core
    sources = [crossed * 2 + r.core, r.zh * 2 + 1 - r.core, crossed * 2 + 1 - r.core]
    y_sources, y_peers = [a.y_down, a.y_far, a.y_up], [a.to_up, a.to_rest[0], a.to_down]
    return [
        (0, SUM_ROWS, r.x, [r.xs[3], r.xs[2], r.xs[1]], r.to_x[1:]),
        (4, SUM_ROWS, place, sources, [r.to_zh, r.to_core, r.to_zh_core]),
        (8, NORM_ROWS, a.y, y_sources, y_peers),
        (12, NORM_ROWS, a.z, [1 - a.z], [a.to_across]),
    ]


def dot(left, right):
    return lax.dot_general(left, right, (((1,), (0,)), ((), ())), preferred_element_type=F32)


def dot_t(left, right):
    return lax.dot_general(left, right, (((1,), (1,)), ((), ())), preferred_element_type=F32)


def normalized(values):
    centred = values - jnp.mean(values, axis=1, keepdims=True)
    variance = jnp.mean(centred * centred, axis=1, keepdims=True)
    rinv = lax.rsqrt(variance + EPS)
    return centred * rinv, rinv


def norm_sums(incoming, normal):
    return jnp.sum(incoming * normal, axis=0, keepdims=True), jnp.sum(incoming, axis=0, keepdims=True)


def norm_back(incoming, normal, rinv, gain):
    scaled = incoming * gain
    inner = scaled - jnp.mean(scaled, axis=1, keepdims=True)
    return rinv * (inner - normal * jnp.mean(scaled * normal, axis=1, keepdims=True))


def turned(values, tables, first, sign):
    rows = pl.ds(first, values.shape[0])
    cosine, minus, plus = tables[0, rows], tables[1, rows], tables[2, rows]
    halves = []
    for lane in range(0, LOCAL, LANES):
        part = values[:, lane : lane + LANES]
        left = pltpu.roll(part, LANES - ROT // 2, 1)
        right = pltpu.roll(part, ROT // 2, 1)
        halves.append(part * cosine + sign * (left * minus + right * plus))
    return jnp.concatenate(halves, axis=1)


def head_lanes(head, rows):
    return lax.broadcasted_iota(jnp.int32, (rows, LOCAL), 1) // HEAD_DIM == head


def only(mask, values):
    return jnp.where(mask, values, jnp.zeros_like(values))


def place_rows(id_rows, frequency, tables, start_rows, start_lanes):
    ids = jnp.max(id_rows[...], axis=1)
    shape = (TENSOR, ROWS)
    index = lax.broadcasted_iota(jnp.int32, shape, 0) * ROWS
    index = (index + lax.broadcasted_iota(jnp.int32, shape, 1)).astype(F32)
    offset = jnp.zeros(shape, F32)
    for number in range(1, DOCS):
        before = ((ids >= 0) & (ids < number)).astype(F32)
        count = jnp.sum(jnp.sum(before, axis=1, keepdims=True), axis=0, keepdims=True)
        offset = jnp.where(ids == number, count, offset)
    start = jnp.where(ids >= 0, offset, index)
    position = index - offset

    def along(values):
        return jnp.concatenate([values[t : t + 1] for t in range(TENSOR)], axis=1)

    angle = frequency[:, :1] * along(position)
    cosine, sine = jnp.cos(angle), jnp.sin(angle)
    none = jnp.zeros_like(sine)
    rest = (HEAD_DIM - ROT) // 8
    columns = (
        [cosine, cosine] + [jnp.ones_like(sine)] * rest,
        [-sine, none] + [none] * rest,
        [none, sine] + [none] * rest,
    )
    for number, parts in enumerate(columns):
        tables[number] = jnp.concatenate(parts + parts, axis=0).T
    lanes = jnp.broadcast_to(along(start), (8, GROUP))
    start_lanes[...] = lanes
    start_rows[...] = jnp.concatenate([lanes] * (LANES // 8), axis=0).T


def vmem(count):
    return [pl.BlockSpec(memory_space=pltpu.VMEM)] * count


def anywhere(count):
    return [pl.BlockSpec(memory_space=pl.ANY)] * count


def pairs(count):
    return [pltpu.SemaphoreType.DMA((count,)), pltpu.SemaphoreType.DMA((count,))]


def params(collective):
    return pltpu.CompilerParams(
        collective_id=collective, has_side_effects=True, vmem_limit_bytes=VMEM_LIMIT
    )


TOP_ROWS, TOP_COTS, TOP_BRANCH = 48, 32, 48


def attention_kernel(
    tokens,
    ids,
    bias,
    out_shard,
    gain1,
    shift1,
    gain2,
    shift2,
    frequency,
    qkv_shard,
    gate_up,
    down,
    own_cots,
    normed2,
    start_lanes,
    logs,
    mixed_kept,
    tables_kept,
    acts_kept,
    attended_kept,
    rows_kept,
    weights_kept,
    cots,
    feed,
    rows,
    weights,
    feed_own,
    cots_own,
    tables,
    acts,
    attended,
    mixed,
    id_rows,
    start_rows,
    parts,
    land,
    total,
    r_sends,
    r_receives,
    c_sends,
    c_receives,
    b_sends,
    b_receives,
    w_sends,
    w_receives,
    f_sends,
    f_receives,
    i_sends,
    i_receives,
    local,
):
    a, r = Around(), Ring()
    rmail, cmail, bmail = Mail(r_sends, r_receives), Mail(c_sends, c_receives), Mail(b_sends, b_receives)
    wmail, fmail, imail = Mail(w_sends, w_receives), Mail(f_sends, f_receives), Mail(i_sends, i_receives)
    peers = a.peers() + a.to_rest + r.peers()
    hail(peers)

    def weight_block(zh, x, core):
        first = pl.multiple_of(r.index(zh, x, core) * ROWS, ROWS)
        return weights.at[:, pl.ds(first, ROWS), :]

    mine = pl.multiple_of(r.dp * ROWS, ROWS)
    loads = [
        pltpu.make_async_copy(qkv_shard, weights.at[pl.ds(0, 3), pl.ds(mine, ROWS)], local.at[0]),
        pltpu.make_async_copy(gate_up, feed_own.at[pl.ds(0, 2 * UNITS)], local.at[1]),
        pltpu.make_async_copy(down, feed_own.at[pl.ds(2 * UNITS, UNITS)], local.at[2]),
        pltpu.make_async_copy(own_cots, cots_own, local.at[3]),
    ]
    for copy in loads:
        copy.start()
    id_rows[a.me] = jnp.broadcast_to(ids[...], (8, ROWS))
    weights[3, pl.ds(mine, ROWS), :] = out_shard[...].T
    normal, _ = normalized(tokens[...].astype(F32))
    rows[a.me] = (normal * gain1[...] + shift1[...]).astype(BF16)
    hear(peers)

    group = [
        (0, a.to_up, a.down),
        (1, a.to_down, a.up),
        (2, a.to_across, a.across),
        (3, a.to_rest[0], a.far),
        (4, a.to_rest[1], a.down_o),
        (5, a.to_rest[2], a.up_o),
        (6, a.to_rest[3], a.far_o),
    ]
    gather = Gather(a, rmail, rows, TOP_ROWS)
    others = Gather(a, cmail, cots, TOP_COTS, cots_own)
    spread = Spread(r, wmail, weight_block)
    feeds = Spread(r, fmail, lambda zh, x, core: feed.at[r.index(zh, x, core)], feed_own)
    scatter = Scatter(a, bmail, parts, land, TOP_BRANCH)
    started = []

    def keep(source, target, number):
        copy = pltpu.make_async_copy(source, target, local.at[number])
        copy.start()
        started.append(copy)

    def begin():
        for number, device, _ in group:
            imail.send(number, id_rows.at[a.me], id_rows.at[a.me], device)
        for number in (0, 1, 2):
            gather.send(number)
        loads[0].wait()
        spread.begin()
        for number in (3, 4, 5):
            gather.send(number)
        for copy in loads[1:]:
            copy.wait()
        keep(feed_own, feed.at[r.dp], 4)
        keep(cots_own, cots.at[a.me], 5)

    def place():
        for number, _, slot in group:
            imail.landed(number, id_rows.at[slot], a.to_up)
        place_rows(id_rows, frequency, tables, start_rows, start_lanes)
        keep(tables, tables_kept, 6)

    def P(y):
        return partial(project, y)

    def project(y):
        first = pl.multiple_of(y * QBLOCK, QBLOCK)
        chunk = rows[pl.ds(2 * y, 2)].reshape(QBLOCK, WIDTH)
        for c in range(3):
            pre = dot(chunk, weights[c]) + bias[pl.ds(c, 1), :]
            if c < 2:
                pre = turned(pre, tables, first, 1.0)
            acts[c, pl.ds(first, QBLOCK), :] = pre.astype(BF16)

    state = {}

    def A(q, *heads):
        return partial(attend, q * QBLOCK, heads)

    def attend(first, heads):
        count = first + QBLOCK
        query = acts[0, pl.ds(first, QBLOCK), :] * BF16(SCALE)
        row = first + lax.broadcasted_iota(jnp.int32, (QBLOCK, count), 0)
        column = lax.broadcasted_iota(jnp.int32, (QBLOCK, count), 1)
        start = start_rows[pl.ds(first, QBLOCK), pl.ds(0, 1)]
        allow = (column <= row) & (column.astype(F32) >= start)
        lane = lax.broadcasted_iota(jnp.int32, (QBLOCK, LANES), 1)

        def one_head(head, carry):
            out, log = carry
            masked = only(head_lanes(head, QBLOCK), query)
            scores = dot_t(masked, acts[1, pl.ds(0, count), :])
            scores = jnp.where(allow, scores, -1e30)
            highest = jnp.max(scores, axis=1, keepdims=True)
            expon = jnp.exp(scores - highest)
            sums = jnp.sum(expon, axis=1, keepdims=True)
            values = only(head_lanes(head, count), acts[2, pl.ds(0, count), :])
            out = out + dot(expon.astype(BF16), values) / sums
            log = jnp.where(lane == head, highest + jnp.log(sums), log)
            return out, log

        zeros = (jnp.zeros((QBLOCK, LOCAL), F32), jnp.zeros((QBLOCK, LANES), F32))
        carry = lax.fori_loop(*heads, one_head, state.pop("attend", zeros))
        if heads[1] < HEADS_DEV:
            state["attend"] = carry
            return
        out = carry[0].astype(BF16)
        attended[pl.ds(first, QBLOCK), :] = out
        logs[:, pl.ds(first, QBLOCK)] = carry[1].T[:8]
        branch = dot_t(out, weights[3]).astype(BF16)
        parts[first // ROWS] = branch[:ROWS]
        parts[first // ROWS + 1] = branch[ROWS:]

    def branch_sums():
        keep(rows, rows_kept, 7)
        keep(weights, weights_kept, 8)
        keep(acts, acts_kept, 9)
        keep(attended, attended_kept, 10)
        scatter.all_direct()

    def norm_half(first, number):
        half = pl.ds(first, HALF)
        after = tokens[half, :].astype(F32) + total[half, :]
        mixed[half, :] = after
        keep(mixed.at[half], mixed_kept.at[half], number)
        normal, _ = normalized(after)
        normed2[half, :] = (normal * gain2[...] + shift2[...]).astype(BF16)

    def norm_top():
        scatter.finish_top(total)
        norm_half(0, 11)

    def norm_low():
        scatter.finish_low(total)
        norm_half(HALF, 12)

    R, C, B, w, f = gather.step, others.step, scatter.step, spread.step, feeds.step
    C_up, C_down, C_across = (partial(others.send, *two) for two in ((0, 3), (1, 4), (2, 5)))
    for step in (
        begin, place, R(0), R(1), w(1), w(3), R(2), R(3), R(4), w(2), w(0), R(6), R(8), C_across,
        R(5), feeds.begin, R(10), C_down, R(9), C_up, R(7), w(4), w(6), R(15), R(16), R(11), R(14),
        w(5), R(13), R(12), spread.finish, P(a.y_down), P(a.y_far), C(1), P(a.y), C(0), P(a.y_up),
        A(0, 0, 4), A(1, 0, 2), f(1), C(2), f(3), C(3), A(1, 2, 4), C(5), A(2, 0, 1), A(2, 1, 2),
        C(8), A(2, 2, 3), C(6), A(2, 3, 4), A(3, 0, 1), C(10), A(3, 1, 2), C(9), A(3, 2, 3), f(2),
        A(3, 3, 4), branch_sums, C(16), C(15), f(0), C(4), C(7), C(14), C(13), C(12), B(0), B(1),
        B(17), B(2), B(3), B(4), f(4), f(6), scatter.over_last, scatter.over_inner, C(11), f(5),
        B(5), feeds.finish, norm_low, norm_top,
    ):
        step()
    for mail in (rmail, cmail, bmail, wmail, fmail, imail):
        mail.finish()
    for copy in started:
        copy.wait()


def attention_forward(tokens, ids, bias, out_shard, norms, frequency, qkv_shard, gate_up, down, cots):
    group = (TENSOR, ROWS, WIDTH)
    weights = (4, WIDTH, LOCAL)
    tables, acts = (3, GROUP, LANES), (3, GROUP, LOCAL)
    return pl.pallas_call(
        attention_kernel,
        out_shape=(
            jax.ShapeDtypeStruct((ROWS, WIDTH), BF16),
            jax.ShapeDtypeStruct((8, GROUP), F32),
            jax.ShapeDtypeStruct((8, GROUP), F32),
            jax.ShapeDtypeStruct((ROWS, WIDTH), F32),
            jax.ShapeDtypeStruct(tables, F32),
            jax.ShapeDtypeStruct(acts, BF16),
            jax.ShapeDtypeStruct((GROUP, LOCAL), BF16),
            jax.ShapeDtypeStruct(group, BF16),
            jax.ShapeDtypeStruct(weights, BF16),
            jax.ShapeDtypeStruct(group, BF16),
            jax.ShapeDtypeStruct((16, 3 * UNITS, ROWS), BF16),
        ),
        in_specs=vmem(9) + anywhere(4),
        out_specs=tuple(vmem(3) + anywhere(8)),
        scratch_shapes=[
            pltpu.VMEM(group, BF16),
            pltpu.VMEM(weights, BF16),
            pltpu.VMEM((3 * UNITS, ROWS), BF16),
            pltpu.VMEM((ROWS, WIDTH), BF16),
            pltpu.VMEM(tables, F32),
            pltpu.VMEM(acts, BF16),
            pltpu.VMEM((GROUP, LOCAL), BF16),
            pltpu.VMEM((ROWS, WIDTH), F32),
            pltpu.VMEM((TENSOR, 8, ROWS), jnp.int32),
            pltpu.VMEM((GROUP, LANES), F32),
            pltpu.VMEM(group, BF16),
            pltpu.VMEM((scatter_rows_needed(TOP_BRANCH), WIDTH), BF16),
            pltpu.VMEM((ROWS, WIDTH), F32),
            *pairs(GATHER_MAILS),
            *pairs(GATHER_MAILS),
            *pairs(SCATTER_MAILS),
            *pairs(SPREAD_MAILS),
            *pairs(SPREAD_MAILS),
            *pairs(7),
            pltpu.SemaphoreType.DMA((13,)),
        ],
        compiler_params=params(0),
        name="attention_forward",
    )(tokens, ids, bias, out_shard, *norms, frequency, qkv_shard, gate_up, down, cots)


TOP_FEED, TOP_FEED_BACK = 64, 48

def feed_kernel(
    gain2,
    own,
    mixed_in,
    cots_own,
    cots_in,
    feed,
    branch_grad,
    norm_grads,
    grad_mixed_kept,
    halves,
    outs_kept,
    rows,
    cots,
    weights,
    parts,
    outs,
    acts,
    grads,
    land,
    core_land,
    mixed,
    own_cots,
    total,
    grad_mixed,
    g_sends,
    g_receives,
    s_sends,
    s_receives,
    w_sends,
    w_receives,
    w_local,
    local,
):
    a, r = Around(), Ring()
    gmail, mail, wmail = Mail(g_sends, g_receives), Mail(s_sends, s_receives), Mail(w_sends, w_receives)
    peers = a.peers() + [r.to_core]
    hail(peers)
    first_load = pltpu.make_async_copy(own, rows.at[a.me], local.at[0])
    loads = [
        pltpu.make_async_copy(feed.at[n], weights.at[:, pl.ds(n * ROWS, ROWS)], w_local.at[n])
        for n in range(16)
    ]
    loads.append(pltpu.make_async_copy(cots_in, cots, local.at[1]))
    late_loads = [
        pltpu.make_async_copy(mixed_in, mixed, local.at[2]),
        pltpu.make_async_copy(cots_own, own_cots, local.at[3]),
    ]
    for copy in [first_load] + loads + late_loads:
        copy.start()
    first_load.wait()
    hear(peers)
    gather = Gather(a, gmail, rows, TOP_FEED)
    scatter = Scatter(a, mail, parts, land, TOP_FEED_BACK)
    started = []

    def keep(source, target, number):
        copy = pltpu.make_async_copy(source, target, local.at[number])
        copy.start()
        started.append(copy)

    def load():
        for copy in loads:
            copy.wait()

    state = {}

    def pair(index, *slots):
        x = jnp.concatenate([rows[slot] for slot in slots], axis=0)
        given = jnp.concatenate([cots[slot] for slot in slots], axis=0)
        gate = dot_t(x, weights[pl.ds(0, UNITS), :])
        upward = dot_t(x, weights[pl.ds(UNITS, UNITS), :])
        grad_hidden = dot_t(given, weights[pl.ds(2 * UNITS, UNITS), :])
        sigma = jax.nn.sigmoid(gate)
        silu = gate * sigma
        hidden = (silu * upward).astype(BF16)
        grad_gate = (grad_hidden * upward * (sigma + silu * (1.0 - sigma))).astype(BF16)
        grad_up = (grad_hidden * silu).astype(BF16)
        state[index] = hidden, grad_gate, grad_up

    def pair_back(index, *slots):
        _, grad_gate, grad_up = state[index]
        back = dot(grad_gate, weights[pl.ds(0, UNITS), :])
        back = (back + dot(grad_up, weights[pl.ds(UNITS, UNITS), :])).astype(BF16)
        for number, slot in enumerate(slots):
            parts[slot] = back[number * ROWS : (number + 1) * ROWS]

    def rest(index, *slots):
        hidden, grad_gate, grad_up = state[index]
        out = dot(hidden, weights[pl.ds(2 * UNITS, UNITS), :]).astype(BF16)
        for number, slot in enumerate(slots):
            chunk = slice(number * ROWS, (number + 1) * ROWS)
            outs[slot] = out[chunk]
            lanes = pl.ds(pl.multiple_of(slot * ROWS, ROWS), ROWS)
            acts[pl.ds(0, UNITS), lanes] = grad_gate[chunk].T
            acts[pl.ds(UNITS, UNITS), lanes] = grad_up[chunk].T
            acts[pl.ds(2 * UNITS, UNITS), lanes] = hidden[chunk].T

    def to_sibling(index):
        return wmail.copy(index, grads.at[index, 1 - r.core], core_land.at[index], r.to_core)

    def weight_grad(index, carry):
        columns = pl.ds(pl.multiple_of(index * 2 * ROWS, 2 * ROWS), 2 * ROWS)
        both = dot(acts[pl.ds(0, 2 * UNITS), :], rows[:, :, columns].reshape(GROUP, 2 * ROWS))
        low = dot(acts[pl.ds(2 * UNITS, UNITS), :], cots[:, :, columns].reshape(GROUP, 2 * ROWS))
        for core in range(2):
            lanes = slice(core * ROWS, (core + 1) * ROWS)
            grads[index, core, pl.ds(0, 2 * UNITS), :] = both[:, lanes].astype(BF16)
            grads[index, core, pl.ds(2 * UNITS, UNITS), :] = low[:, lanes].astype(BF16)
        to_sibling(index).start()
        return carry

    def core_sum(index, carry):
        to_sibling(index).wait()
        core_land[index] = added(grads[index, r.core], core_land[index]).astype(BF16)
        return carry

    def core_sums(first, last):
        lax.fori_loop(first, last, core_sum, 0)
        keep(core_land.at[pl.ds(first, last - first)], halves.at[pl.ds(first, last - first)], 4 + first // 4)

    def keep_outs():
        keep(outs, outs_kept, 6)

    def second_norm():
        for copy in late_loads:
            copy.wait()
        mixed[...], state["rinv"] = normalized(mixed[...])

    def norm_half(first, number):
        half = pl.ds(first, HALF)
        incoming, normal = total[half, :], mixed[half, :]
        rinv = state["rinv"][first : first + HALF]
        back = norm_back(incoming, normal, rinv, gain2[...])
        back = own_cots[half, :].astype(F32) + back
        grad_mixed[half, :] = back
        keep(grad_mixed.at[half], grad_mixed_kept.at[half], number)
        branch_grad[half, :] = back.astype(BF16)
        sums = jnp.concatenate(norm_sums(incoming, normal), axis=0)
        norm_grads[...] = sums + norm_grads[...] if "summed" in state else sums
        state["summed"] = True

    def norm_top():
        scatter.finish_top(total)
        norm_half(0, 7)

    def norm_low():
        scatter.finish_low(total)
        norm_half(HALF, 8)

    couples = [(a.me, a.across), (a.down, a.up), (a.far, a.down_o), (a.far_o, a.up_o)]
    directs = [(9,), (18, 8), (3, 17, 6, 5), (0, 1, 2, 7, 4)]
    G, S = gather.step, scatter.step

    def P(index):
        return partial(pair, index, *couples[index])

    def Q(index):
        return partial(pair_back, index, *couples[index])

    def T(index):
        return partial(rest, index, *couples[index])

    def D(index):
        return partial(scatter.direct, *directs[index])

    def W(index):
        return partial(lax.fori_loop, 2 * index, 2 * index + 2, weight_grad, 0)

    def K(index):
        return partial(core_sums, 4 * index, 4 * index + 4)

    for step in (
        partial(gather.send, *range(6)), load, G(0), G(1), G(2), second_norm, G(3), G(4), G(5),
        P(1), T(1), P(0), G(6), G(7), Q(0), D(0), G(8), T(0), G(9), G(10), Q(1), D(1), G(15), G(16),
        G(11), P(2), Q(2), D(2), G(14), G(13), T(2), G(12), P(3), Q(3), D(3), S(17), T(3),
        keep_outs, W(0), S(0), W(1), S(1), W(2), S(2), S(3), W(3), scatter.over_last, S(4), K(0),
        scatter.over_inner, K(1), S(5), norm_low, norm_top,
    ):
        step()
    gmail.finish()
    mail.finish()
    for copy in started:
        copy.wait()


def feed_forward(gain2, own, mixed, own_cots, cots, feed):
    group = (TENSOR, ROWS, WIDTH)
    blocks = (8, 3 * UNITS, ROWS)
    return pl.pallas_call(
        feed_kernel,
        out_shape=(
            jax.ShapeDtypeStruct((ROWS, WIDTH), BF16),
            jax.ShapeDtypeStruct((2, WIDTH), F32),
            jax.ShapeDtypeStruct((ROWS, WIDTH), F32),
            jax.ShapeDtypeStruct(blocks, BF16),
            jax.ShapeDtypeStruct(group, BF16),
        ),
        in_specs=vmem(1) + anywhere(5),
        out_specs=tuple(vmem(2) + anywhere(3)),
        scratch_shapes=[
            pltpu.VMEM(group, BF16),
            pltpu.VMEM(group, BF16),
            pltpu.VMEM((3 * UNITS, WIDTH), BF16),
            pltpu.VMEM(group, BF16),
            pltpu.VMEM(group, BF16),
            pltpu.VMEM((3 * UNITS, GROUP), BF16),
            pltpu.VMEM((8, 2, 3 * UNITS, ROWS), BF16),
            pltpu.VMEM((scatter_rows_needed(TOP_FEED_BACK), WIDTH), BF16),
            pltpu.VMEM(blocks, BF16),
            pltpu.VMEM((ROWS, WIDTH), F32),
            pltpu.VMEM((ROWS, WIDTH), BF16),
            pltpu.VMEM((ROWS, WIDTH), F32),
            pltpu.VMEM((ROWS, WIDTH), F32),
            *pairs(GATHER_MAILS),
            *pairs(SCATTER_MAILS),
            *pairs(8),
            pltpu.SemaphoreType.DMA((16,)),
            pltpu.SemaphoreType.DMA((9,)),
        ],
        compiler_params=params(1),
        name="feed_forward",
    )(gain2, own, mixed, own_cots, cots, feed)


TOP_GRADS, TOP_OUTS, TOP_BACK = 48, 32, 48

def attention_back_kernel(
    gain1,
    shift1,
    norm2_grads,
    own,
    grad_mixed_in,
    mixed_in,
    tokens_in,
    tables_in,
    start_in,
    acts_in,
    attended_in,
    logs_in,
    weights_in,
    halves,
    first_rows,
    outs,
    layer_out,
    token_grad,
    qkv_grad,
    out_grad,
    gate_up_grad,
    down_grad,
    sums,
    grad_mixed,
    mixed,
    tokens,
    tables,
    start_lanes,
    acts,
    attended,
    logs,
    weights,
    rows,
    before,
    grad_out,
    grads_qkv,
    keys_turned,
    turns,
    parts,
    out_parts,
    grads,
    land,
    out_land,
    core_land,
    w_land,
    f_land,
    own_halves,
    total,
    boxes,
    g_sends,
    g_receives,
    s_sends,
    s_receives,
    o_sends,
    o_receives,
    k_sends,
    k_receives,
    w_sends,
    w_receives,
    f_sends,
    f_receives,
    a_sends,
    a_receives,
    local,
):
    a, r = Around(), Ring()
    gmail, mail, omail = Mail(g_sends, g_receives), Mail(s_sends, s_receives), Mail(o_sends, o_receives)
    kmail, wmail, fmail = Mail(k_sends, k_receives), Mail(w_sends, w_receives), Mail(f_sends, f_receives)
    amail = Mail(a_sends, a_receives)
    peers = a.peers() + a.to_rest[:1] + r.peers() + [r.to_zh_core]
    hail(peers)
    loads = {}
    for number, (name, source, target) in enumerate(
        (
            ("own", own, rows.at[a.me]),
            ("acts", acts_in, acts),
            ("attended", attended_in, attended),
            ("outs", outs, out_parts),
            ("weights", weights_in, weights),
            ("logs", logs_in, logs),
            ("start", start_in, start_lanes),
            ("half", halves.at[r.zh * 4 + r.x], own_halves.at[0]),
            ("other", halves.at[(1 - r.zh) * 4 + r.x], own_halves.at[1]),
            ("tables", tables_in, tables),
            ("before", first_rows, before),
            ("mixed", mixed_in, mixed),
            ("tokens", tokens_in, tokens),
            ("grad_mixed", grad_mixed_in, grad_mixed),
        )
    ):
        loads[name] = pltpu.make_async_copy(source, target, local.at[number])
        loads[name].start()

    def loaded(*names):
        for name in names:
            loads.pop(name).wait()

    loaded("own")
    hear(peers)
    gather = Gather(a, gmail, rows, TOP_GRADS)
    out_scatter = Scatter(a, omail, out_parts, out_land, TOP_OUTS)
    scatter = Scatter(a, mail, parts, land, TOP_BACK)
    every = EverySum(amail, boxes, sum_stages(a, r))
    feed_fold = Fold(r, fmail, halves, lambda side: own_halves[side], f_land)
    fold = Fold(r, wmail, core_land, lambda side: core_land[fold.place(side, 0)], w_land)

    def turn():
        loaded("acts", "attended")
        keys_turned[...] = acts[1].T
        turns[pl.ds(3 * LOCAL, LOCAL), :] = attended[...].T
        grads_qkv[1] = jnp.zeros((GROUP, LOCAL), F32)
        grads_qkv[2] = jnp.zeros((GROUP, LOCAL), F32)
        loaded("outs", "weights", "logs", "start")

    def back_project(y):
        chunk = rows[pl.ds(2 * y, 2)].reshape(QBLOCK, WIDTH)
        first = pl.multiple_of(y * QBLOCK, QBLOCK)
        grad_out[pl.ds(first, QBLOCK), :] = dot(chunk, weights[3]).astype(BF16)

    state = {}

    def attend(first, heads):
        count = first + QBLOCK
        span = pl.ds(first, QBLOCK)
        query = acts[0, span, :] * BF16(SCALE)
        given = grad_out[span, :]
        row = lax.broadcasted_iota(jnp.int32, (count, QBLOCK), 0)
        column = first + lax.broadcasted_iota(jnp.int32, (count, QBLOCK), 1)
        allow = (row <= column) & (row.astype(F32) >= start_lanes[pl.ds(0, 1), span])
        overlap = given.astype(F32) * attended[span, :].astype(F32)
        lane = lax.broadcasted_iota(jnp.int32, (QBLOCK, LANES), 1)
        inner = jnp.zeros((QBLOCK, LANES), F32)
        for head in range(*heads):
            summed = jnp.sum(only(head_lanes(head, QBLOCK), overlap), axis=1, keepdims=True)
            inner = jnp.where(lane == head, summed, inner)
        inner = inner.T[:8]
        head_row = lax.broadcasted_iota(jnp.int32, (8, QBLOCK), 0)
        head_rows = lax.broadcasted_iota(jnp.int32, (LOCAL, count), 0) // HEAD_DIM

        def one_head(head, turned_query):
            mask = head_lanes(head, QBLOCK)
            masked, masked_given = only(mask, query), only(mask, given)
            log = jnp.sum(only(head_row == head, logs[:, span]), axis=0, keepdims=True)
            mean = jnp.sum(only(head_row == head, inner), axis=0, keepdims=True)
            scores = dot_t(acts[1, pl.ds(0, count), :], masked)
            probs = only(allow, jnp.exp(scores - log))
            grad_probs = dot_t(acts[2, pl.ds(0, count), :], masked_given)
            grad_scores = (probs * (grad_probs - mean)).astype(BF16)
            grads_qkv[2, pl.ds(0, count), :] += dot(probs.astype(BF16), masked_given)
            grads_qkv[1, pl.ds(0, count), :] += dot(grad_scores, masked)
            keys = only(head_rows == head, keys_turned[:, pl.ds(0, count)])
            return turned_query + dot(keys, grad_scores)

        so_far = state.pop("attend", jnp.zeros((LOCAL, QBLOCK), F32))
        so_far = lax.fori_loop(*heads, one_head, so_far)
        if heads[1] < HEADS_DEV:
            state["attend"] = so_far
        else:
            grads_qkv[0, span, :] = so_far.T * SCALE

    def input_grad(y):
        if "tables" in loads:
            loaded("tables", "before")
        first = pl.multiple_of(y * QBLOCK, QBLOCK)
        span = pl.ds(first, QBLOCK)
        back = jnp.zeros((QBLOCK, WIDTH), F32)
        new = []
        for c in range(3):
            pre = grads_qkv[c, span, :]
            if c < 2:
                pre = turned(pre, tables, first, -1.0)
            pre = pre.astype(BF16)
            new.append(jnp.sum(pre.astype(F32), axis=0, keepdims=True))
            back = back + dot_t(pre, weights[c])
            turns[pl.ds(c * LOCAL, LOCAL), span] = pre.T
        parts[pl.ds(2 * y, 2)] = back.astype(BF16).reshape(2, ROWS, WIDTH)
        state["bias"] = state.get("bias", 0.0) + jnp.concatenate(new, axis=0)

    def to_sibling(index):
        return kmail.copy(index, grads.at[index, 1 - r.core], core_land.at[index], r.to_core)

    def weight_grad(index, carry):
        columns = pl.ds(pl.multiple_of(index * 2 * ROWS, 2 * ROWS), 2 * ROWS)
        three = dot(
            turns[pl.ds(0, 3 * LOCAL), :], before[:, :, columns].reshape(GROUP, 2 * ROWS)
        )
        last = dot(turns[pl.ds(3 * LOCAL, LOCAL), :], rows[:, :, columns].reshape(GROUP, 2 * ROWS))
        for core in range(2):
            lanes = slice(core * ROWS, (core + 1) * ROWS)
            grads[index, core, pl.ds(0, 3 * LOCAL), :] = three[:, lanes].astype(BF16)
            grads[index, core, pl.ds(3 * LOCAL, LOCAL), :] = last[:, lanes].astype(BF16)
        to_sibling(index).start()
        return carry

    def weight_grads(first):
        lax.fori_loop(first, first + 2, weight_grad, 0)

    def core_sum(index, carry):
        to_sibling(index).wait()
        core_land[index] = added(grads[index, r.core], core_land[index]).astype(BF16)
        return carry

    def feed_cross():
        loaded("other")
        feed_fold.cross()

    def feed_result():
        loaded("half")
        feed_fold.near()
        feed_sum = feed_fold.result()
        gate_up_grad[...] = feed_sum[: 2 * UNITS]
        down_grad[...] = feed_sum[2 * UNITS :]

    def weight_result():
        fold.near()
        shard = fold.result()
        for c in range(3):
            qkv_grad[c] = shard[c * LOCAL : (c + 1) * LOCAL].T
        out_grad[...] = shard[3 * LOCAL :]

    def layer_result():
        loaded("mixed")
        out_scatter.finish_top(total)
        out_scatter.finish_low(total)
        layer_out[...] = (mixed[...] + total[...]).astype(BF16)

    def first_norm():
        loaded("tokens", "grad_mixed")
        mixed[...], state["rinv"] = normalized(tokens[...].astype(F32))

    def norm_half(first):
        half = pl.ds(first, HALF)
        rinv = state["rinv"][first : first + HALF]
        back = norm_back(total[half, :], mixed[half, :], rinv, gain1[...])
        token_grad[half, :] = (grad_mixed[half, :] + back).astype(BF16)

    def norm_top():
        scatter.finish_top(total)
        norm_half(0)

    def norm_low():
        scatter.finish_low(total)
        norm_half(HALF)

    def norm1_sums(y):
        part = parts[pl.ds(2 * y, 2)].reshape(QBLOCK, WIDTH).astype(F32)
        scaled = before[pl.ds(2 * y, 2)].reshape(QBLOCK, WIDTH).astype(F32) - shift1[...]
        sums = jnp.concatenate(norm_sums(part, scaled), axis=0)
        state["norm1"] = sums + state["norm1"] if "norm1" in state else sums

    def by_lanes(*values):
        values = jnp.concatenate(values, axis=0)
        width = values.shape[1]
        return jnp.concatenate([values[:, k : k + LANES] for k in range(0, width, LANES)], axis=0)

    def first_sums():
        norm1 = state["norm1"]
        norms = by_lanes(norm1[:1] / gain1[...], norm1[1:], norm2_grads[...])
        spare = jnp.zeros((SUM_ROWS - NORM_ROWS - 3 * LOCAL // LANES, LANES), F32)
        every.first(jnp.concatenate([norms, by_lanes(state["bias"]), spare], axis=0))

    def last_sums():
        sums[pl.ds(0, NORM_ROWS), :] = every.take(3)
        sums[pl.ds(NORM_ROWS, SUM_ROWS - NORM_ROWS), :] = every.kept[NORM_ROWS:]

    G, O, S = gather.step, out_scatter.step, scatter.step

    def P(y):
        return partial(back_project, y)

    def A(q, *heads):
        return partial(attend, q * QBLOCK, heads)

    def I(y):
        return partial(input_grad, y)

    def N(y):
        return partial(norm1_sums, y)

    def W(index):
        return partial(weight_grads, 2 * index)

    def K(index):
        return partial(lax.fori_loop, 4 * index, 4 * index + 4, core_sum, 0)

    for step in (
        partial(gather.send, *range(6)), partial(feed_fold.send, *range(6)), turn, G(0), G(1), G(2),
        G(3), G(4), G(5), P(a.y), G(7), G(6), G(8), out_scatter.direct_across, G(10), G(11),
        out_scatter.direct_down, G(9), out_scatter.direct_up, G(15), G(16), G(12), P(a.y_down),
        P(a.y_up), G(14), O(2), G(13), P(a.y_far), A(0, 0, 4), A(1, 0, 2), O(1), O(4), A(1, 2, 4),
        O(0), O(17), A(2, 0, 1), A(2, 1, 2), feed_cross, A(2, 2, 3), A(2, 3, 4), A(3, 0, 1),
        A(3, 1, 2), A(3, 2, 3), A(3, 3, 4), I(a.y_far), I(a.y_up), I(a.y_down), I(a.y),
        scatter.from_across, O(5), scatter.from_down_pair, N(a.y), W(0), out_scatter.over_inner,
        scatter.from_up_pair, N(a.y_up), W(1), scatter.from_far_pair, W(2), W(3),
        out_scatter.over_last, N(a.y_down), N(a.y_far), first_sums, K(0), K(1),
        partial(fold.send, *range(6)), S(0), feed_result, O(3), every.second, S(4), S(3), S(1),
        S(17), scatter.over_last, S(2), scatter.over_inner, layer_result, every.third, first_norm,
        S(5), fold.cross, norm_low, every.fourth, norm_top, weight_result, last_sums,
    ):
        step()
    for some in (gmail, mail, omail, kmail, wmail, fmail, amail):
        some.finish()


def attention_backward(*operands):
    group = (TENSOR, ROWS, WIDTH)
    block, feed_block = (4 * LOCAL, ROWS), (3 * UNITS, ROWS)
    return pl.pallas_call(
        attention_back_kernel,
        out_shape=(
            jax.ShapeDtypeStruct((ROWS, WIDTH), BF16),
            jax.ShapeDtypeStruct((ROWS, WIDTH), BF16),
            jax.ShapeDtypeStruct((3, ROWS, LOCAL), F32),
            jax.ShapeDtypeStruct((LOCAL, ROWS), F32),
            jax.ShapeDtypeStruct((2 * UNITS, ROWS), F32),
            jax.ShapeDtypeStruct((UNITS, ROWS), F32),
            jax.ShapeDtypeStruct((SUM_ROWS, LANES), F32),
        ),
        in_specs=vmem(3) + anywhere(13),
        out_specs=tuple(vmem(7)),
        scratch_shapes=[
            pltpu.VMEM((ROWS, WIDTH), F32),
            pltpu.VMEM((ROWS, WIDTH), F32),
            pltpu.VMEM((ROWS, WIDTH), BF16),
            pltpu.VMEM((3, GROUP, LANES), F32),
            pltpu.VMEM((8, GROUP), F32),
            pltpu.VMEM((3, GROUP, LOCAL), BF16),
            pltpu.VMEM((GROUP, LOCAL), BF16),
            pltpu.VMEM((8, GROUP), F32),
            pltpu.VMEM((4, WIDTH, LOCAL), BF16),
            pltpu.VMEM(group, BF16),
            pltpu.VMEM(group, BF16),
            pltpu.VMEM((GROUP, LOCAL), BF16),
            pltpu.VMEM((3, GROUP, LOCAL), F32),
            pltpu.VMEM((LOCAL, GROUP), BF16),
            pltpu.VMEM((4 * LOCAL, GROUP), BF16),
            pltpu.VMEM(group, BF16),
            pltpu.VMEM(group, BF16),
            pltpu.VMEM((8, 2) + block, BF16),
            pltpu.VMEM((scatter_rows_needed(TOP_BACK), WIDTH), BF16),
            pltpu.VMEM((scatter_rows_needed(TOP_OUTS), WIDTH), BF16),
            pltpu.VMEM((8,) + block, BF16),
            pltpu.VMEM((FOLD_MAILS,) + block, BF16),
            pltpu.VMEM((FOLD_MAILS,) + feed_block, BF16),
            pltpu.VMEM((2,) + feed_block, BF16),
            pltpu.VMEM((ROWS, WIDTH), F32),
            pltpu.VMEM((SUM_BOXES, SUM_ROWS, LANES), F32),
            *pairs(GATHER_MAILS),
            *pairs(SCATTER_MAILS),
            *pairs(SCATTER_MAILS),
            *pairs(8),
            *pairs(FOLD_MAILS),
            *pairs(FOLD_MAILS),
            *pairs(SUM_MAILS),
            pltpu.SemaphoreType.DMA((14,)),
        ],
        compiler_params=params(2),
        name="attention_backward",
    )(*operands)


def results_kernel(
    layer_in, token_in, qkv_in, out_in, gate_up_in, down_in, sums, layer, token, qkv, out, gate_up, down, *norms
):
    bias = norms[4]
    for source, target in (
        (layer_in, layer),
        (token_in, token),
        (qkv_in, qkv),
        (out_in, out),
        (gate_up_in, gate_up),
        (down_in, down),
    ):
        target[...] = source[...]
    for k in range(WIDTH // LANES):
        for number in range(4):
            norms[number][pl.ds(k, 1), :] = sums[pl.ds(4 * k + number, 1), :]
    for k in range(LOCAL // LANES):
        bias[:, pl.ds(k * LANES, LANES)] = sums[pl.ds(NORM_ROWS + 3 * k, 3), :]


def results(*values):
    shapes = [jax.ShapeDtypeStruct(item.shape, item.dtype) for item in values[:6]]
    shapes += [jax.ShapeDtypeStruct((WIDTH // LANES, LANES), F32)] * 4
    shapes.append(jax.ShapeDtypeStruct((3, LOCAL), F32))
    return pl.pallas_call(
        results_kernel,
        out_shape=tuple(shapes),
        in_specs=vmem(7),
        out_specs=tuple(vmem(len(shapes))),
        name="results",
    )(*values)


def body(
    tokens,
    doc_ids,
    qkv_weight,
    qkv_bias,
    out_weight,
    norm1_gain,
    norm1_shift,
    norm2_gain,
    norm2_shift,
    gate_up_weight,
    down_weight,
    cotangent,
):
    norms = [item[None] for item in (norm1_gain, norm1_shift, norm2_gain, norm2_shift)]
    frequency = np.power(10000.0, -2.0 * np.arange(ROT // 2) / ROT).astype(np.float32)
    frequency = jnp.asarray(np.tile(frequency[:, None], (1, LANES)))
    gate_up = jnp.swapaxes(gate_up_weight, 1, 2).reshape(2 * UNITS, ROWS)
    normed2, start, logs, mixed, tables, acts, attended, rows, weights, cots, feed = attention_forward(
        tokens,
        doc_ids[None],
        qkv_bias,
        out_weight,
        norms,
        frequency,
        qkv_weight,
        gate_up,
        down_weight,
        cotangent,
    )
    branch_grad, norm2_grads, grad_mixed, halves, outs = feed_forward(
        norms[2], normed2, mixed, cotangent, cots, feed
    )
    backward = attention_backward(
        norms[0],
        norms[1],
        norm2_grads,
        branch_grad,
        grad_mixed,
        mixed,
        tokens,
        tables,
        start,
        acts,
        attended,
        logs,
        weights,
        halves,
        rows,
        outs,
    )
    layer_out, token_grad, qkv_grad, out_grad, gate_up_grad, down_grad, *sums = results(*backward)
    return (
        layer_out,
        token_grad,
        qkv_grad,
        sums[4],
        out_grad,
        sums[0].reshape(WIDTH),
        sums[1].reshape(WIDTH),
        sums[2].reshape(WIDTH),
        sums[3].reshape(WIDTH),
        jnp.swapaxes(gate_up_grad.reshape(2, UNITS, ROWS), 1, 2),
        down_grad,
    )


def solution(mesh):
    in_specs = (
        P(("dp", "tensor"), None),
        P(("dp", "tensor")),
        P(None, "dp", "tensor"),
        P(None, "tensor"),
        P("tensor", "dp"),
        P(),
        P(),
        P(),
        P(),
        P(None, "dp", "tensor"),
        P("tensor", "dp"),
        P(("dp", "tensor"), None),
    )
    out_specs = (
        P(("dp", "tensor"), None),
        P(("dp", "tensor"), None),
        P(None, "dp", "tensor"),
        P(None, "tensor"),
        P("tensor", "dp"),
        P(),
        P(),
        P(),
        P(),
        P(None, "dp", "tensor"),
        P("tensor", "dp"),
    )
    return jax.shard_map(body, mesh=mesh, in_specs=in_specs, out_specs=out_specs, check_vma=False)
```

```python
from functools import partial

import jax
import jax.numpy as jnp
import numpy as np
from jax import lax
from jax.experimental import pallas as pl
from jax.experimental.pallas import tpu as pltpu
from jax.sharding import PartitionSpec as P

HEAD_DIM = 64
ROT = 16
DOCS = 4
EPS = 1e-05
SCALE = HEAD_DIM ** (-0.5)

ROWS = 128
WIDTH = 2048
TENSOR = 8
GROUP = ROWS * TENSOR
HALF = ROWS // 2
HEADS_DEV = 4
LOCAL = HEADS_DEV * HEAD_DIM
QBLOCK = 256
UNITS = 704
LANES = 128
MESH = pl.DeviceIdType.MESH
BF16 = jnp.bfloat16
F32 = jnp.float32
VMEM_LIMIT = 62 * 2**20


class Around:
    def __init__(self):
        dp, tensor = lax.axis_index("dp"), lax.axis_index("tensor")
        y, z = tensor // 2, lax.rem(tensor, 2)
        up, down, far = lax.rem(y + 1, 4), lax.rem(y + 3, 4), lax.rem(y + 2, 4)
        other = 1 - z
        self.me, self.across = y * 2 + z, y * 2 + other
        self.up, self.down, self.far = up * 2 + z, down * 2 + z, far * 2 + z
        self.up_o, self.down_o, self.far_o = up * 2 + other, down * 2 + other, far * 2 + other
        self.y, self.z = y, z
        self.y_up, self.y_down, self.y_far = up, down, far
        self.to_up, self.to_down, self.to_across = (dp, self.up), (dp, self.down), (dp, self.across)
        self.to_rest = [(dp, slot) for slot in (self.far, self.up_o, self.down_o, self.far_o)]

    def peers(self):
        return [self.to_up, self.to_down, self.to_across]


class Ring:
    def __init__(self):
        dp, tensor = lax.axis_index("dp"), lax.axis_index("tensor")
        zh, x, core = dp // 8, lax.rem(dp // 2, 4), lax.rem(dp, 2)
        self.zh, self.x, self.core, self.dp, self.tensor = zh, x, core, dp, tensor
        self.xs = [lax.rem(x + step, 4) for step in range(4)]
        self.to_x = [(self.index(zh, self.xs[step], core), tensor) for step in range(4)]
        self.to_zh = (self.index(1 - zh, x, core), tensor)
        self.to_core = (self.index(zh, x, 1 - core), tensor)
        self.to_zh_core = (self.index(1 - zh, x, 1 - core), tensor)

    def index(self, zh, x, core):
        return zh * 8 + x * 2 + core

    def peers(self):
        return self.to_x[1:] + [self.to_zh, self.to_core]


def hail(peers):
    barrier = pltpu.get_barrier_semaphore()
    for peer in peers:
        pl.semaphore_signal(barrier, inc=1, device_id=peer, device_id_type=MESH)


def hear(peers):
    pl.semaphore_wait(pltpu.get_barrier_semaphore(), len(peers))


class Mail:
    def __init__(self, sends, receives):
        self.sends, self.receives = sends, receives
        self.out = []

    def copy(self, number, source, target, device):
        return pltpu.make_async_remote_copy(
            src_ref=source,
            dst_ref=target,
            send_sem=self.sends.at[number],
            recv_sem=self.receives.at[number],
            device_id=device,
            device_id_type=MESH,
        )

    def send(self, number, source, target, device):
        copy = self.copy(number, source, target, device)
        copy.start()
        self.out.append(copy)

    def landed(self, number, target, device):
        self.copy(number, target, target, device).wait_recv()

    def finish(self):
        for copy in self.out:
            copy.wait_send()
        self.out = []


MIDDLE = {64: 96, 48: 96, 32: 80}
GATHER_MAILS = 17


class Gather:
    def __init__(self, around, mail, rows, top, own=None):
        a, middle = around, MIDDLE[top]
        self.mail, self.rows, self.own = mail, rows, own
        self.messages = [
            (a.to_up, a.me, 0, HALF, a.down),
            (a.to_down, a.me, HALF, ROWS, a.up),
            (a.to_across, a.me, top, ROWS, a.across),
            (a.to_up, a.me, HALF, ROWS, a.down),
            (a.to_down, a.me, 0, HALF, a.up),
            (a.to_across, a.me, 0, top, a.across),
            (a.to_up, a.down, 0, HALF, a.far),
            (a.to_across, a.down, 0, top, a.down_o),
            (a.to_down, a.up, HALF, ROWS, a.far),
            (a.to_up, a.across, top, middle, a.down_o),
            (a.to_down, a.across, middle, ROWS, a.up_o),
            (a.to_across, a.up, 0, top, a.up_o),
            (a.to_across, a.far, 0, top, a.far_o),
            (a.to_up, a.down_o, top, middle, a.far_o),
            (a.to_down, a.up_o, middle, ROWS, a.far_o),
            (a.to_up, a.across, middle, ROWS, a.down_o),
            (a.to_down, a.across, top, middle, a.up_o),
        ]

    def part(self, slot, first, last):
        return self.rows.at[slot, pl.ds(first, last - first)]

    def send(self, *numbers):
        for number in numbers:
            device, slot, first, last, _ = self.messages[number]
            target = source = self.part(slot, first, last)
            if number < 6 and self.own is not None:
                source = self.own.at[pl.ds(first, last - first)]
            self.mail.send(number, source, target, device)

    def step(self, number):
        return partial(self.on, number)

    def on(self, number):
        device, _, first, last, slot = self.messages[number]
        self.mail.landed(number, self.part(slot, first, last), device)
        followers = {0: (6, 7), 1: (8,), 2: (9, 10, 15, 16), 4: (11,), 6: (12,), 9: (13,), 10: (14,)}
        self.send(*followers.get(number, ()))


def added(*terms):
    total = terms[0].astype(F32)
    for term in terms[1:]:
        total = total + term.astype(F32)
    return total


SCATTER_MAILS = 21


def scatter_boxes(top):
    middle = MIDDLE[top]
    last, inner, rest = ROWS - middle, middle - top, HALF - top
    counts = (last, inner, top, HALF, top, top, last, inner, HALF, top)
    counts += (top, inner, last, HALF, top, top, inner, rest, rest, rest, last, inner, last)
    order = [*range(17), 20, 17, 18, 19, 21, 22]
    firsts = [0] * len(counts)
    for before, number in zip(order, order[1:]):
        firsts[number] = firsts[before] + counts[before]
    return counts, tuple(firsts)


def scatter_rows_needed(top):
    return sum(scatter_boxes(top)[0])


class Scatter:
    def __init__(self, around, mail, parts, land, top):
        self.a, self.mail, self.parts, self.land, self.top = around, mail, parts, land, top
        self.middle = MIDDLE[top]
        self.counts, self.firsts = scatter_boxes(top)
        self.crossed = False

    def part(self, slot, first, last):
        return self.parts.at[slot, pl.ds(first, last - first)]

    def box(self, number):
        return self.land.at[pl.ds(self.firsts[number], self.counts[number])]

    def got(self, number):
        self.mail.landed(number, self.box(number), self.a.to_up)

    def fold(self, stage, slot, first, *others):
        terms = [self.part(slot, first, first + self.counts[stage])[...], self.box(stage)[...]]
        terms += [self.box(other)[...] for other in others]
        self.box(stage)[...] = added(*terms).astype(BF16)

    def direct(self, *numbers):
        a, top, middle = self.a, self.top, self.middle
        messages = {
            0: (a.far_o, middle, a.to_up),
            1: (a.far_o, top, a.to_down),
            2: (a.far_o, 0, a.to_across),
            3: (a.far, HALF, a.to_up),
            17: (a.far, top, a.to_down),
            4: (a.up_o, 0, a.to_across),
            7: (a.up_o, top, a.to_up),
            5: (a.down_o, 0, a.to_across),
            6: (a.down_o, middle, a.to_down),
            18: (a.up, top, a.to_up),
            8: (a.down, HALF, a.to_down),
            9: (a.across, 0, a.to_across),
        }
        for number in numbers:
            slot, first, device = messages[number]
            source = self.part(slot, first, first + self.counts[number])
            self.mail.send(number, source, self.box(number), device)

    def from_far_pair(self):
        self.direct(0, 1, 2, 3, 17)

    def from_up_pair(self):
        self.direct(7, 4, 18)

    def from_down_pair(self):
        self.direct(6, 5, 8)

    def from_across(self):
        self.direct(9)

    def direct_up(self):
        self.direct(0, 3, 7, 18)

    def direct_down(self):
        self.direct(1, 17, 6, 8)

    def direct_across(self):
        self.direct(2, 4, 5, 9)

    def step(self, number):
        return partial(self.on, number)

    def on(self, number):
        a, box = self.a, self.box
        follower, slot, first, device, *others = {
            1: (11, a.down_o, self.top, a.to_down),
            0: (12, a.up_o, self.middle, a.to_up),
            2: (10, a.far, 0, a.to_down),
            3: (13, a.up, HALF, a.to_up),
            17: (19, a.down, self.top, a.to_down),
            4: (14, a.up, 0, a.to_up),
            5: (15, a.down, 0, a.to_down, 10),
        }[number]
        for other in (number, *others):
            self.got(other)
        self.fold(number, slot, first, *others)
        self.mail.send(follower, box(number), box(follower), device)

    def over(self, number, made, first, *landed):
        for other in landed:
            self.got(other)
        own = self.part(self.a.across, first, first + self.counts[number])
        terms = [own[...]] + [self.box(other)[...] for other in landed]
        self.box(made)[...] = added(*terms).astype(BF16)
        self.mail.send(number, self.box(made), self.box(number), self.a.to_across)

    def over_inner(self):
        self.over(16, 21, self.top, 7, 11)

    def over_last(self):
        self.over(20, 22, self.middle, 6, 12)

    def all_direct(self):
        self.direct(0, 1, 2, 3, 17, 7, 4, 6, 5, 18, 8, 9)

    def boxed(self, number, first, last):
        return self.land[pl.ds(self.firsts[number] + first, last - first), :]

    def finish_top(self, total):
        a, top = self.a, self.top
        for number in (9, 14, 15, 18, 19):
            self.got(number)
        if not self.crossed:
            self.got(16)
            self.crossed = True
        total[pl.ds(0, top), :] = added(
            self.part(a.me, 0, top)[...], *(self.box(k)[...] for k in (9, 14, 15))
        )
        total[pl.ds(top, HALF - top), :] = added(
            self.part(a.me, top, HALF)[...],
            self.box(18)[...],
            self.box(19)[...],
            self.boxed(16, 0, HALF - top),
        )

    def finish_low(self, total):
        for number in (8, 13, 20):
            self.got(number)
        if not self.crossed:
            self.got(16)
            self.crossed = True
        total[pl.ds(HALF, HALF), :] = added(
            self.part(self.a.me, HALF, ROWS)[...],
            self.box(8)[...],
            self.box(13)[...],
            self.boxed(16, HALF - self.top, ROWS - self.top),
        )


class Spread:
    def __init__(self, ring, mail, block, own_shard=None):
        r = self.r = ring
        self.mail, self.block, self.own = mail, block, own_shard
        own, cross = (r.zh, r.x), (1 - r.zh, r.x)
        self.messages = [(r.to_zh, own, cross)]
        self.messages += [(r.to_x[k], own, (r.zh, r.xs[4 - k])) for k in (1, 2, 3)]
        self.messages += [(r.to_x[k], cross, (1 - r.zh, r.xs[4 - k])) for k in (1, 2, 3)]
        self.messages += [(r.to_core, own, own), (r.to_core, cross, cross)]
        self.messages += [(r.to_core, self.messages[k][2], self.messages[k][2]) for k in range(1, 7)]

    def send(self, number):
        device, place, _ = self.messages[number]
        block = self.block(*place, self.r.core)
        source = self.own if self.own is not None and number in (0, 1, 2, 3, 7) else block
        self.mail.send(number, source, block, device)

    def step(self, number):
        return partial(self.on, number)

    def begin(self):
        for number in (0, 1, 3, 2, 7):
            self.send(number)

    def on(self, number):
        device, _, place = self.messages[number]
        core = self.r.core if number < 7 else 1 - self.r.core
        self.mail.landed(number, self.block(*place, core), device)
        if number == 0:
            for follower in (4, 6, 5, 8):
                self.send(follower)
        elif number < 7:
            self.send(number + 8)

    def finish(self):
        for number in range(7, SPREAD_MAILS):
            self.on(number)


SPREAD_MAILS = 15
FOLDS = [(side, step) for step in (1, 3, 2, 0) for side in (1, 0)]


class Fold:
    def __init__(self, ring, mail, grads, own, land):
        self.r, self.mail, self.grads, self.own, self.land = ring, mail, grads, own, land

    def place(self, side, step):
        zh = 1 - self.r.zh if side else self.r.zh
        return zh * 4 + self.r.xs[step]

    def send(self, *numbers):
        for number in numbers:
            side, step = FOLDS[number]
            source = self.grads.at[self.place(side, step)]
            self.mail.send(number, source, self.land.at[number], self.r.to_x[step])

    def cross(self):
        for number in (0, 2, 4):
            self.mail.landed(number, self.land.at[number], self.r.to_core)
        self.land[0] = added(self.own(1), self.land[0], self.land[2], self.land[4]).astype(BF16)
        self.mail.send(6, self.land.at[0], self.land.at[6], self.r.to_zh)

    def near(self):
        for number in (1, 3, 5):
            self.mail.landed(number, self.land.at[number], self.r.to_core)

    def result(self):
        self.mail.landed(6, self.land.at[6], self.r.to_core)
        land = self.land
        return added(self.own(0), land[1], land[3], land[5], land[6])


FOLD_MAILS = 7

SUM_ROWS, NORM_ROWS = 72, 64
SUM_BOXES, SUM_MAILS = 14, 13


class EverySum:
    def __init__(self, mail, boxes, stages):
        self.mail, self.boxes, self.stages = mail, boxes, stages

    def give(self, stage, values):
        base, count, mine, _, peers = self.stages[stage]
        view = pl.ds(0, count)
        self.boxes[base + mine, view] = values
        for number, peer in enumerate(peers):
            box = self.boxes.at[base + mine, view]
            self.mail.send(base + number, box, box, peer)

    def take(self, stage):
        base, count, _, sources, peers = self.stages[stage]
        view = pl.ds(0, count)
        for number, source in enumerate(sources):
            self.mail.landed(base + number, self.boxes.at[base + source, view], peers[0])
        result = self.boxes[base, view]
        for k in range(1, len(peers) + 1):
            result = result + self.boxes[base + k, view]
        return result

    def first(self, values):
        self.give(0, values)

    def second(self):
        self.give(1, self.take(0))

    def third(self):
        self.kept = self.take(1)
        self.give(2, self.kept[: self.stages[2][1]])

    def fourth(self):
        self.give(3, self.take(2))


def sum_stages(a, r):
    crossed = 1 - r.zh
    place = r.zh * 2 + r.core
    sources = [crossed * 2 + r.core, r.zh * 2 + 1 - r.core, crossed * 2 + 1 - r.core]
    y_sources, y_peers = [a.y_down, a.y_far, a.y_up], [a.to_up, a.to_rest[0], a.to_down]
    return [
        (0, SUM_ROWS, r.x, [r.xs[3], r.xs[2], r.xs[1]], r.to_x[1:]),
        (4, SUM_ROWS, place, sources, [r.to_zh, r.to_core, r.to_zh_core]),
        (8, NORM_ROWS, a.y, y_sources, y_peers),
        (12, NORM_ROWS, a.z, [1 - a.z], [a.to_across]),
    ]


def dot(left, right):
    return lax.dot_general(left, right, (((1,), (0,)), ((), ())), preferred_element_type=F32)


def dot_t(left, right):
    return lax.dot_general(left, right, (((1,), (1,)), ((), ())), preferred_element_type=F32)


def normalized(values):
    centred = values - jnp.mean(values, axis=1, keepdims=True)
    variance = jnp.mean(centred * centred, axis=1, keepdims=True)
    rinv = lax.rsqrt(variance + EPS)
    return centred * rinv, rinv


def norm_sums(incoming, normal):
    return jnp.sum(incoming * normal, axis=0, keepdims=True), jnp.sum(incoming, axis=0, keepdims=True)


def norm_back(incoming, normal, rinv, gain):
    scaled = incoming * gain
    inner = scaled - jnp.mean(scaled, axis=1, keepdims=True)
    return rinv * (inner - normal * jnp.mean(scaled * normal, axis=1, keepdims=True))


def turned(values, tables, first, sign):
    rows = pl.ds(first, values.shape[0])
    cosine, minus, plus = tables[0, rows], tables[1, rows], tables[2, rows]
    halves = []
    for lane in range(0, LOCAL, LANES):
        part = values[:, lane : lane + LANES]
        left = pltpu.roll(part, LANES - ROT // 2, 1)
        right = pltpu.roll(part, ROT // 2, 1)
        halves.append(part * cosine + sign * (left * minus + right * plus))
    return jnp.concatenate(halves, axis=1)


def head_lanes(head, rows):
    return lax.broadcasted_iota(jnp.int32, (rows, LOCAL), 1) // HEAD_DIM == head


def only(mask, values):
    return jnp.where(mask, values, jnp.zeros_like(values))


def place_rows(id_rows, frequency, tables, start_rows, start_lanes):
    ids = jnp.max(id_rows[...], axis=1)
    shape = (TENSOR, ROWS)
    index = lax.broadcasted_iota(jnp.int32, shape, 0) * ROWS
    index = (index + lax.broadcasted_iota(jnp.int32, shape, 1)).astype(F32)
    offset = jnp.zeros(shape, F32)
    for number in range(1, DOCS):
        before = ((ids >= 0) & (ids < number)).astype(F32)
        count = jnp.sum(jnp.sum(before, axis=1, keepdims=True), axis=0, keepdims=True)
        offset = jnp.where(ids == number, count, offset)
    start = jnp.where(ids >= 0, offset, index)
    position = index - offset

    def along(values):
        return jnp.concatenate([values[t : t + 1] for t in range(TENSOR)], axis=1)

    angle = frequency[:, :1] * along(position)
    cosine, sine = jnp.cos(angle), jnp.sin(angle)
    none = jnp.zeros_like(sine)
    rest = (HEAD_DIM - ROT) // 8
    columns = (
        [cosine, cosine] + [jnp.ones_like(sine)] * rest,
        [-sine, none] + [none] * rest,
        [none, sine] + [none] * rest,
    )
    for number, parts in enumerate(columns):
        tables[number] = jnp.concatenate(parts + parts, axis=0).T
    lanes = jnp.broadcast_to(along(start), (8, GROUP))
    start_lanes[...] = lanes
    start_rows[...] = jnp.concatenate([lanes] * (LANES // 8), axis=0).T


def vmem(count):
    return [pl.BlockSpec(memory_space=pltpu.VMEM)] * count


def anywhere(count):
    return [pl.BlockSpec(memory_space=pl.ANY)] * count


def pairs(count):
    return [pltpu.SemaphoreType.DMA((count,)), pltpu.SemaphoreType.DMA((count,))]


def params(collective):
    return pltpu.CompilerParams(
        collective_id=collective, has_side_effects=True, vmem_limit_bytes=VMEM_LIMIT
    )


TOP_ROWS, TOP_COTS, TOP_BRANCH = 48, 32, 48


def attention_kernel(
    tokens,
    ids,
    bias,
    out_shard,
    gain1,
    shift1,
    gain2,
    shift2,
    frequency,
    qkv_shard,
    gate_up,
    down,
    own_cots,
    start_lanes,
    logs,
    normed2_kept,
    mixed_kept,
    tables_kept,
    acts_kept,
    attended_kept,
    rows_kept,
    weights_kept,
    cots,
    feed,
    rows,
    weights,
    feed_own,
    cots_own,
    tables,
    acts,
    attended,
    mixed,
    normed2,
    id_rows,
    start_rows,
    parts,
    land,
    total,
    r_sends,
    r_receives,
    c_sends,
    c_receives,
    b_sends,
    b_receives,
    w_sends,
    w_receives,
    f_sends,
    f_receives,
    i_sends,
    i_receives,
    local,
):
    a, r = Around(), Ring()
    rmail, cmail, bmail = Mail(r_sends, r_receives), Mail(c_sends, c_receives), Mail(b_sends, b_receives)
    wmail, fmail, imail = Mail(w_sends, w_receives), Mail(f_sends, f_receives), Mail(i_sends, i_receives)
    peers = a.peers() + a.to_rest + r.peers()
    hail(peers)

    def weight_block(zh, x, core):
        first = pl.multiple_of(r.index(zh, x, core) * ROWS, ROWS)
        return weights.at[:, pl.ds(first, ROWS), :]

    mine = pl.multiple_of(r.dp * ROWS, ROWS)
    loads = [
        pltpu.make_async_copy(qkv_shard, weights.at[pl.ds(0, 3), pl.ds(mine, ROWS)], local.at[0]),
        pltpu.make_async_copy(gate_up, feed_own.at[pl.ds(0, 2 * UNITS)], local.at[1]),
        pltpu.make_async_copy(down, feed_own.at[pl.ds(2 * UNITS, UNITS)], local.at[2]),
        pltpu.make_async_copy(own_cots, cots_own, local.at[3]),
    ]
    for copy in loads:
        copy.start()
    id_rows[a.me] = jnp.broadcast_to(ids[...], (8, ROWS))

    def first_norm(first):
        half = pl.ds(first, HALF)
        normal, _ = normalized(tokens[half, :].astype(F32))
        rows[a.me, half] = (normal * gain1[...] + shift1[...]).astype(BF16)

    first_norm(0)
    hear(peers)

    group = [
        (0, a.to_up, a.down),
        (1, a.to_down, a.up),
        (2, a.to_across, a.across),
        (3, a.to_rest[0], a.far),
        (4, a.to_rest[1], a.down_o),
        (5, a.to_rest[2], a.up_o),
        (6, a.to_rest[3], a.far_o),
    ]
    gather = Gather(a, rmail, rows, TOP_ROWS)
    others = Gather(a, cmail, cots, TOP_COTS, cots_own)
    spread = Spread(r, wmail, weight_block)
    feeds = Spread(r, fmail, lambda zh, x, core: feed.at[r.index(zh, x, core)], feed_own)
    scatter = Scatter(a, bmail, parts, land, TOP_BRANCH)
    started = []

    def keep(source, target, number):
        copy = pltpu.make_async_copy(source, target, local.at[number])
        copy.start()
        started.append(copy)

    def begin():
        gather.send(0)
        for number, device, _ in group:
            imail.send(number, id_rows.at[a.me], id_rows.at[a.me], device)
        first_norm(HALF)
        gather.send(1, 2)
        weights[3, pl.ds(mine, ROWS), :] = out_shard[...].T
        loads[0].wait()
        spread.begin()
        gather.send(3, 4, 5)
        for copy in loads[1:]:
            copy.wait()
        keep(feed_own, feed.at[r.dp], 4)
        keep(cots_own, cots.at[a.me], 5)

    def place():
        for number, _, slot in group:
            imail.landed(number, id_rows.at[slot], a.to_up)
        place_rows(id_rows, frequency, tables, start_rows, start_lanes)
        keep(tables, tables_kept, 6)

    def P(y):
        return partial(project, y)

    def project(y):
        first = pl.multiple_of(y * QBLOCK, QBLOCK)
        chunk = rows[pl.ds(2 * y, 2)].reshape(QBLOCK, WIDTH)
        for c in range(3):
            pre = dot(chunk, weights[c]) + bias[pl.ds(c, 1), :]
            if c < 2:
                pre = turned(pre, tables, first, 1.0)
            acts[c, pl.ds(first, QBLOCK), :] = pre.astype(BF16)

    state = {}

    def A(q, *heads):
        return partial(attend, q * QBLOCK, heads)

    def attend(first, heads):
        count = first + QBLOCK
        query = acts[0, pl.ds(first, QBLOCK), :] * BF16(SCALE)
        row = first + lax.broadcasted_iota(jnp.int32, (QBLOCK, count), 0)
        column = lax.broadcasted_iota(jnp.int32, (QBLOCK, count), 1)
        start = start_rows[pl.ds(first, QBLOCK), pl.ds(0, 1)]
        allow = (column <= row) & (column.astype(F32) >= start)
        lane = lax.broadcasted_iota(jnp.int32, (QBLOCK, LANES), 1)

        def one_head(head, carry):
            out, log = carry
            masked = only(head_lanes(head, QBLOCK), query)
            scores = dot_t(masked, acts[1, pl.ds(0, count), :])
            scores = jnp.where(allow, scores, -1e30)
            highest = jnp.max(scores, axis=1, keepdims=True)
            expon = jnp.exp(scores - highest)
            sums = jnp.sum(expon, axis=1, keepdims=True)
            values = only(head_lanes(head, count), acts[2, pl.ds(0, count), :])
            out = out + dot(expon.astype(BF16), values) / sums
            log = jnp.where(lane == head, highest + jnp.log(sums), log)
            return out, log

        zeros = (jnp.zeros((QBLOCK, LOCAL), F32), jnp.zeros((QBLOCK, LANES), F32))
        carry = lax.fori_loop(*heads, one_head, state.pop("attend", zeros))
        if heads[1] < HEADS_DEV:
            state["attend"] = carry
            return
        out = carry[0].astype(BF16)
        attended[pl.ds(first, QBLOCK), :] = out
        logs[:, pl.ds(first, QBLOCK)] = carry[1].T[:8]
        branch = dot_t(out, weights[3]).astype(BF16)
        parts[first // ROWS] = branch[:ROWS]
        parts[first // ROWS + 1] = branch[ROWS:]

    def branch_sums():
        keep(rows, rows_kept, 7)
        keep(weights, weights_kept, 8)
        keep(acts, acts_kept, 9)
        keep(attended, attended_kept, 10)
        scatter.all_direct()

    def norm_half(first, number):
        half = pl.ds(first, HALF)
        after = tokens[half, :].astype(F32) + total[half, :]
        mixed[half, :] = after
        keep(mixed.at[half], mixed_kept.at[half], number)
        normal, _ = normalized(after)
        normed2[half, :] = (normal * gain2[...] + shift2[...]).astype(BF16)
        keep(normed2.at[half], normed2_kept.at[half], number + 2)

    def norm_top():
        scatter.finish_top(total)
        norm_half(0, 11)

    def norm_low():
        scatter.finish_low(total)
        norm_half(HALF, 12)

    R, C, B, w, f = gather.step, others.step, scatter.step, spread.step, feeds.step
    C_up, C_down, C_across = (partial(others.send, *two) for two in ((0, 3), (1, 4), (2, 5)))
    for step in (
        begin, R(0), place, R(1), R(2), w(3), w(1), R(3), R(4), w(2), w(0), R(6), C_across,
        feeds.begin, R(8), R(5), R(10), C_down, R(9), C_up, R(7), w(4), w(6), R(15), R(16), R(11),
        R(14), R(13), w(5), R(12), spread.finish, P(a.y_down), P(a.y_far), C(1), C(0), P(a.y),
        P(a.y_up), A(0, 0, 4), A(1, 0, 2), C(2), C(3), f(1), f(3), A(1, 2, 4), C(5), A(2, 0, 1),
        A(2, 1, 2), A(2, 2, 3), C(6), C(8), A(2, 3, 4), A(3, 0, 1), A(3, 1, 2), C(10), C(9),
        A(3, 2, 3), f(2), A(3, 3, 4), branch_sums, C(15), C(16), C(4), f(0), C(7), C(14), C(13),
        C(12), B(0), B(1), B(17), B(2), B(3), B(4), f(4), f(6), scatter.over_last,
        scatter.over_inner, C(11), f(5), B(5), feeds.finish, norm_low, norm_top,
    ):
        step()
    for mail in (rmail, cmail, bmail, wmail, fmail, imail):
        mail.finish()
    for copy in started:
        copy.wait()


def attention_forward(tokens, ids, bias, out_shard, norms, frequency, qkv_shard, gate_up, down, cots):
    group = (TENSOR, ROWS, WIDTH)
    weights = (4, WIDTH, LOCAL)
    tables, acts = (3, GROUP, LANES), (3, GROUP, LOCAL)
    return pl.pallas_call(
        attention_kernel,
        out_shape=(
            jax.ShapeDtypeStruct((8, GROUP), F32),
            jax.ShapeDtypeStruct((8, GROUP), F32),
            jax.ShapeDtypeStruct((ROWS, WIDTH), BF16),
            jax.ShapeDtypeStruct((ROWS, WIDTH), F32),
            jax.ShapeDtypeStruct(tables, F32),
            jax.ShapeDtypeStruct(acts, BF16),
            jax.ShapeDtypeStruct((GROUP, LOCAL), BF16),
            jax.ShapeDtypeStruct(group, BF16),
            jax.ShapeDtypeStruct(weights, BF16),
            jax.ShapeDtypeStruct(group, BF16),
            jax.ShapeDtypeStruct((16, 3 * UNITS, ROWS), BF16),
        ),
        in_specs=vmem(9) + anywhere(4),
        out_specs=tuple(vmem(2) + anywhere(9)),
        scratch_shapes=[
            pltpu.VMEM(group, BF16),
            pltpu.VMEM(weights, BF16),
            pltpu.VMEM((3 * UNITS, ROWS), BF16),
            pltpu.VMEM((ROWS, WIDTH), BF16),
            pltpu.VMEM(tables, F32),
            pltpu.VMEM(acts, BF16),
            pltpu.VMEM((GROUP, LOCAL), BF16),
            pltpu.VMEM((ROWS, WIDTH), F32),
            pltpu.VMEM((ROWS, WIDTH), BF16),
            pltpu.VMEM((TENSOR, 8, ROWS), jnp.int32),
            pltpu.VMEM((GROUP, LANES), F32),
            pltpu.VMEM(group, BF16),
            pltpu.VMEM((scatter_rows_needed(TOP_BRANCH), WIDTH), BF16),
            pltpu.VMEM((ROWS, WIDTH), F32),
            *pairs(GATHER_MAILS),
            *pairs(GATHER_MAILS),
            *pairs(SCATTER_MAILS),
            *pairs(SPREAD_MAILS),
            *pairs(SPREAD_MAILS),
            *pairs(7),
            pltpu.SemaphoreType.DMA((15,)),
        ],
        compiler_params=params(0),
        name="attention_forward",
    )(tokens, ids, bias, out_shard, *norms, frequency, qkv_shard, gate_up, down, cots)


TOP_FEED, TOP_FEED_BACK = 64, 48

def feed_kernel(
    gain2,
    own,
    mixed_in,
    cots_own,
    cots_in,
    feed,
    norm_grads,
    branch_grad_kept,
    grad_mixed_kept,
    halves,
    outs_kept,
    rows,
    cots,
    weights,
    parts,
    outs,
    acts,
    grads,
    land,
    core_land,
    mixed,
    own_cots,
    total,
    grad_mixed,
    branch_grad,
    g_sends,
    g_receives,
    s_sends,
    s_receives,
    w_sends,
    w_receives,
    w_local,
    local,
):
    a, r = Around(), Ring()
    gmail, mail, wmail = Mail(g_sends, g_receives), Mail(s_sends, s_receives), Mail(w_sends, w_receives)
    peers = a.peers() + [r.to_core]
    hail(peers)
    first_load = pltpu.make_async_copy(own, rows.at[a.me], local.at[0])
    loads = [
        pltpu.make_async_copy(feed.at[n], weights.at[:, pl.ds(n * ROWS, ROWS)], w_local.at[n])
        for n in range(16)
    ]
    loads.append(pltpu.make_async_copy(cots_in, cots, local.at[1]))
    late_loads = [
        pltpu.make_async_copy(mixed_in, mixed, local.at[2]),
        pltpu.make_async_copy(cots_own, own_cots, local.at[3]),
    ]
    for copy in [first_load] + loads + late_loads:
        copy.start()
    hear(peers)
    gather = Gather(a, gmail, rows, TOP_FEED, own)
    scatter = Scatter(a, mail, parts, land, TOP_FEED_BACK)
    started = []

    def keep(source, target, number):
        copy = pltpu.make_async_copy(source, target, local.at[number])
        copy.start()
        started.append(copy)

    def load():
        for copy in [first_load] + loads:
            copy.wait()

    state = {}

    def pair(index, *slots):
        x = jnp.concatenate([rows[slot] for slot in slots], axis=0)
        given = jnp.concatenate([cots[slot] for slot in slots], axis=0)
        gate = dot_t(x, weights[pl.ds(0, UNITS), :])
        upward = dot_t(x, weights[pl.ds(UNITS, UNITS), :])
        grad_hidden = dot_t(given, weights[pl.ds(2 * UNITS, UNITS), :])
        sigma = jax.nn.sigmoid(gate)
        silu = gate * sigma
        hidden = (silu * upward).astype(BF16)
        grad_gate = (grad_hidden * upward * (sigma + silu * (1.0 - sigma))).astype(BF16)
        grad_up = (grad_hidden * silu).astype(BF16)
        state[index] = hidden, grad_gate, grad_up

    def pair_back(index, *slots):
        _, grad_gate, grad_up = state[index]
        back = dot(grad_gate, weights[pl.ds(0, UNITS), :])
        back = (back + dot(grad_up, weights[pl.ds(UNITS, UNITS), :])).astype(BF16)
        for number, slot in enumerate(slots):
            parts[slot] = back[number * ROWS : (number + 1) * ROWS]

    def rest(index, *slots):
        hidden, grad_gate, grad_up = state[index]
        out = dot(hidden, weights[pl.ds(2 * UNITS, UNITS), :]).astype(BF16)
        for number, slot in enumerate(slots):
            chunk = slice(number * ROWS, (number + 1) * ROWS)
            outs[slot] = out[chunk]
            lanes = pl.ds(pl.multiple_of(slot * ROWS, ROWS), ROWS)
            acts[pl.ds(0, UNITS), lanes] = grad_gate[chunk].T
            acts[pl.ds(UNITS, UNITS), lanes] = grad_up[chunk].T
            acts[pl.ds(2 * UNITS, UNITS), lanes] = hidden[chunk].T

    def to_sibling(index):
        return wmail.copy(index, grads.at[index, 1 - r.core], core_land.at[index], r.to_core)

    def weight_grad(index, carry):
        columns = pl.ds(pl.multiple_of(index * 2 * ROWS, 2 * ROWS), 2 * ROWS)
        both = dot(acts[pl.ds(0, 2 * UNITS), :], rows[:, :, columns].reshape(GROUP, 2 * ROWS))
        low = dot(acts[pl.ds(2 * UNITS, UNITS), :], cots[:, :, columns].reshape(GROUP, 2 * ROWS))
        for core in range(2):
            lanes = slice(core * ROWS, (core + 1) * ROWS)
            grads[index, core, pl.ds(0, 2 * UNITS), :] = both[:, lanes].astype(BF16)
            grads[index, core, pl.ds(2 * UNITS, UNITS), :] = low[:, lanes].astype(BF16)
        to_sibling(index).start()
        return carry

    def core_sum(index, carry):
        to_sibling(index).wait()
        core_land[index] = added(grads[index, r.core], core_land[index]).astype(BF16)
        return carry

    def core_sums(first, last):
        lax.fori_loop(first, last, core_sum, 0)
        keep(core_land.at[pl.ds(first, last - first)], halves.at[pl.ds(first, last - first)], 4 + first // 4)

    def keep_outs():
        keep(outs, outs_kept, 6)

    def second_norm():
        for copy in late_loads:
            copy.wait()
        mixed[...], state["rinv"] = normalized(mixed[...])

    def norm_half(first, number):
        half = pl.ds(first, HALF)
        incoming, normal = total[half, :], mixed[half, :]
        rinv = state["rinv"][first : first + HALF]
        back = norm_back(incoming, normal, rinv, gain2[...])
        back = own_cots[half, :].astype(F32) + back
        grad_mixed[half, :] = back
        keep(grad_mixed.at[half], grad_mixed_kept.at[half], number)
        branch_grad[half, :] = back.astype(BF16)
        keep(branch_grad.at[half], branch_grad_kept.at[half], number + 2)
        sums = jnp.concatenate(norm_sums(incoming, normal), axis=0)
        norm_grads[...] = sums + norm_grads[...] if "summed" in state else sums
        state["summed"] = True

    def norm_top():
        scatter.finish_top(total)
        norm_half(0, 7)

    def norm_low():
        scatter.finish_low(total)
        norm_half(HALF, 8)

    couples = [(a.me, a.across), (a.down, a.up), (a.far, a.down_o), (a.far_o, a.up_o)]
    directs = [(9,), (18, 8), (3, 17, 6, 5), (0, 1, 2, 7, 4)]
    G, S = gather.step, scatter.step

    def P(index):
        return partial(pair, index, *couples[index])

    def Q(index):
        return partial(pair_back, index, *couples[index])

    def T(index):
        return partial(rest, index, *couples[index])

    def D(index):
        return partial(scatter.direct, *directs[index])

    def W(index):
        return partial(lax.fori_loop, 2 * index, 2 * index + 2, weight_grad, 0)

    def K(index):
        return partial(core_sums, 4 * index, 4 * index + 4)

    for step in (
        partial(gather.send, *range(6)), load, G(0), G(1), G(2), second_norm, G(3), G(4), G(5),
        P(1), T(1), P(0), G(6), G(7), Q(0), D(0), G(8), T(0), G(9), G(10), Q(1), D(1), G(15), G(16),
        G(11), P(2), Q(2), D(2), G(14), G(13), T(2), G(12), P(3), Q(3), D(3), S(17), T(3),
        keep_outs, W(0), S(0), W(1), S(1), W(2), S(2), S(3), W(3), scatter.over_last, S(4), K(0),
        scatter.over_inner, K(1), S(5), norm_low, norm_top,
    ):
        step()
    gmail.finish()
    mail.finish()
    for copy in started:
        copy.wait()


def feed_forward(gain2, own, mixed, own_cots, cots, feed):
    group = (TENSOR, ROWS, WIDTH)
    blocks = (8, 3 * UNITS, ROWS)
    return pl.pallas_call(
        feed_kernel,
        out_shape=(
            jax.ShapeDtypeStruct((2, WIDTH), F32),
            jax.ShapeDtypeStruct((ROWS, WIDTH), BF16),
            jax.ShapeDtypeStruct((ROWS, WIDTH), F32),
            jax.ShapeDtypeStruct(blocks, BF16),
            jax.ShapeDtypeStruct(group, BF16),
        ),
        in_specs=vmem(1) + anywhere(5),
        out_specs=tuple(vmem(1) + anywhere(4)),
        scratch_shapes=[
            pltpu.VMEM(group, BF16),
            pltpu.VMEM(group, BF16),
            pltpu.VMEM((3 * UNITS, WIDTH), BF16),
            pltpu.VMEM(group, BF16),
            pltpu.VMEM(group, BF16),
            pltpu.VMEM((3 * UNITS, GROUP), BF16),
            pltpu.VMEM((8, 2, 3 * UNITS, ROWS), BF16),
            pltpu.VMEM((scatter_rows_needed(TOP_FEED_BACK), WIDTH), BF16),
            pltpu.VMEM(blocks, BF16),
            pltpu.VMEM((ROWS, WIDTH), F32),
            pltpu.VMEM((ROWS, WIDTH), BF16),
            pltpu.VMEM((ROWS, WIDTH), F32),
            pltpu.VMEM((ROWS, WIDTH), F32),
            pltpu.VMEM((ROWS, WIDTH), BF16),
            *pairs(GATHER_MAILS),
            *pairs(SCATTER_MAILS),
            *pairs(8),
            pltpu.SemaphoreType.DMA((16,)),
            pltpu.SemaphoreType.DMA((11,)),
        ],
        compiler_params=params(1),
        name="feed_forward",
    )(gain2, own, mixed, own_cots, cots, feed)


TOP_GRADS, TOP_OUTS, TOP_BACK = 48, 32, 48

def attention_back_kernel(
    gain1,
    shift1,
    norm2_grads,
    own,
    grad_mixed_in,
    mixed_in,
    tokens_in,
    tables_in,
    start_in,
    acts_in,
    attended_in,
    logs_in,
    weights_in,
    halves,
    first_rows,
    outs,
    sums,
    layer_kept,
    token_kept,
    qkv_kept,
    out_kept,
    gate_up_kept,
    down_kept,
    layer_out,
    token_grad,
    qkv_grad,
    out_grad,
    feed_grad,
    grad_mixed,
    mixed,
    tokens,
    tables,
    start_lanes,
    acts,
    attended,
    logs,
    weights,
    rows,
    before,
    grad_out,
    grads_qkv,
    keys_turned,
    turns,
    parts,
    out_parts,
    grads,
    land,
    out_land,
    core_land,
    w_land,
    f_land,
    own_halves,
    total,
    boxes,
    g_sends,
    g_receives,
    s_sends,
    s_receives,
    o_sends,
    o_receives,
    k_sends,
    k_receives,
    w_sends,
    w_receives,
    f_sends,
    f_receives,
    a_sends,
    a_receives,
    local,
):
    a, r = Around(), Ring()
    gmail, mail, omail = Mail(g_sends, g_receives), Mail(s_sends, s_receives), Mail(o_sends, o_receives)
    kmail, wmail, fmail = Mail(k_sends, k_receives), Mail(w_sends, w_receives), Mail(f_sends, f_receives)
    amail = Mail(a_sends, a_receives)
    peers = a.peers() + a.to_rest[:1] + r.peers() + [r.to_zh_core]
    hail(peers)
    loads = {}
    for number, (name, source, target) in enumerate(
        (
            ("own", own, rows.at[a.me]),
            ("acts", acts_in, acts),
            ("attended", attended_in, attended),
            ("outs", outs, out_parts),
            ("weights", weights_in, weights),
            ("logs", logs_in, logs),
            ("start", start_in, start_lanes),
            ("half", halves.at[r.zh * 4 + r.x], own_halves.at[0]),
            ("other", halves.at[(1 - r.zh) * 4 + r.x], own_halves.at[1]),
            ("tables", tables_in, tables),
            ("before", first_rows, before),
            ("mixed", mixed_in, mixed),
            ("tokens", tokens_in, tokens),
            ("grad_mixed", grad_mixed_in, grad_mixed),
        )
    ):
        loads[name] = pltpu.make_async_copy(source, target, local.at[number])
        loads[name].start()

    started = []

    def keep(source, target, number):
        copy = pltpu.make_async_copy(source, target, local.at[number])
        copy.start()
        started.append(copy)

    def loaded(*names):
        for name in names:
            loads.pop(name).wait()

    hear(peers)
    gather = Gather(a, gmail, rows, TOP_GRADS, own)
    out_scatter = Scatter(a, omail, out_parts, out_land, TOP_OUTS)
    scatter = Scatter(a, mail, parts, land, TOP_BACK)
    every = EverySum(amail, boxes, sum_stages(a, r))
    feed_fold = Fold(r, fmail, halves, lambda side: own_halves[side], f_land)
    fold = Fold(r, wmail, core_land, lambda side: core_land[fold.place(side, 0)], w_land)

    def turn():
        loaded("acts", "attended")
        keys_turned[...] = acts[1].T
        turns[pl.ds(3 * LOCAL, LOCAL), :] = attended[...].T
        grads_qkv[1] = jnp.zeros((GROUP, LOCAL), F32)
        grads_qkv[2] = jnp.zeros((GROUP, LOCAL), F32)
        loaded("own", "outs", "weights", "logs", "start")

    def back_project(y):
        chunk = rows[pl.ds(2 * y, 2)].reshape(QBLOCK, WIDTH)
        first = pl.multiple_of(y * QBLOCK, QBLOCK)
        grad_out[pl.ds(first, QBLOCK), :] = dot(chunk, weights[3]).astype(BF16)

    state = {}

    def attend(first, heads):
        count = first + QBLOCK
        span = pl.ds(first, QBLOCK)
        query = acts[0, span, :] * BF16(SCALE)
        given = grad_out[span, :]
        row = lax.broadcasted_iota(jnp.int32, (count, QBLOCK), 0)
        column = first + lax.broadcasted_iota(jnp.int32, (count, QBLOCK), 1)
        allow = (row <= column) & (row.astype(F32) >= start_lanes[pl.ds(0, 1), span])
        overlap = given.astype(F32) * attended[span, :].astype(F32)
        lane = lax.broadcasted_iota(jnp.int32, (QBLOCK, LANES), 1)
        inner = jnp.zeros((QBLOCK, LANES), F32)
        for head in range(*heads):
            summed = jnp.sum(only(head_lanes(head, QBLOCK), overlap), axis=1, keepdims=True)
            inner = jnp.where(lane == head, summed, inner)
        inner = inner.T[:8]
        head_row = lax.broadcasted_iota(jnp.int32, (8, QBLOCK), 0)
        head_rows = lax.broadcasted_iota(jnp.int32, (LOCAL, count), 0) // HEAD_DIM

        def one_head(head, turned_query):
            mask = head_lanes(head, QBLOCK)
            masked, masked_given = only(mask, query), only(mask, given)
            log = jnp.sum(only(head_row == head, logs[:, span]), axis=0, keepdims=True)
            mean = jnp.sum(only(head_row == head, inner), axis=0, keepdims=True)
            scores = dot_t(acts[1, pl.ds(0, count), :], masked)
            probs = only(allow, jnp.exp(scores - log))
            grad_probs = dot_t(acts[2, pl.ds(0, count), :], masked_given)
            grad_scores = (probs * (grad_probs - mean)).astype(BF16)
            grads_qkv[2, pl.ds(0, count), :] += dot(probs.astype(BF16), masked_given)
            grads_qkv[1, pl.ds(0, count), :] += dot(grad_scores, masked)
            keys = only(head_rows == head, keys_turned[:, pl.ds(0, count)])
            return turned_query + dot(keys, grad_scores)

        so_far = state.pop("attend", jnp.zeros((LOCAL, QBLOCK), F32))
        so_far = lax.fori_loop(*heads, one_head, so_far)
        if heads[1] < HEADS_DEV:
            state["attend"] = so_far
        else:
            grads_qkv[0, span, :] = so_far.T * SCALE

    def input_grad(y):
        if "tables" in loads:
            loaded("tables", "before")
        first = pl.multiple_of(y * QBLOCK, QBLOCK)
        span = pl.ds(first, QBLOCK)
        back = jnp.zeros((QBLOCK, WIDTH), F32)
        new = []
        for c in range(3):
            pre = grads_qkv[c, span, :]
            if c < 2:
                pre = turned(pre, tables, first, -1.0)
            pre = pre.astype(BF16)
            new.append(jnp.sum(pre.astype(F32), axis=0, keepdims=True))
            back = back + dot_t(pre, weights[c])
            turns[pl.ds(c * LOCAL, LOCAL), span] = pre.T
        parts[pl.ds(2 * y, 2)] = back.astype(BF16).reshape(2, ROWS, WIDTH)
        state["bias"] = state.get("bias", 0.0) + jnp.concatenate(new, axis=0)

    def to_sibling(index):
        return kmail.copy(index, grads.at[index, 1 - r.core], core_land.at[index], r.to_core)

    def weight_grad(index, carry):
        columns = pl.ds(pl.multiple_of(index * 2 * ROWS, 2 * ROWS), 2 * ROWS)
        three = dot(
            turns[pl.ds(0, 3 * LOCAL), :], before[:, :, columns].reshape(GROUP, 2 * ROWS)
        )
        last = dot(turns[pl.ds(3 * LOCAL, LOCAL), :], rows[:, :, columns].reshape(GROUP, 2 * ROWS))
        for core in range(2):
            lanes = slice(core * ROWS, (core + 1) * ROWS)
            grads[index, core, pl.ds(0, 3 * LOCAL), :] = three[:, lanes].astype(BF16)
            grads[index, core, pl.ds(3 * LOCAL, LOCAL), :] = last[:, lanes].astype(BF16)
        to_sibling(index).start()
        return carry

    def weight_grads(first):
        lax.fori_loop(first, first + 2, weight_grad, 0)

    def core_sum(index, carry):
        to_sibling(index).wait()
        core_land[index] = added(grads[index, r.core], core_land[index]).astype(BF16)
        return carry

    def feed_cross():
        loaded("other")
        feed_fold.cross()

    def feed_result():
        loaded("half")
        feed_fold.near()
        feed_sum = feed_fold.result()
        feed_grad[...] = feed_sum
        keep(feed_grad.at[pl.ds(0, 2 * UNITS)], gate_up_kept, 14)
        keep(feed_grad.at[pl.ds(2 * UNITS, UNITS)], down_kept, 15)

    def weight_result():
        fold.near()
        shard = fold.result()
        for c in range(3):
            qkv_grad[c] = shard[c * LOCAL : (c + 1) * LOCAL].T
        out_grad[...] = shard[3 * LOCAL :]
        keep(qkv_grad, qkv_kept, 16)
        keep(out_grad, out_kept, 17)

    def layer_result():
        loaded("mixed")
        out_scatter.finish_top(total)
        out_scatter.finish_low(total)
        layer_out[...] = (mixed[...] + total[...]).astype(BF16)
        keep(layer_out, layer_kept, 18)

    def first_norm():
        loaded("tokens", "grad_mixed")
        mixed[...], state["rinv"] = normalized(tokens[...].astype(F32))

    def norm_half(first, number):
        half = pl.ds(first, HALF)
        rinv = state["rinv"][first : first + HALF]
        back = norm_back(total[half, :], mixed[half, :], rinv, gain1[...])
        token_grad[half, :] = (grad_mixed[half, :] + back).astype(BF16)
        keep(token_grad.at[half], token_kept.at[half], number)

    def norm_top():
        scatter.finish_top(total)
        norm_half(0, 19)

    def norm_low():
        scatter.finish_low(total)
        norm_half(HALF, 20)

    def norm1_sums(y):
        part = parts[pl.ds(2 * y, 2)].reshape(QBLOCK, WIDTH).astype(F32)
        scaled = before[pl.ds(2 * y, 2)].reshape(QBLOCK, WIDTH).astype(F32) - shift1[...]
        sums = jnp.concatenate(norm_sums(part, scaled), axis=0)
        state["norm1"] = sums + state["norm1"] if "norm1" in state else sums

    def by_lanes(*values):
        values = jnp.concatenate(values, axis=0)
        width = values.shape[1]
        return jnp.concatenate([values[:, k : k + LANES] for k in range(0, width, LANES)], axis=0)

    def first_sums():
        norm1 = state["norm1"]
        norms = by_lanes(norm1[:1] / gain1[...], norm1[1:], norm2_grads[...])
        spare = jnp.zeros((SUM_ROWS - NORM_ROWS - 3 * LOCAL // LANES, LANES), F32)
        every.first(jnp.concatenate([norms, by_lanes(state["bias"]), spare], axis=0))

    def last_sums():
        sums[pl.ds(0, NORM_ROWS), :] = every.take(3)
        sums[pl.ds(NORM_ROWS, SUM_ROWS - NORM_ROWS), :] = every.kept[NORM_ROWS:]

    G, O, S = gather.step, out_scatter.step, scatter.step

    def P(y):
        return partial(back_project, y)

    def A(q, *heads):
        return partial(attend, q * QBLOCK, heads)

    def I(y):
        return partial(input_grad, y)

    def N(y):
        return partial(norm1_sums, y)

    def W(index):
        return partial(weight_grads, 2 * index)

    def K(index):
        return partial(lax.fori_loop, 4 * index, 4 * index + 4, core_sum, 0)

    for step in (
        partial(gather.send, *range(6)), partial(feed_fold.send, *range(6)), turn, G(0), G(1), G(2),
        G(3), G(4), G(5), P(a.y), G(7), G(6), G(8), out_scatter.direct_across, G(10), G(11),
        out_scatter.direct_down, G(9), out_scatter.direct_up, G(15), G(16), G(12), P(a.y_down),
        P(a.y_up), G(14), O(2), G(13), P(a.y_far), A(0, 0, 4), A(1, 0, 2), O(1), A(1, 2, 4),
        A(2, 0, 1), A(2, 1, 2), O(17), O(0), O(4), feed_cross, A(2, 2, 3), O(3), A(2, 3, 4),
        A(3, 0, 1), A(3, 1, 2), A(3, 2, 3), A(3, 3, 4), I(a.y_far), I(a.y_up), I(a.y_down),
        scatter.from_down_pair, N(a.y_down), I(a.y), out_scatter.over_last, scatter.from_across,
        scatter.from_up_pair, W(0), feed_result, O(5), W(1), W(2), W(3), scatter.from_far_pair,
        N(a.y_far), N(a.y_up), out_scatter.over_inner, N(a.y), first_sums, K(0), K(1),
        partial(fold.send, *range(6)), S(0), every.second, S(4), S(1), S(17), S(3), S(2),
        scatter.over_last, scatter.over_inner, layer_result, every.third, first_norm, S(5),
        fold.cross, norm_low, every.fourth, norm_top, weight_result, last_sums,
    ):
        step()
    for some in (gmail, mail, omail, kmail, wmail, fmail, amail):
        some.finish()
    for copy in started:
        copy.wait()


def attention_backward(*operands):
    group = (TENSOR, ROWS, WIDTH)
    block, feed_block = (4 * LOCAL, ROWS), (3 * UNITS, ROWS)
    return pl.pallas_call(
        attention_back_kernel,
        out_shape=(
            jax.ShapeDtypeStruct((SUM_ROWS, LANES), F32),
            jax.ShapeDtypeStruct((ROWS, WIDTH), BF16),
            jax.ShapeDtypeStruct((ROWS, WIDTH), BF16),
            jax.ShapeDtypeStruct((3, ROWS, LOCAL), F32),
            jax.ShapeDtypeStruct((LOCAL, ROWS), F32),
            jax.ShapeDtypeStruct((2 * UNITS, ROWS), F32),
            jax.ShapeDtypeStruct((UNITS, ROWS), F32),
        ),
        in_specs=vmem(3) + anywhere(13),
        out_specs=tuple(vmem(1) + anywhere(6)),
        scratch_shapes=[
            pltpu.VMEM((ROWS, WIDTH), BF16),
            pltpu.VMEM((ROWS, WIDTH), BF16),
            pltpu.VMEM((3, ROWS, LOCAL), F32),
            pltpu.VMEM((LOCAL, ROWS), F32),
            pltpu.VMEM(feed_block, F32),
            pltpu.VMEM((ROWS, WIDTH), F32),
            pltpu.VMEM((ROWS, WIDTH), F32),
            pltpu.VMEM((ROWS, WIDTH), BF16),
            pltpu.VMEM((3, GROUP, LANES), F32),
            pltpu.VMEM((8, GROUP), F32),
            pltpu.VMEM((3, GROUP, LOCAL), BF16),
            pltpu.VMEM((GROUP, LOCAL), BF16),
            pltpu.VMEM((8, GROUP), F32),
            pltpu.VMEM((4, WIDTH, LOCAL), BF16),
            pltpu.VMEM(group, BF16),
            pltpu.VMEM(group, BF16),
            pltpu.VMEM((GROUP, LOCAL), BF16),
            pltpu.VMEM((3, GROUP, LOCAL), F32),
            pltpu.VMEM((LOCAL, GROUP), BF16),
            pltpu.VMEM((4 * LOCAL, GROUP), BF16),
            pltpu.VMEM(group, BF16),
            pltpu.VMEM(group, BF16),
            pltpu.VMEM((8, 2) + block, BF16),
            pltpu.VMEM((scatter_rows_needed(TOP_BACK), WIDTH), BF16),
            pltpu.VMEM((scatter_rows_needed(TOP_OUTS), WIDTH), BF16),
            pltpu.VMEM((8,) + block, BF16),
            pltpu.VMEM((FOLD_MAILS,) + block, BF16),
            pltpu.VMEM((FOLD_MAILS,) + feed_block, BF16),
            pltpu.VMEM((2,) + feed_block, BF16),
            pltpu.VMEM((ROWS, WIDTH), F32),
            pltpu.VMEM((SUM_BOXES, SUM_ROWS, LANES), F32),
            *pairs(GATHER_MAILS),
            *pairs(SCATTER_MAILS),
            *pairs(SCATTER_MAILS),
            *pairs(8),
            *pairs(FOLD_MAILS),
            *pairs(FOLD_MAILS),
            *pairs(SUM_MAILS),
            pltpu.SemaphoreType.DMA((21,)),
        ],
        compiler_params=params(2),
        name="attention_backward",
    )(*operands)


def results_kernel(
    sums, layer_in, token_in, qkv_in, out_in, gate_up_in, down_in, layer, token, qkv, out, gate_up, down, *norms
):
    bias = norms[4]
    for source, target in (
        (layer_in, layer),
        (token_in, token),
        (qkv_in, qkv),
        (out_in, out),
        (gate_up_in, gate_up),
        (down_in, down),
    ):
        target[...] = source[...]
    for k in range(WIDTH // LANES):
        for number in range(4):
            norms[number][pl.ds(k, 1), :] = sums[pl.ds(4 * k + number, 1), :]
    for k in range(LOCAL // LANES):
        bias[:, pl.ds(k * LANES, LANES)] = sums[pl.ds(NORM_ROWS + 3 * k, 3), :]


def results(*values):
    shapes = [jax.ShapeDtypeStruct(item.shape, item.dtype) for item in values[1:]]
    shapes += [jax.ShapeDtypeStruct((WIDTH // LANES, LANES), F32)] * 4
    shapes.append(jax.ShapeDtypeStruct((3, LOCAL), F32))
    return pl.pallas_call(
        results_kernel,
        out_shape=tuple(shapes),
        in_specs=vmem(7),
        out_specs=tuple(vmem(len(shapes))),
        name="results",
    )(*values)


def body(
    tokens,
    doc_ids,
    qkv_weight,
    qkv_bias,
    out_weight,
    norm1_gain,
    norm1_shift,
    norm2_gain,
    norm2_shift,
    gate_up_weight,
    down_weight,
    cotangent,
):
    norms = [item[None] for item in (norm1_gain, norm1_shift, norm2_gain, norm2_shift)]
    frequency = np.power(10000.0, -2.0 * np.arange(ROT // 2) / ROT).astype(np.float32)
    frequency = jnp.asarray(np.tile(frequency[:, None], (1, LANES)))
    gate_up = jnp.swapaxes(gate_up_weight, 1, 2).reshape(2 * UNITS, ROWS)
    start, logs, normed2, mixed, tables, acts, attended, rows, weights, cots, feed = attention_forward(
        tokens,
        doc_ids[None],
        qkv_bias,
        out_weight,
        norms,
        frequency,
        qkv_weight,
        gate_up,
        down_weight,
        cotangent,
    )
    norm2_grads, branch_grad, grad_mixed, halves, outs = feed_forward(
        norms[2], normed2, mixed, cotangent, cots, feed
    )
    backward = attention_backward(
        norms[0],
        norms[1],
        norm2_grads,
        branch_grad,
        grad_mixed,
        mixed,
        tokens,
        tables,
        start,
        acts,
        attended,
        logs,
        weights,
        halves,
        rows,
        outs,
    )
    layer_out, token_grad, qkv_grad, out_grad, gate_up_grad, down_grad, *sums = results(*backward)
    return (
        layer_out,
        token_grad,
        qkv_grad,
        sums[4],
        out_grad,
        sums[0].reshape(WIDTH),
        sums[1].reshape(WIDTH),
        sums[2].reshape(WIDTH),
        sums[3].reshape(WIDTH),
        jnp.swapaxes(gate_up_grad.reshape(2, UNITS, ROWS), 1, 2),
        down_grad,
    )


def solution(mesh):
    in_specs = (
        P(("dp", "tensor"), None),
        P(("dp", "tensor")),
        P(None, "dp", "tensor"),
        P(None, "tensor"),
        P("tensor", "dp"),
        P(),
        P(),
        P(),
        P(),
        P(None, "dp", "tensor"),
        P("tensor", "dp"),
        P(("dp", "tensor"), None),
    )
    out_specs = (
        P(("dp", "tensor"), None),
        P(("dp", "tensor"), None),
        P(None, "dp", "tensor"),
        P(None, "tensor"),
        P("tensor", "dp"),
        P(),
        P(),
        P(),
        P(),
        P(None, "dp", "tensor"),
        P("tensor", "dp"),
    )
    return jax.shard_map(body, mesh=mesh, in_specs=in_specs, out_specs=out_specs, check_vma=False)
```

```python
from functools import partial

import jax
import jax.numpy as jnp
import numpy as np
from jax import lax
from jax.experimental import pallas as pl
from jax.experimental.pallas import tpu as pltpu
from jax.sharding import PartitionSpec as P

HEAD_DIM = 64
ROT = 16
DOCS = 4
EPS = 1e-05
SCALE = HEAD_DIM ** (-0.5)

ROWS = 128
WIDTH = 2048
TENSOR = 8
GROUP = ROWS * TENSOR
HALF = ROWS // 2
HEADS_DEV = 4
LOCAL = HEADS_DEV * HEAD_DIM
QBLOCK = 256
UNITS = 704
LANES = 128
MESH = pl.DeviceIdType.MESH
BF16 = jnp.bfloat16
F32 = jnp.float32
VMEM_LIMIT = 62 * 2**20


class Around:
    def __init__(self):
        dp, tensor = lax.axis_index("dp"), lax.axis_index("tensor")
        y, z = tensor // 2, lax.rem(tensor, 2)
        up, down, far = lax.rem(y + 1, 4), lax.rem(y + 3, 4), lax.rem(y + 2, 4)
        other = 1 - z
        self.me, self.across = y * 2 + z, y * 2 + other
        self.up, self.down, self.far = up * 2 + z, down * 2 + z, far * 2 + z
        self.up_o, self.down_o, self.far_o = up * 2 + other, down * 2 + other, far * 2 + other
        self.y, self.z = y, z
        self.y_up, self.y_down, self.y_far = up, down, far
        self.to_up, self.to_down, self.to_across = (dp, self.up), (dp, self.down), (dp, self.across)
        self.to_rest = [(dp, slot) for slot in (self.far, self.up_o, self.down_o, self.far_o)]

    def peers(self):
        return [self.to_up, self.to_down, self.to_across]


class Ring:
    def __init__(self):
        dp, tensor = lax.axis_index("dp"), lax.axis_index("tensor")
        zh, x, core = dp // 8, lax.rem(dp // 2, 4), lax.rem(dp, 2)
        self.zh, self.x, self.core, self.dp, self.tensor = zh, x, core, dp, tensor
        self.xs = [lax.rem(x + step, 4) for step in range(4)]
        self.to_x = [(self.index(zh, self.xs[step], core), tensor) for step in range(4)]
        self.to_zh = (self.index(1 - zh, x, core), tensor)
        self.to_core = (self.index(zh, x, 1 - core), tensor)
        self.to_zh_core = (self.index(1 - zh, x, 1 - core), tensor)

    def index(self, zh, x, core):
        return zh * 8 + x * 2 + core

    def peers(self):
        return self.to_x[1:] + [self.to_zh, self.to_core]


def hail(peers):
    barrier = pltpu.get_barrier_semaphore()
    for peer in peers:
        pl.semaphore_signal(barrier, inc=1, device_id=peer, device_id_type=MESH)


def hear(peers):
    pl.semaphore_wait(pltpu.get_barrier_semaphore(), len(peers))


class Mail:
    def __init__(self, sends, receives):
        self.sends, self.receives = sends, receives
        self.out = []

    def copy(self, number, source, target, device):
        return pltpu.make_async_remote_copy(
            src_ref=source,
            dst_ref=target,
            send_sem=self.sends.at[number],
            recv_sem=self.receives.at[number],
            device_id=device,
            device_id_type=MESH,
        )

    def send(self, number, source, target, device):
        copy = self.copy(number, source, target, device)
        copy.start()
        self.out.append(copy)

    def landed(self, number, target, device):
        self.copy(number, target, target, device).wait_recv()

    def finish(self):
        for copy in self.out:
            copy.wait_send()
        self.out = []


MIDDLE = {64: 96, 48: 96, 32: 80}
GATHER_MAILS = 17


class Gather:
    def __init__(self, around, mail, rows, top, own=None):
        a, middle = around, MIDDLE[top]
        self.mail, self.rows, self.own = mail, rows, own
        self.messages = [
            (a.to_up, a.me, 0, HALF, a.down),
            (a.to_down, a.me, HALF, ROWS, a.up),
            (a.to_across, a.me, top, ROWS, a.across),
            (a.to_up, a.me, HALF, ROWS, a.down),
            (a.to_down, a.me, 0, HALF, a.up),
            (a.to_across, a.me, 0, top, a.across),
            (a.to_up, a.down, 0, HALF, a.far),
            (a.to_across, a.down, 0, top, a.down_o),
            (a.to_down, a.up, HALF, ROWS, a.far),
            (a.to_up, a.across, top, middle, a.down_o),
            (a.to_down, a.across, middle, ROWS, a.up_o),
            (a.to_across, a.up, 0, top, a.up_o),
            (a.to_across, a.far, 0, top, a.far_o),
            (a.to_up, a.down_o, top, middle, a.far_o),
            (a.to_down, a.up_o, middle, ROWS, a.far_o),
            (a.to_up, a.across, middle, ROWS, a.down_o),
            (a.to_down, a.across, top, middle, a.up_o),
        ]

    def part(self, slot, first, last):
        return self.rows.at[slot, pl.ds(first, last - first)]

    def send(self, *numbers):
        for number in numbers:
            device, slot, first, last, _ = self.messages[number]
            target = source = self.part(slot, first, last)
            if number < 6 and self.own is not None:
                source = self.own.at[pl.ds(first, last - first)]
            self.mail.send(number, source, target, device)

    def step(self, number):
        return partial(self.on, number)

    def on(self, number):
        device, _, first, last, slot = self.messages[number]
        self.mail.landed(number, self.part(slot, first, last), device)
        followers = {0: (6, 7), 1: (8,), 2: (9, 10, 15, 16), 4: (11,), 6: (12,), 9: (13,), 10: (14,)}
        self.send(*followers.get(number, ()))


def added(*terms):
    total = terms[0].astype(F32)
    for term in terms[1:]:
        total = total + term.astype(F32)
    return total


SCATTER_MAILS = 21


def scatter_boxes(top):
    middle = MIDDLE[top]
    last, inner, rest = ROWS - middle, middle - top, HALF - top
    counts = (last, inner, top, HALF, top, top, last, inner, HALF, top)
    counts += (top, inner, last, HALF, top, top, inner, rest, rest, rest, last, inner, last)
    order = [*range(17), 20, 17, 18, 19, 21, 22]
    firsts = [0] * len(counts)
    for before, number in zip(order, order[1:]):
        firsts[number] = firsts[before] + counts[before]
    return counts, tuple(firsts)


def scatter_rows_needed(top):
    return sum(scatter_boxes(top)[0])


class Scatter:
    def __init__(self, around, mail, parts, land, top):
        self.a, self.mail, self.parts, self.land, self.top = around, mail, parts, land, top
        self.middle = MIDDLE[top]
        self.counts, self.firsts = scatter_boxes(top)
        self.crossed = False

    def part(self, slot, first, last):
        return self.parts.at[slot, pl.ds(first, last - first)]

    def box(self, number):
        return self.land.at[pl.ds(self.firsts[number], self.counts[number])]

    def got(self, number):
        self.mail.landed(number, self.box(number), self.a.to_up)

    def fold(self, stage, slot, first, *others):
        terms = [self.part(slot, first, first + self.counts[stage])[...], self.box(stage)[...]]
        terms += [self.box(other)[...] for other in others]
        self.box(stage)[...] = added(*terms).astype(BF16)

    def direct(self, *numbers):
        a, top, middle = self.a, self.top, self.middle
        messages = {
            0: (a.far_o, middle, a.to_up),
            1: (a.far_o, top, a.to_down),
            2: (a.far_o, 0, a.to_across),
            3: (a.far, HALF, a.to_up),
            17: (a.far, top, a.to_down),
            4: (a.up_o, 0, a.to_across),
            7: (a.up_o, top, a.to_up),
            5: (a.down_o, 0, a.to_across),
            6: (a.down_o, middle, a.to_down),
            18: (a.up, top, a.to_up),
            8: (a.down, HALF, a.to_down),
            9: (a.across, 0, a.to_across),
        }
        for number in numbers:
            slot, first, device = messages[number]
            source = self.part(slot, first, first + self.counts[number])
            self.mail.send(number, source, self.box(number), device)

    def from_far_pair(self):
        self.direct(0, 1, 2, 3, 17)

    def from_up_pair(self):
        self.direct(7, 4, 18)

    def from_down_pair(self):
        self.direct(6, 5, 8)

    def from_across(self):
        self.direct(9)

    def direct_up(self):
        self.direct(0, 3, 7, 18)

    def direct_down(self):
        self.direct(1, 17, 6, 8)

    def direct_across(self):
        self.direct(2, 4, 5, 9)

    def step(self, number):
        return partial(self.on, number)

    def on(self, number):
        a, box = self.a, self.box
        follower, slot, first, device, *others = {
            1: (11, a.down_o, self.top, a.to_down),
            0: (12, a.up_o, self.middle, a.to_up),
            2: (10, a.far, 0, a.to_down),
            3: (13, a.up, HALF, a.to_up),
            17: (19, a.down, self.top, a.to_down),
            4: (14, a.up, 0, a.to_up),
            5: (15, a.down, 0, a.to_down, 10),
        }[number]
        for other in (number, *others):
            self.got(other)
        self.fold(number, slot, first, *others)
        self.mail.send(follower, box(number), box(follower), device)

    def over(self, number, made, first, *landed):
        for other in landed:
            self.got(other)
        own = self.part(self.a.across, first, first + self.counts[number])
        terms = [own[...]] + [self.box(other)[...] for other in landed]
        self.box(made)[...] = added(*terms).astype(BF16)
        self.mail.send(number, self.box(made), self.box(number), self.a.to_across)

    def over_inner(self):
        self.over(16, 21, self.top, 7, 11)

    def over_last(self):
        self.over(20, 22, self.middle, 6, 12)

    def all_direct(self):
        self.direct(0, 1, 2, 3, 17, 7, 4, 6, 5, 18, 8, 9)

    def boxed(self, number, first, last):
        return self.land[pl.ds(self.firsts[number] + first, last - first), :]

    def finish_top(self, total):
        a, top = self.a, self.top
        for number in (9, 14, 15, 18, 19):
            self.got(number)
        if not self.crossed:
            self.got(16)
            self.crossed = True
        total[pl.ds(0, top), :] = added(
            self.part(a.me, 0, top)[...], *(self.box(k)[...] for k in (9, 14, 15))
        )
        total[pl.ds(top, HALF - top), :] = added(
            self.part(a.me, top, HALF)[...],
            self.box(18)[...],
            self.box(19)[...],
            self.boxed(16, 0, HALF - top),
        )

    def finish_low(self, total):
        for number in (8, 13, 20):
            self.got(number)
        if not self.crossed:
            self.got(16)
            self.crossed = True
        total[pl.ds(HALF, HALF), :] = added(
            self.part(self.a.me, HALF, ROWS)[...],
            self.box(8)[...],
            self.box(13)[...],
            self.boxed(16, HALF - self.top, ROWS - self.top),
        )


class Spread:
    def __init__(self, ring, mail, block, own_shard=None):
        r = self.r = ring
        self.mail, self.block, self.own = mail, block, own_shard
        own, cross = (r.zh, r.x), (1 - r.zh, r.x)
        self.messages = [(r.to_zh, own, cross)]
        self.messages += [(r.to_x[k], own, (r.zh, r.xs[4 - k])) for k in (1, 2, 3)]
        self.messages += [(r.to_x[k], cross, (1 - r.zh, r.xs[4 - k])) for k in (1, 2, 3)]
        self.messages += [(r.to_core, own, own), (r.to_core, cross, cross)]
        self.messages += [(r.to_core, self.messages[k][2], self.messages[k][2]) for k in range(1, 7)]

    def send(self, number):
        device, place, _ = self.messages[number]
        block = self.block(*place, self.r.core)
        source = self.own if self.own is not None and number in (0, 1, 2, 3, 7) else block
        self.mail.send(number, source, block, device)

    def step(self, number):
        return partial(self.on, number)

    def begin(self):
        for number in (0, 1, 3, 2, 7):
            self.send(number)

    def on(self, number):
        device, _, place = self.messages[number]
        core = self.r.core if number < 7 else 1 - self.r.core
        self.mail.landed(number, self.block(*place, core), device)
        if number == 0:
            for follower in (4, 6, 5, 8):
                self.send(follower)
        elif number < 7:
            self.send(number + 8)

    def finish(self):
        for number in range(7, SPREAD_MAILS):
            self.on(number)


SPREAD_MAILS = 15
FOLDS = [(side, step) for step in (1, 3, 2, 0) for side in (1, 0)]


class Fold:
    def __init__(self, ring, mail, grads, own, land):
        self.r, self.mail, self.grads, self.own, self.land = ring, mail, grads, own, land

    def place(self, side, step):
        zh = 1 - self.r.zh if side else self.r.zh
        return zh * 4 + self.r.xs[step]

    def send(self, *numbers):
        for number in numbers:
            side, step = FOLDS[number]
            source = self.grads.at[self.place(side, step)]
            self.mail.send(number, source, self.land.at[number], self.r.to_x[step])

    def cross(self):
        for number in (0, 2, 4):
            self.mail.landed(number, self.land.at[number], self.r.to_core)
        self.land[0] = added(self.own(1), self.land[0], self.land[2], self.land[4]).astype(BF16)
        self.mail.send(6, self.land.at[0], self.land.at[6], self.r.to_zh)

    def near(self):
        for number in (1, 3, 5):
            self.mail.landed(number, self.land.at[number], self.r.to_core)

    def result(self):
        self.mail.landed(6, self.land.at[6], self.r.to_core)
        land = self.land
        return added(self.own(0), land[1], land[3], land[5], land[6])


FOLD_MAILS = 7

SUM_ROWS, NORM_ROWS = 72, 64
SUM_BOXES, SUM_MAILS = 14, 13


class EverySum:
    def __init__(self, mail, boxes, stages):
        self.mail, self.boxes, self.stages = mail, boxes, stages

    def give(self, stage, values):
        base, count, mine, _, peers = self.stages[stage]
        view = pl.ds(0, count)
        self.boxes[base + mine, view] = values
        for number, peer in enumerate(peers):
            box = self.boxes.at[base + mine, view]
            self.mail.send(base + number, box, box, peer)

    def take(self, stage):
        base, count, _, sources, peers = self.stages[stage]
        view = pl.ds(0, count)
        for number, source in enumerate(sources):
            self.mail.landed(base + number, self.boxes.at[base + source, view], peers[0])
        result = self.boxes[base, view]
        for k in range(1, len(peers) + 1):
            result = result + self.boxes[base + k, view]
        return result

    def first(self, values):
        self.give(0, values)

    def second(self):
        self.give(1, self.take(0))

    def third(self):
        self.kept = self.take(1)
        self.give(2, self.kept[: self.stages[2][1]])

    def fourth(self):
        self.give(3, self.take(2))


def sum_stages(a, r):
    crossed = 1 - r.zh
    place = r.zh * 2 + r.core
    sources = [crossed * 2 + r.core, r.zh * 2 + 1 - r.core, crossed * 2 + 1 - r.core]
    y_sources, y_peers = [a.y_down, a.y_far, a.y_up], [a.to_up, a.to_rest[0], a.to_down]
    return [
        (0, SUM_ROWS, r.x, [r.xs[3], r.xs[2], r.xs[1]], r.to_x[1:]),
        (4, SUM_ROWS, place, sources, [r.to_zh, r.to_core, r.to_zh_core]),
        (8, NORM_ROWS, a.y, y_sources, y_peers),
        (12, NORM_ROWS, a.z, [1 - a.z], [a.to_across]),
    ]


def dot(left, right):
    return lax.dot_general(left, right, (((1,), (0,)), ((), ())), preferred_element_type=F32)


def dot_t(left, right):
    return lax.dot_general(left, right, (((1,), (1,)), ((), ())), preferred_element_type=F32)


def normalized(values):
    centred = values - jnp.mean(values, axis=1, keepdims=True)
    variance = jnp.mean(centred * centred, axis=1, keepdims=True)
    rinv = lax.rsqrt(variance + EPS)
    return centred * rinv, rinv


def norm_sums(incoming, normal):
    return jnp.sum(incoming * normal, axis=0, keepdims=True), jnp.sum(incoming, axis=0, keepdims=True)


def norm_back(incoming, normal, rinv, gain):
    scaled = incoming * gain
    inner = scaled - jnp.mean(scaled, axis=1, keepdims=True)
    return rinv * (inner - normal * jnp.mean(scaled * normal, axis=1, keepdims=True))


def turned(values, tables, first, sign):
    rows = pl.ds(first, values.shape[0])
    cosine, minus, plus = tables[0, rows], tables[1, rows], tables[2, rows]
    halves = []
    for lane in range(0, LOCAL, LANES):
        part = values[:, lane : lane + LANES]
        left = pltpu.roll(part, LANES - ROT // 2, 1)
        right = pltpu.roll(part, ROT // 2, 1)
        halves.append(part * cosine + sign * (left * minus + right * plus))
    return jnp.concatenate(halves, axis=1)


def head_lanes(head, rows):
    return lax.broadcasted_iota(jnp.int32, (rows, LOCAL), 1) // HEAD_DIM == head


def only(mask, values):
    return jnp.where(mask, values, jnp.zeros_like(values))


def place_rows(id_rows, frequency, tables, start_rows, start_lanes):
    ids = jnp.max(id_rows[...], axis=1)
    shape = (TENSOR, ROWS)
    index = lax.broadcasted_iota(jnp.int32, shape, 0) * ROWS
    index = (index + lax.broadcasted_iota(jnp.int32, shape, 1)).astype(F32)
    offset = jnp.zeros(shape, F32)
    for number in range(1, DOCS):
        before = ((ids >= 0) & (ids < number)).astype(F32)
        count = jnp.sum(jnp.sum(before, axis=1, keepdims=True), axis=0, keepdims=True)
        offset = jnp.where(ids == number, count, offset)
    start = jnp.where(ids >= 0, offset, index)
    position = index - offset

    def along(values):
        return jnp.concatenate([values[t : t + 1] for t in range(TENSOR)], axis=1)

    angle = frequency[:, :1] * along(position)
    cosine, sine = jnp.cos(angle), jnp.sin(angle)
    none = jnp.zeros_like(sine)
    rest = (HEAD_DIM - ROT) // 8
    columns = (
        [cosine, cosine] + [jnp.ones_like(sine)] * rest,
        [-sine, none] + [none] * rest,
        [none, sine] + [none] * rest,
    )
    for number, parts in enumerate(columns):
        tables[number] = jnp.concatenate(parts + parts, axis=0).T
    lanes = jnp.broadcast_to(along(start), (8, GROUP))
    start_lanes[...] = lanes
    start_rows[...] = jnp.concatenate([lanes] * (LANES // 8), axis=0).T


def vmem(count):
    return [pl.BlockSpec(memory_space=pltpu.VMEM)] * count


def anywhere(count):
    return [pl.BlockSpec(memory_space=pl.ANY)] * count


def pairs(count):
    return [pltpu.SemaphoreType.DMA((count,)), pltpu.SemaphoreType.DMA((count,))]


def params(collective):
    return pltpu.CompilerParams(
        collective_id=collective, has_side_effects=True, vmem_limit_bytes=VMEM_LIMIT
    )


TOP_ROWS, TOP_COTS, TOP_BRANCH = 32, 48, 48


def attention_kernel(
    tokens,
    ids,
    bias,
    out_shard,
    gain1,
    shift1,
    gain2,
    shift2,
    frequency,
    qkv_shard,
    gate_up,
    down,
    own_cots,
    start_lanes,
    logs,
    normed2_kept,
    mixed_kept,
    tables_kept,
    acts_kept,
    attended_kept,
    rows_kept,
    weights_kept,
    cots,
    feed,
    rows,
    weights,
    feed_own,
    cots_own,
    tables,
    acts,
    attended,
    mixed,
    normed2,
    id_rows,
    start_rows,
    parts,
    land,
    total,
    r_sends,
    r_receives,
    c_sends,
    c_receives,
    b_sends,
    b_receives,
    w_sends,
    w_receives,
    f_sends,
    f_receives,
    i_sends,
    i_receives,
    local,
):
    a, r = Around(), Ring()
    rmail, cmail, bmail = Mail(r_sends, r_receives), Mail(c_sends, c_receives), Mail(b_sends, b_receives)
    wmail, fmail, imail = Mail(w_sends, w_receives), Mail(f_sends, f_receives), Mail(i_sends, i_receives)
    peers = a.peers() + a.to_rest + r.peers()
    hail(peers)

    def weight_block(zh, x, core):
        first = pl.multiple_of(r.index(zh, x, core) * ROWS, ROWS)
        return weights.at[:, pl.ds(first, ROWS), :]

    mine = pl.multiple_of(r.dp * ROWS, ROWS)
    loads = [
        pltpu.make_async_copy(qkv_shard, weights.at[pl.ds(0, 3), pl.ds(mine, ROWS)], local.at[0]),
        pltpu.make_async_copy(gate_up, feed_own.at[pl.ds(0, 2 * UNITS)], local.at[1]),
        pltpu.make_async_copy(down, feed_own.at[pl.ds(2 * UNITS, UNITS)], local.at[2]),
        pltpu.make_async_copy(own_cots, cots_own, local.at[3]),
    ]
    for copy in loads:
        copy.start()
    id_rows[a.me] = jnp.broadcast_to(ids[...], (8, ROWS))

    def first_norm(first):
        half = pl.ds(first, HALF)
        normal, _ = normalized(tokens[half, :].astype(F32))
        rows[a.me, half] = (normal * gain1[...] + shift1[...]).astype(BF16)

    first_norm(0)
    hear(peers)

    group = [
        (0, a.to_up, a.down),
        (1, a.to_down, a.up),
        (2, a.to_across, a.across),
        (3, a.to_rest[0], a.far),
        (4, a.to_rest[1], a.down_o),
        (5, a.to_rest[2], a.up_o),
        (6, a.to_rest[3], a.far_o),
    ]
    gather = Gather(a, rmail, rows, TOP_ROWS)
    others = Gather(a, cmail, cots, TOP_COTS, cots_own)
    spread = Spread(r, wmail, weight_block)
    feeds = Spread(r, fmail, lambda zh, x, core: feed.at[r.index(zh, x, core)], feed_own)
    scatter = Scatter(a, bmail, parts, land, TOP_BRANCH)
    started = []

    def keep(source, target, number):
        copy = pltpu.make_async_copy(source, target, local.at[number])
        copy.start()
        started.append(copy)

    def begin():
        gather.send(0)
        for number, device, _ in group:
            imail.send(number, id_rows.at[a.me], id_rows.at[a.me], device)
        first_norm(HALF)
        gather.send(1, 2)
        weights[3, pl.ds(mine, ROWS), :] = out_shard[...].T
        loads[0].wait()
        spread.begin()
        gather.send(3, 4, 5)
        for copy in loads[1:]:
            copy.wait()
        keep(feed_own, feed.at[r.dp], 4)
        keep(cots_own, cots.at[a.me], 5)

    def place():
        for number, _, slot in group:
            imail.landed(number, id_rows.at[slot], a.to_up)
        place_rows(id_rows, frequency, tables, start_rows, start_lanes)
        keep(tables, tables_kept, 6)

    def P(y):
        return partial(project, y)

    def project(y):
        first = pl.multiple_of(y * QBLOCK, QBLOCK)
        chunk = rows[pl.ds(2 * y, 2)].reshape(QBLOCK, WIDTH)
        for c in range(3):
            pre = dot(chunk, weights[c]) + bias[pl.ds(c, 1), :]
            if c < 2:
                pre = turned(pre, tables, first, 1.0)
            acts[c, pl.ds(first, QBLOCK), :] = pre.astype(BF16)

    state = {}

    def A(q, *heads):
        return partial(attend, q * QBLOCK, heads)

    def attend(first, heads):
        count = first + QBLOCK
        query = acts[0, pl.ds(first, QBLOCK), :] * BF16(SCALE)
        row = first + lax.broadcasted_iota(jnp.int32, (QBLOCK, count), 0)
        column = lax.broadcasted_iota(jnp.int32, (QBLOCK, count), 1)
        start = start_rows[pl.ds(first, QBLOCK), pl.ds(0, 1)]
        allow = (column <= row) & (column.astype(F32) >= start)
        lane = lax.broadcasted_iota(jnp.int32, (QBLOCK, LANES), 1)

        def one_head(head, carry):
            out, log = carry
            masked = only(head_lanes(head, QBLOCK), query)
            scores = dot_t(masked, acts[1, pl.ds(0, count), :])
            scores = jnp.where(allow, scores, -1e30)
            highest = jnp.max(scores, axis=1, keepdims=True)
            expon = jnp.exp(scores - highest)
            sums = jnp.sum(expon, axis=1, keepdims=True)
            values = only(head_lanes(head, count), acts[2, pl.ds(0, count), :])
            out = out + dot(expon.astype(BF16), values) / sums
            log = jnp.where(lane == head, highest + jnp.log(sums), log)
            return out, log

        zeros = (jnp.zeros((QBLOCK, LOCAL), F32), jnp.zeros((QBLOCK, LANES), F32))
        carry = lax.fori_loop(*heads, one_head, state.pop("attend", zeros))
        if heads[1] < HEADS_DEV:
            state["attend"] = carry
            return
        out = carry[0].astype(BF16)
        attended[pl.ds(first, QBLOCK), :] = out
        logs[:, pl.ds(first, QBLOCK)] = carry[1].T[:8]
        branch = dot_t(out, weights[3]).astype(BF16)
        parts[first // ROWS] = branch[:ROWS]
        parts[first // ROWS + 1] = branch[ROWS:]

    def branch_sums():
        keep(rows, rows_kept, 7)
        keep(weights, weights_kept, 8)
        keep(acts, acts_kept, 9)
        keep(attended, attended_kept, 10)
        scatter.all_direct()

    def norm_half(first, number):
        half = pl.ds(first, HALF)
        after = tokens[half, :].astype(F32) + total[half, :]
        mixed[half, :] = after
        keep(mixed.at[half], mixed_kept.at[half], number)
        normal, _ = normalized(after)
        normed2[half, :] = (normal * gain2[...] + shift2[...]).astype(BF16)
        keep(normed2.at[half], normed2_kept.at[half], number + 2)

    def norm_top():
        scatter.finish_top(total)
        norm_half(0, 11)

    def norm_low():
        scatter.finish_low(total)
        norm_half(HALF, 12)

    R, C, B, w, f = gather.step, others.step, scatter.step, spread.step, feeds.step
    C_up, C_down, C_across = (partial(others.send, *two) for two in ((0, 3), (1, 4), (2, 5)))
    for step in (
        begin, R(0), place, w(3), R(1), w(1), R(2), R(3), R(4), w(2), w(0), R(6), C_across,
        feeds.begin, R(8), R(5), R(7), R(9), C_up, R(10), C_down, R(11), w(4), w(6), R(15), R(16),
        R(12), R(13), w(5), R(14), spread.finish, P(a.y), C(2), P(a.y_up), C(0), C(1), P(a.y_down),
        C(5), P(a.y_far), A(0, 0, 4), C(3), f(1), f(3), A(1, 0, 2), C(4), A(1, 2, 4), A(2, 0, 1),
        C(9), C(10), A(2, 1, 2), A(2, 2, 3), C(15), A(2, 3, 4), A(3, 0, 1), A(3, 1, 2), A(3, 2, 3),
        f(2), A(3, 3, 4), branch_sums, C(8), C(6), C(7), C(16), f(0), C(14), C(13), C(11), B(0),
        B(1), B(2), B(17), B(3), B(4), f(4), f(6), scatter.over_last, scatter.over_inner, C(12),
        B(5), f(5), norm_low, norm_top, feeds.finish,
    ):
        step()
    for mail in (rmail, cmail, bmail, wmail, fmail, imail):
        mail.finish()
    for copy in started:
        copy.wait()


def attention_forward(tokens, ids, bias, out_shard, norms, frequency, qkv_shard, gate_up, down, cots):
    group = (TENSOR, ROWS, WIDTH)
    weights = (4, WIDTH, LOCAL)
    tables, acts = (3, GROUP, LANES), (3, GROUP, LOCAL)
    return pl.pallas_call(
        attention_kernel,
        out_shape=(
            jax.ShapeDtypeStruct((8, GROUP), F32),
            jax.ShapeDtypeStruct((8, GROUP), F32),
            jax.ShapeDtypeStruct((ROWS, WIDTH), BF16),
            jax.ShapeDtypeStruct((ROWS, WIDTH), F32),
            jax.ShapeDtypeStruct(tables, F32),
            jax.ShapeDtypeStruct(acts, BF16),
            jax.ShapeDtypeStruct((GROUP, LOCAL), BF16),
            jax.ShapeDtypeStruct(group, BF16),
            jax.ShapeDtypeStruct(weights, BF16),
            jax.ShapeDtypeStruct(group, BF16),
            jax.ShapeDtypeStruct((16, 3 * UNITS, ROWS), BF16),
        ),
        in_specs=vmem(9) + anywhere(4),
        out_specs=tuple(vmem(2) + anywhere(9)),
        scratch_shapes=[
            pltpu.VMEM(group, BF16),
            pltpu.VMEM(weights, BF16),
            pltpu.VMEM((3 * UNITS, ROWS), BF16),
            pltpu.VMEM((ROWS, WIDTH), BF16),
            pltpu.VMEM(tables, F32),
            pltpu.VMEM(acts, BF16),
            pltpu.VMEM((GROUP, LOCAL), BF16),
            pltpu.VMEM((ROWS, WIDTH), F32),
            pltpu.VMEM((ROWS, WIDTH), BF16),
            pltpu.VMEM((TENSOR, 8, ROWS), jnp.int32),
            pltpu.VMEM((GROUP, LANES), F32),
            pltpu.VMEM(group, BF16),
            pltpu.VMEM((scatter_rows_needed(TOP_BRANCH), WIDTH), BF16),
            pltpu.VMEM((ROWS, WIDTH), F32),
            *pairs(GATHER_MAILS),
            *pairs(GATHER_MAILS),
            *pairs(SCATTER_MAILS),
            *pairs(SPREAD_MAILS),
            *pairs(SPREAD_MAILS),
            *pairs(7),
            pltpu.SemaphoreType.DMA((15,)),
        ],
        compiler_params=params(0),
        name="attention_forward",
    )(tokens, ids, bias, out_shard, *norms, frequency, qkv_shard, gate_up, down, cots)


TOP_FEED, TOP_FEED_BACK = 64, 48

def feed_kernel(
    gain2,
    own,
    mixed_in,
    cots_own,
    cots_in,
    feed,
    norm_grads,
    branch_grad_kept,
    grad_mixed_kept,
    halves,
    outs_kept,
    rows,
    cots,
    weights,
    parts,
    outs,
    acts,
    grads,
    land,
    core_land,
    mixed,
    own_cots,
    total,
    grad_mixed,
    branch_grad,
    g_sends,
    g_receives,
    s_sends,
    s_receives,
    w_sends,
    w_receives,
    w_local,
    local,
):
    a, r = Around(), Ring()
    gmail, mail, wmail = Mail(g_sends, g_receives), Mail(s_sends, s_receives), Mail(w_sends, w_receives)
    peers = a.peers() + [r.to_core]
    hail(peers)
    first_load = pltpu.make_async_copy(own, rows.at[a.me], local.at[0])
    loads = [
        pltpu.make_async_copy(feed.at[n], weights.at[:, pl.ds(n * ROWS, ROWS)], w_local.at[n])
        for n in range(16)
    ]
    loads.append(pltpu.make_async_copy(cots_in, cots, local.at[1]))
    late_loads = [
        pltpu.make_async_copy(mixed_in, mixed, local.at[2]),
        pltpu.make_async_copy(cots_own, own_cots, local.at[3]),
    ]
    for copy in [first_load] + loads + late_loads:
        copy.start()
    hear(peers)
    gather = Gather(a, gmail, rows, TOP_FEED, own)
    scatter = Scatter(a, mail, parts, land, TOP_FEED_BACK)
    started = []

    def keep(source, target, number):
        copy = pltpu.make_async_copy(source, target, local.at[number])
        copy.start()
        started.append(copy)

    def load():
        for copy in [first_load] + loads:
            copy.wait()

    state = {}

    def pair(index, *slots):
        x = jnp.concatenate([rows[slot] for slot in slots], axis=0)
        given = jnp.concatenate([cots[slot] for slot in slots], axis=0)
        gate = dot_t(x, weights[pl.ds(0, UNITS), :])
        upward = dot_t(x, weights[pl.ds(UNITS, UNITS), :])
        grad_hidden = dot_t(given, weights[pl.ds(2 * UNITS, UNITS), :])
        sigma = jax.nn.sigmoid(gate)
        silu = gate * sigma
        hidden = (silu * upward).astype(BF16)
        grad_gate = (grad_hidden * upward * (sigma + silu * (1.0 - sigma))).astype(BF16)
        grad_up = (grad_hidden * silu).astype(BF16)
        state[index] = hidden, grad_gate, grad_up

    def pair_back(index, *slots):
        _, grad_gate, grad_up = state[index]
        back = dot(grad_gate, weights[pl.ds(0, UNITS), :])
        back = (back + dot(grad_up, weights[pl.ds(UNITS, UNITS), :])).astype(BF16)
        for number, slot in enumerate(slots):
            parts[slot] = back[number * ROWS : (number + 1) * ROWS]

    def rest(index, *slots):
        hidden, grad_gate, grad_up = state[index]
        out = dot(hidden, weights[pl.ds(2 * UNITS, UNITS), :]).astype(BF16)
        for number, slot in enumerate(slots):
            chunk = slice(number * ROWS, (number + 1) * ROWS)
            outs[slot] = out[chunk]
            lanes = pl.ds(pl.multiple_of(slot * ROWS, ROWS), ROWS)
            acts[pl.ds(0, UNITS), lanes] = grad_gate[chunk].T
            acts[pl.ds(UNITS, UNITS), lanes] = grad_up[chunk].T
            acts[pl.ds(2 * UNITS, UNITS), lanes] = hidden[chunk].T

    def to_sibling(index):
        return wmail.copy(index, grads.at[index, 1 - r.core], core_land.at[index], r.to_core)

    def weight_grad(index, carry):
        columns = pl.ds(pl.multiple_of(index * 2 * ROWS, 2 * ROWS), 2 * ROWS)
        both = dot(acts[pl.ds(0, 2 * UNITS), :], rows[:, :, columns].reshape(GROUP, 2 * ROWS))
        low = dot(acts[pl.ds(2 * UNITS, UNITS), :], cots[:, :, columns].reshape(GROUP, 2 * ROWS))
        for core in range(2):
            lanes = slice(core * ROWS, (core + 1) * ROWS)
            grads[index, core, pl.ds(0, 2 * UNITS), :] = both[:, lanes].astype(BF16)
            grads[index, core, pl.ds(2 * UNITS, UNITS), :] = low[:, lanes].astype(BF16)
        to_sibling(index).start()
        return carry

    def core_sum(index, carry):
        to_sibling(index).wait()
        core_land[index] = added(grads[index, r.core], core_land[index]).astype(BF16)
        return carry

    def core_sums(first, last):
        lax.fori_loop(first, last, core_sum, 0)
        keep(core_land.at[pl.ds(first, last - first)], halves.at[pl.ds(first, last - first)], 4 + first // 4)

    def keep_outs():
        keep(outs, outs_kept, 6)

    def second_norm():
        for copy in late_loads:
            copy.wait()
        mixed[...], state["rinv"] = normalized(mixed[...])

    def norm_half(first, number):
        half = pl.ds(first, HALF)
        incoming, normal = total[half, :], mixed[half, :]
        rinv = state["rinv"][first : first + HALF]
        back = norm_back(incoming, normal, rinv, gain2[...])
        back = own_cots[half, :].astype(F32) + back
        grad_mixed[half, :] = back
        keep(grad_mixed.at[half], grad_mixed_kept.at[half], number)
        branch_grad[half, :] = back.astype(BF16)
        keep(branch_grad.at[half], branch_grad_kept.at[half], number + 2)
        sums = jnp.concatenate(norm_sums(incoming, normal), axis=0)
        norm_grads[...] = sums + norm_grads[...] if "summed" in state else sums
        state["summed"] = True

    def norm_top():
        scatter.finish_top(total)
        norm_half(0, 7)

    def norm_low():
        scatter.finish_low(total)
        norm_half(HALF, 8)

    couples = [(a.me, a.across), (a.down, a.up), (a.far, a.down_o), (a.far_o, a.up_o)]
    directs = [(9,), (18, 8), (3, 17, 6, 5), (0, 1, 2, 7, 4)]
    G, S = gather.step, scatter.step

    def P(index):
        return partial(pair, index, *couples[index])

    def Q(index):
        return partial(pair_back, index, *couples[index])

    def T(index):
        return partial(rest, index, *couples[index])

    def D(index):
        return partial(scatter.direct, *directs[index])

    def W(index):
        return partial(lax.fori_loop, 2 * index, 2 * index + 2, weight_grad, 0)

    def K(index):
        return partial(core_sums, 4 * index, 4 * index + 4)

    for step in (
        partial(gather.send, *range(6)), load, G(0), G(1), G(2), second_norm, G(3), G(4), G(5),
        P(1), T(1), P(0), G(6), G(7), Q(0), D(0), G(8), T(0), G(9), G(10), Q(1), D(1), G(15), G(16),
        G(11), P(2), Q(2), D(2), G(14), G(13), T(2), G(12), P(3), Q(3), D(3), S(17), T(3),
        keep_outs, W(0), S(0), W(1), S(1), W(2), S(2), S(3), W(3), scatter.over_last, S(4), K(0),
        scatter.over_inner, K(1), S(5), norm_low, norm_top,
    ):
        step()
    gmail.finish()
    mail.finish()
    for copy in started:
        copy.wait()


def feed_forward(gain2, own, mixed, own_cots, cots, feed):
    group = (TENSOR, ROWS, WIDTH)
    blocks = (8, 3 * UNITS, ROWS)
    return pl.pallas_call(
        feed_kernel,
        out_shape=(
            jax.ShapeDtypeStruct((2, WIDTH), F32),
            jax.ShapeDtypeStruct((ROWS, WIDTH), BF16),
            jax.ShapeDtypeStruct((ROWS, WIDTH), F32),
            jax.ShapeDtypeStruct(blocks, BF16),
            jax.ShapeDtypeStruct(group, BF16),
        ),
        in_specs=vmem(1) + anywhere(5),
        out_specs=tuple(vmem(1) + anywhere(4)),
        scratch_shapes=[
            pltpu.VMEM(group, BF16),
            pltpu.VMEM(group, BF16),
            pltpu.VMEM((3 * UNITS, WIDTH), BF16),
            pltpu.VMEM(group, BF16),
            pltpu.VMEM(group, BF16),
            pltpu.VMEM((3 * UNITS, GROUP), BF16),
            pltpu.VMEM((8, 2, 3 * UNITS, ROWS), BF16),
            pltpu.VMEM((scatter_rows_needed(TOP_FEED_BACK), WIDTH), BF16),
            pltpu.VMEM(blocks, BF16),
            pltpu.VMEM((ROWS, WIDTH), F32),
            pltpu.VMEM((ROWS, WIDTH), BF16),
            pltpu.VMEM((ROWS, WIDTH), F32),
            pltpu.VMEM((ROWS, WIDTH), F32),
            pltpu.VMEM((ROWS, WIDTH), BF16),
            *pairs(GATHER_MAILS),
            *pairs(SCATTER_MAILS),
            *pairs(8),
            pltpu.SemaphoreType.DMA((16,)),
            pltpu.SemaphoreType.DMA((11,)),
        ],
        compiler_params=params(1),
        name="feed_forward",
    )(gain2, own, mixed, own_cots, cots, feed)


TOP_GRADS, TOP_OUTS, TOP_BACK = 48, 32, 48

def attention_back_kernel(
    gain1,
    shift1,
    norm2_grads,
    own,
    grad_mixed_in,
    mixed_in,
    tokens_in,
    tables_in,
    start_in,
    acts_in,
    attended_in,
    logs_in,
    weights_in,
    halves,
    first_rows,
    outs,
    sums,
    layer_kept,
    token_kept,
    qkv_kept,
    out_kept,
    gate_up_kept,
    down_kept,
    layer_out,
    token_grad,
    qkv_grad,
    out_grad,
    feed_grad,
    grad_mixed,
    mixed,
    tokens,
    tables,
    start_lanes,
    acts,
    attended,
    logs,
    weights,
    rows,
    before,
    grad_out,
    grads_qkv,
    keys_turned,
    turns,
    parts,
    out_parts,
    grads,
    land,
    out_land,
    core_land,
    w_land,
    f_land,
    own_halves,
    total,
    boxes,
    g_sends,
    g_receives,
    s_sends,
    s_receives,
    o_sends,
    o_receives,
    k_sends,
    k_receives,
    w_sends,
    w_receives,
    f_sends,
    f_receives,
    a_sends,
    a_receives,
    local,
):
    a, r = Around(), Ring()
    gmail, mail, omail = Mail(g_sends, g_receives), Mail(s_sends, s_receives), Mail(o_sends, o_receives)
    kmail, wmail, fmail = Mail(k_sends, k_receives), Mail(w_sends, w_receives), Mail(f_sends, f_receives)
    amail = Mail(a_sends, a_receives)
    peers = a.peers() + a.to_rest[:1] + r.peers() + [r.to_zh_core]
    hail(peers)
    loads = {}
    for number, (name, source, target) in enumerate(
        (
            ("own", own, rows.at[a.me]),
            ("acts", acts_in, acts),
            ("attended", attended_in, attended),
            ("outs", outs, out_parts),
            ("weights", weights_in, weights),
            ("logs", logs_in, logs),
            ("start", start_in, start_lanes),
            ("half", halves.at[r.zh * 4 + r.x], own_halves.at[0]),
            ("other", halves.at[(1 - r.zh) * 4 + r.x], own_halves.at[1]),
            ("tables", tables_in, tables),
            ("before", first_rows, before),
            ("mixed", mixed_in, mixed),
            ("tokens", tokens_in, tokens),
            ("grad_mixed", grad_mixed_in, grad_mixed),
        )
    ):
        loads[name] = pltpu.make_async_copy(source, target, local.at[number])
        loads[name].start()

    started = []

    def keep(source, target, number):
        copy = pltpu.make_async_copy(source, target, local.at[number])
        copy.start()
        started.append(copy)

    def loaded(*names):
        for name in names:
            loads.pop(name).wait()

    hear(peers)
    gather = Gather(a, gmail, rows, TOP_GRADS, own)
    out_scatter = Scatter(a, omail, out_parts, out_land, TOP_OUTS)
    scatter = Scatter(a, mail, parts, land, TOP_BACK)
    every = EverySum(amail, boxes, sum_stages(a, r))
    feed_fold = Fold(r, fmail, halves, lambda side: own_halves[side], f_land)
    fold = Fold(r, wmail, core_land, lambda side: core_land[fold.place(side, 0)], w_land)

    def turn():
        loaded("acts", "attended")
        keys_turned[...] = acts[1].T
        turns[pl.ds(3 * LOCAL, LOCAL), :] = attended[...].T
        grads_qkv[1] = jnp.zeros((GROUP, LOCAL), F32)
        grads_qkv[2] = jnp.zeros((GROUP, LOCAL), F32)
        loaded("own", "outs", "weights", "logs", "start")

    def back_project(y):
        chunk = rows[pl.ds(2 * y, 2)].reshape(QBLOCK, WIDTH)
        first = pl.multiple_of(y * QBLOCK, QBLOCK)
        grad_out[pl.ds(first, QBLOCK), :] = dot(chunk, weights[3]).astype(BF16)

    state = {}

    def attend(first, heads):
        count = first + QBLOCK
        span = pl.ds(first, QBLOCK)
        query = acts[0, span, :] * BF16(SCALE)
        given = grad_out[span, :]
        row = lax.broadcasted_iota(jnp.int32, (count, QBLOCK), 0)
        column = first + lax.broadcasted_iota(jnp.int32, (count, QBLOCK), 1)
        allow = (row <= column) & (row.astype(F32) >= start_lanes[pl.ds(0, 1), span])
        overlap = given.astype(F32) * attended[span, :].astype(F32)
        lane = lax.broadcasted_iota(jnp.int32, (QBLOCK, LANES), 1)
        inner = jnp.zeros((QBLOCK, LANES), F32)
        for head in range(*heads):
            summed = jnp.sum(only(head_lanes(head, QBLOCK), overlap), axis=1, keepdims=True)
            inner = jnp.where(lane == head, summed, inner)
        inner = inner.T[:8]
        head_row = lax.broadcasted_iota(jnp.int32, (8, QBLOCK), 0)
        head_rows = lax.broadcasted_iota(jnp.int32, (LOCAL, count), 0) // HEAD_DIM

        def one_head(head, turned_query):
            mask = head_lanes(head, QBLOCK)
            masked, masked_given = only(mask, query), only(mask, given)
            log = jnp.sum(only(head_row == head, logs[:, span]), axis=0, keepdims=True)
            mean = jnp.sum(only(head_row == head, inner), axis=0, keepdims=True)
            scores = dot_t(acts[1, pl.ds(0, count), :], masked)
            probs = only(allow, jnp.exp(scores - log))
            grad_probs = dot_t(acts[2, pl.ds(0, count), :], masked_given)
            grad_scores = (probs * (grad_probs - mean)).astype(BF16)
            grads_qkv[2, pl.ds(0, count), :] += dot(probs.astype(BF16), masked_given)
            grads_qkv[1, pl.ds(0, count), :] += dot(grad_scores, masked)
            keys = only(head_rows == head, keys_turned[:, pl.ds(0, count)])
            return turned_query + dot(keys, grad_scores)

        so_far = state.pop("attend", jnp.zeros((LOCAL, QBLOCK), F32))
        so_far = lax.fori_loop(*heads, one_head, so_far)
        if heads[1] < HEADS_DEV:
            state["attend"] = so_far
        else:
            grads_qkv[0, span, :] = so_far.T * SCALE

    def input_grad(y):
        if "tables" in loads:
            loaded("tables", "before")
        first = pl.multiple_of(y * QBLOCK, QBLOCK)
        span = pl.ds(first, QBLOCK)
        back = jnp.zeros((QBLOCK, WIDTH), F32)
        new = []
        for c in range(3):
            pre = grads_qkv[c, span, :]
            if c < 2:
                pre = turned(pre, tables, first, -1.0)
            pre = pre.astype(BF16)
            new.append(jnp.sum(pre.astype(F32), axis=0, keepdims=True))
            back = back + dot_t(pre, weights[c])
            turns[pl.ds(c * LOCAL, LOCAL), span] = pre.T
        parts[pl.ds(2 * y, 2)] = back.astype(BF16).reshape(2, ROWS, WIDTH)
        state["bias"] = state.get("bias", 0.0) + jnp.concatenate(new, axis=0)

    def to_sibling(index):
        return kmail.copy(index, grads.at[index, 1 - r.core], core_land.at[index], r.to_core)

    def weight_grad(index, carry):
        columns = pl.ds(pl.multiple_of(index * 2 * ROWS, 2 * ROWS), 2 * ROWS)
        three = dot(
            turns[pl.ds(0, 3 * LOCAL), :], before[:, :, columns].reshape(GROUP, 2 * ROWS)
        )
        last = dot(turns[pl.ds(3 * LOCAL, LOCAL), :], rows[:, :, columns].reshape(GROUP, 2 * ROWS))
        for core in range(2):
            lanes = slice(core * ROWS, (core + 1) * ROWS)
            grads[index, core, pl.ds(0, 3 * LOCAL), :] = three[:, lanes].astype(BF16)
            grads[index, core, pl.ds(3 * LOCAL, LOCAL), :] = last[:, lanes].astype(BF16)
        to_sibling(index).start()
        return carry

    def weight_grads(first):
        lax.fori_loop(first, first + 2, weight_grad, 0)

    def core_sum(index, carry):
        to_sibling(index).wait()
        core_land[index] = added(grads[index, r.core], core_land[index]).astype(BF16)
        return carry

    def feed_cross():
        loaded("other")
        feed_fold.cross()

    def feed_result():
        loaded("half")
        feed_fold.near()
        feed_sum = feed_fold.result()
        feed_grad[...] = feed_sum
        keep(feed_grad.at[pl.ds(0, 2 * UNITS)], gate_up_kept, 14)
        keep(feed_grad.at[pl.ds(2 * UNITS, UNITS)], down_kept, 15)

    def weight_result():
        fold.near()
        shard = fold.result()
        for c in range(3):
            qkv_grad[c] = shard[c * LOCAL : (c + 1) * LOCAL].T
        out_grad[...] = shard[3 * LOCAL :]
        keep(qkv_grad, qkv_kept, 16)
        keep(out_grad, out_kept, 17)

    def layer_result():
        loaded("mixed")
        out_scatter.finish_top(total)
        out_scatter.finish_low(total)
        layer_out[...] = (mixed[...] + total[...]).astype(BF16)
        keep(layer_out, layer_kept, 18)

    def first_norm():
        loaded("tokens", "grad_mixed")
        mixed[...], state["rinv"] = normalized(tokens[...].astype(F32))

    def norm_half(first, number):
        half = pl.ds(first, HALF)
        rinv = state["rinv"][first : first + HALF]
        back = norm_back(total[half, :], mixed[half, :], rinv, gain1[...])
        token_grad[half, :] = (grad_mixed[half, :] + back).astype(BF16)
        keep(token_grad.at[half], token_kept.at[half], number)

    def norm_top():
        scatter.finish_top(total)
        norm_half(0, 19)

    def norm_low():
        scatter.finish_low(total)
        norm_half(HALF, 20)

    def norm1_sums(y):
        part = parts[pl.ds(2 * y, 2)].reshape(QBLOCK, WIDTH).astype(F32)
        scaled = before[pl.ds(2 * y, 2)].reshape(QBLOCK, WIDTH).astype(F32) - shift1[...]
        sums = jnp.concatenate(norm_sums(part, scaled), axis=0)
        state["norm1"] = sums + state["norm1"] if "norm1" in state else sums

    def by_lanes(*values):
        values = jnp.concatenate(values, axis=0)
        width = values.shape[1]
        return jnp.concatenate([values[:, k : k + LANES] for k in range(0, width, LANES)], axis=0)

    def first_sums():
        norm1 = state["norm1"]
        norms = by_lanes(norm1[:1] / gain1[...], norm1[1:], norm2_grads[...])
        spare = jnp.zeros((SUM_ROWS - NORM_ROWS - 3 * LOCAL // LANES, LANES), F32)
        every.first(jnp.concatenate([norms, by_lanes(state["bias"]), spare], axis=0))

    def last_sums():
        sums[pl.ds(0, NORM_ROWS), :] = every.take(3)
        sums[pl.ds(NORM_ROWS, SUM_ROWS - NORM_ROWS), :] = every.kept[NORM_ROWS:]

    G, O, S = gather.step, out_scatter.step, scatter.step

    def P(y):
        return partial(back_project, y)

    def A(q, *heads):
        return partial(attend, q * QBLOCK, heads)

    def I(y):
        return partial(input_grad, y)

    def N(y):
        return partial(norm1_sums, y)

    def W(index):
        return partial(weight_grads, 2 * index)

    def K(index):
        return partial(lax.fori_loop, 4 * index, 4 * index + 4, core_sum, 0)

    for step in (
        partial(gather.send, *range(6)), partial(feed_fold.send, *range(6)), turn, G(0), G(1), G(2),
        G(3), G(4), G(5), P(a.y), G(7), G(6), G(8), out_scatter.direct_across, G(10), G(11),
        out_scatter.direct_down, G(9), out_scatter.direct_up, G(15), G(16), G(12), P(a.y_down),
        P(a.y_up), G(14), O(2), G(13), P(a.y_far), A(0, 0, 4), A(1, 0, 2), O(1), A(1, 2, 4),
        A(2, 0, 1), A(2, 1, 2), O(17), O(0), O(4), feed_cross, A(2, 2, 3), O(3), A(2, 3, 4),
        A(3, 0, 1), A(3, 1, 2), A(3, 2, 3), A(3, 3, 4), I(a.y_far), I(a.y_up), I(a.y_down),
        scatter.from_down_pair, N(a.y_down), I(a.y), out_scatter.over_last, scatter.from_across,
        scatter.from_up_pair, W(0), feed_result, O(5), W(1), W(2), W(3), scatter.from_far_pair,
        N(a.y_far), N(a.y_up), out_scatter.over_inner, N(a.y), first_sums, K(0), K(1),
        partial(fold.send, *range(6)), S(0), every.second, S(4), S(1), S(17), S(3), S(2),
        scatter.over_last, scatter.over_inner, layer_result, every.third, first_norm, S(5),
        fold.cross, norm_low, every.fourth, norm_top, weight_result, last_sums,
    ):
        step()
    for some in (gmail, mail, omail, kmail, wmail, fmail, amail):
        some.finish()
    for copy in started:
        copy.wait()


def attention_backward(*operands):
    group = (TENSOR, ROWS, WIDTH)
    block, feed_block = (4 * LOCAL, ROWS), (3 * UNITS, ROWS)
    return pl.pallas_call(
        attention_back_kernel,
        out_shape=(
            jax.ShapeDtypeStruct((SUM_ROWS, LANES), F32),
            jax.ShapeDtypeStruct((ROWS, WIDTH), BF16),
            jax.ShapeDtypeStruct((ROWS, WIDTH), BF16),
            jax.ShapeDtypeStruct((3, ROWS, LOCAL), F32),
            jax.ShapeDtypeStruct((LOCAL, ROWS), F32),
            jax.ShapeDtypeStruct((2 * UNITS, ROWS), F32),
            jax.ShapeDtypeStruct((UNITS, ROWS), F32),
        ),
        in_specs=vmem(3) + anywhere(13),
        out_specs=tuple(vmem(1) + anywhere(6)),
        scratch_shapes=[
            pltpu.VMEM((ROWS, WIDTH), BF16),
            pltpu.VMEM((ROWS, WIDTH), BF16),
            pltpu.VMEM((3, ROWS, LOCAL), F32),
            pltpu.VMEM((LOCAL, ROWS), F32),
            pltpu.VMEM(feed_block, F32),
            pltpu.VMEM((ROWS, WIDTH), F32),
            pltpu.VMEM((ROWS, WIDTH), F32),
            pltpu.VMEM((ROWS, WIDTH), BF16),
            pltpu.VMEM((3, GROUP, LANES), F32),
            pltpu.VMEM((8, GROUP), F32),
            pltpu.VMEM((3, GROUP, LOCAL), BF16),
            pltpu.VMEM((GROUP, LOCAL), BF16),
            pltpu.VMEM((8, GROUP), F32),
            pltpu.VMEM((4, WIDTH, LOCAL), BF16),
            pltpu.VMEM(group, BF16),
            pltpu.VMEM(group, BF16),
            pltpu.VMEM((GROUP, LOCAL), BF16),
            pltpu.VMEM((3, GROUP, LOCAL), F32),
            pltpu.VMEM((LOCAL, GROUP), BF16),
            pltpu.VMEM((4 * LOCAL, GROUP), BF16),
            pltpu.VMEM(group, BF16),
            pltpu.VMEM(group, BF16),
            pltpu.VMEM((8, 2) + block, BF16),
            pltpu.VMEM((scatter_rows_needed(TOP_BACK), WIDTH), BF16),
            pltpu.VMEM((scatter_rows_needed(TOP_OUTS), WIDTH), BF16),
            pltpu.VMEM((8,) + block, BF16),
            pltpu.VMEM((FOLD_MAILS,) + block, BF16),
            pltpu.VMEM((FOLD_MAILS,) + feed_block, BF16),
            pltpu.VMEM((2,) + feed_block, BF16),
            pltpu.VMEM((ROWS, WIDTH), F32),
            pltpu.VMEM((SUM_BOXES, SUM_ROWS, LANES), F32),
            *pairs(GATHER_MAILS),
            *pairs(SCATTER_MAILS),
            *pairs(SCATTER_MAILS),
            *pairs(8),
            *pairs(FOLD_MAILS),
            *pairs(FOLD_MAILS),
            *pairs(SUM_MAILS),
            pltpu.SemaphoreType.DMA((21,)),
        ],
        compiler_params=params(2),
        name="attention_backward",
    )(*operands)


def results_kernel(
    sums, layer_in, token_in, qkv_in, out_in, gate_up_in, down_in, layer, token, qkv, out, gate_up, down, *norms
):
    bias = norms[4]
    for source, target in (
        (layer_in, layer),
        (token_in, token),
        (qkv_in, qkv),
        (out_in, out),
        (gate_up_in, gate_up),
        (down_in, down),
    ):
        target[...] = source[...]
    for k in range(WIDTH // LANES):
        for number in range(4):
            norms[number][pl.ds(k, 1), :] = sums[pl.ds(4 * k + number, 1), :]
    for k in range(LOCAL // LANES):
        bias[:, pl.ds(k * LANES, LANES)] = sums[pl.ds(NORM_ROWS + 3 * k, 3), :]


def results(*values):
    shapes = [jax.ShapeDtypeStruct(item.shape, item.dtype) for item in values[1:]]
    shapes += [jax.ShapeDtypeStruct((WIDTH // LANES, LANES), F32)] * 4
    shapes.append(jax.ShapeDtypeStruct((3, LOCAL), F32))
    return pl.pallas_call(
        results_kernel,
        out_shape=tuple(shapes),
        in_specs=vmem(7),
        out_specs=tuple(vmem(len(shapes))),
        name="results",
    )(*values)


def body(
    tokens,
    doc_ids,
    qkv_weight,
    qkv_bias,
    out_weight,
    norm1_gain,
    norm1_shift,
    norm2_gain,
    norm2_shift,
    gate_up_weight,
    down_weight,
    cotangent,
):
    norms = [item[None] for item in (norm1_gain, norm1_shift, norm2_gain, norm2_shift)]
    frequency = np.power(10000.0, -2.0 * np.arange(ROT // 2) / ROT).astype(np.float32)
    frequency = jnp.asarray(np.tile(frequency[:, None], (1, LANES)))
    gate_up = jnp.swapaxes(gate_up_weight, 1, 2).reshape(2 * UNITS, ROWS)
    start, logs, normed2, mixed, tables, acts, attended, rows, weights, cots, feed = attention_forward(
        tokens,
        doc_ids[None],
        qkv_bias,
        out_weight,
        norms,
        frequency,
        qkv_weight,
        gate_up,
        down_weight,
        cotangent,
    )
    norm2_grads, branch_grad, grad_mixed, halves, outs = feed_forward(
        norms[2], normed2, mixed, cotangent, cots, feed
    )
    backward = attention_backward(
        norms[0],
        norms[1],
        norm2_grads,
        branch_grad,
        grad_mixed,
        mixed,
        tokens,
        tables,
        start,
        acts,
        attended,
        logs,
        weights,
        halves,
        rows,
        outs,
    )
    layer_out, token_grad, qkv_grad, out_grad, gate_up_grad, down_grad, *sums = results(*backward)
    return (
        layer_out,
        token_grad,
        qkv_grad,
        sums[4],
        out_grad,
        sums[0].reshape(WIDTH),
        sums[1].reshape(WIDTH),
        sums[2].reshape(WIDTH),
        sums[3].reshape(WIDTH),
        jnp.swapaxes(gate_up_grad.reshape(2, UNITS, ROWS), 1, 2),
        down_grad,
    )


def solution(mesh):
    in_specs = (
        P(("dp", "tensor"), None),
        P(("dp", "tensor")),
        P(None, "dp", "tensor"),
        P(None, "tensor"),
        P("tensor", "dp"),
        P(),
        P(),
        P(),
        P(),
        P(None, "dp", "tensor"),
        P("tensor", "dp"),
        P(("dp", "tensor"), None),
    )
    out_specs = (
        P(("dp", "tensor"), None),
        P(("dp", "tensor"), None),
        P(None, "dp", "tensor"),
        P(None, "tensor"),
        P("tensor", "dp"),
        P(),
        P(),
        P(),
        P(),
        P(None, "dp", "tensor"),
        P("tensor", "dp"),
    )
    return jax.shard_map(body, mesh=mesh, in_specs=in_specs, out_specs=out_specs, check_vma=False)
```
